32 devices in a mesh: diamond: 2 (over x), tile: 16 (over z, y, core).
Axes of the slice: x: 2, y: 2, z: 4, core: 2. Of those that a mesh axis runs over, the one named last changes fastest.
Arguments:
- adjoint_temp: float32 [2, 16, 256, 128], P('diamond', 'tile'), may hold values from -6 to 6
- misfit: float32 [2, 16, 256, 128], P('diamond', 'tile'), may hold values from -4 to 4
- viscosity: float32 [2, 16, 256, 128], P('diamond', 'tile'), may hold values from 0.1 to 10
- velocity: float32 [3, 2, 16, 256, 128], P(None, 'diamond', 'tile'), may hold values from -6 to 6
- forcing: float32 [3, 2, 16, 256, 128], P(None, 'diamond', 'tile'), may hold values from -9 to 9
- edge_table: int32 [2, 256], replicated, may hold values from 0 to 255, as said below
- pole_table: int32 [2, 256], replicated, may hold values from 0 to 255, as said below
Outputs:
- solution: float32 [3, 2, 16, 256, 128], P(None, 'diamond', 'tile')
- residual: float32 [3, 2, 16, 256, 128], P(None, 'diamond', 'tile')
- adjoint_next: float32 [2, 16, 256, 128], P('diamond', 'tile')
The draws below stay inside these ranges and needn't reach their ends.
Inputs may be any that keep to these rules, and one draw needn't show every extreme that they name: `edge_table`: each row of the table is a permutation of the 256 nodes, and row 1 is the inverse permutation of row 0. `pole_table`: each row of the table is a permutation of the 256 nodes, and row 1 is the inverse permutation of row 0.
All inputs are finite; a program needn't handle non-finite values.
Results may differ from the reference program's by a relative error of at most 0.008.
Values sent between devices are 32-bit elements; how exact they have to be, the bound alone decides.
No kernel may reach another device: no remote copies, remote signals or barrier semaphores. Data moves between devices by JAX's collectives and lax.ppermute only.
A program may use at most 64 MiB of HBM per device.

```python
import math
import jax
import jax.numpy as jnp

NY = 256
NR = 128
ITERS = 3
GROUPS = 2
NX = 16


def table_pair(key, count):
    order = jax.random.permutation(key, jnp.arange(count, dtype=jnp.int32))
    inverse = jnp.argsort(order)
    return jnp.stack([order, inverse]).astype(jnp.int32)


def draw_edge_table(key, part):
    key = jax.random.fold_in(key, 11)
    return table_pair(key, NY)


def draw_pole_table(key, part):
    key = jax.random.fold_in(key, 23)
    return table_pair(key, NY)


def draw_forcing(key, part):
    key = jax.random.fold_in(key, 37)
    place = jnp.arange(NX, dtype=jnp.float32) / (NX - 1)
    ramp = place[None, None, :, None, None]
    rough = jnp.clip(jax.random.normal(key, (3, GROUPS, NX, NY, NR), jnp.float32), -5.5, 5.5)
    return rough + 3.0 * ramp


def block_levels(own_key, extent, split, least, largest):
    level, own = 1.0, jax.random.fold_in(own_key, 6)
    for axis_at, shards_of in split:
        draws = jnp.exp(jax.random.uniform(jax.random.fold_in(own, axis_at), (shards_of,), jnp.float32, least / len(split), largest / len(split)))
        level = level * jnp.repeat(draws, extent[axis_at] // shards_of).reshape([-1 if axis == axis_at else 1 for axis in range(len(extent))])
    return level


def gaussian(key, shape, deviation, most, shards=(), kind=jnp.bfloat16):
    array = jax.random.normal(key, shape, jnp.float32) * deviation
    if len(shards) > 0:
        array = block_levels(key, shape, shards, -0.22, 0.18) * array
    return jnp.clip(array, min=-most, max=most).astype(kind)


def setup_inputs(seed: int = 0) -> dict:
    key_list = jax.random.split(jax.random.key(seed), 8)
    adjoint_temp = gaussian(key_list[0], (GROUPS, NX, NY, NR), 1.0, 6.0, ((0, 2), (1, 16)), jnp.float32)
    misfit = gaussian(key_list[1], (GROUPS, NX, NY, NR), 0.5, 4.0, ((0, 2), (1, 16)), jnp.float32)
    viscosity = jnp.clip(jnp.exp(math.log(10.0) - 4.6051702 * jax.random.uniform(key_list[2], (GROUPS, NX, NY, NR), jnp.float32) ** block_levels(key_list[2], (GROUPS, NX, NY, NR), ((0, 2), (1, 16)), -0.2, 0.2)), 0.1, 10.0)
    velocity = gaussian(key_list[3], (3, GROUPS, NX, NY, NR), 1.0, 6.0, ((1, 2), (2, 16)), jnp.float32)
    forcing = draw_forcing(jax.random.fold_in(key_list[7], 71), 0)
    edge_table = draw_edge_table(jax.random.fold_in(key_list[7], 71), 0)
    pole_table = draw_pole_table(jax.random.fold_in(key_list[7], 71), 0)
    return dict(adjoint_temp=adjoint_temp, misfit=misfit, viscosity=viscosity, velocity=velocity, forcing=forcing, edge_table=edge_table, pole_table=pole_table)


TIME_STEP = 0.1
DIFFUSION = 1.0
MASS_TERM = 0.5
BUOYANCY = 1.0


def partner_rows(edge_rows, table):
    flipped = edge_rows[::-1]
    first = jnp.take(flipped[0], table[0], axis=0)
    second = jnp.take(flipped[1], table[1], axis=0)
    return jnp.stack([first, second])


def neighbours(field, edge_table, pole_table):
    x_after = jnp.concatenate([field[:, 1:], partner_rows(field[:, -1], edge_table)[:, None]], axis=1)
    x_before = jnp.concatenate([partner_rows(field[:, 0], pole_table)[:, None], field[:, :-1]], axis=1)
    zeros_y = jnp.zeros_like(field[:, :, :1])
    y_after = jnp.concatenate([field[:, :, 1:], zeros_y], axis=2)
    y_before = jnp.concatenate([zeros_y, field[:, :, :-1]], axis=2)
    zeros_r = jnp.zeros_like(field[:, :, :, :1])
    r_after = jnp.concatenate([field[:, :, :, 1:], zeros_r], axis=3)
    r_before = jnp.concatenate([zeros_r, field[:, :, :, :-1]], axis=3)
    return [x_after, x_before, y_after, y_before, r_after, r_before]


def face_masks(count_y, count_r):
    y_place = jnp.arange(count_y)[:, None]
    r_place = jnp.arange(count_r)
    unity = jnp.ones((1, 1), jnp.float32)
    return [unity, unity,
            (y_place < count_y - 1).astype(jnp.float32), (y_place > 0).astype(jnp.float32),
            (r_place < count_r - 1).astype(jnp.float32), (r_place > 0).astype(jnp.float32)]


def reference(adjoint_temp, misfit, viscosity, velocity, forcing, edge_table, pole_table):
    temp_near = neighbours(adjoint_temp, edge_table, pole_table)
    visc_near = neighbours(viscosity, edge_table, pole_table)
    laplace = sum(temp_near) - 6.0 * adjoint_temp
    transport = 0.5 * (velocity[0] * (temp_near[0] - temp_near[1])
                       + velocity[1] * (temp_near[2] - temp_near[3])
                       + velocity[2] * (temp_near[4] - temp_near[5]))
    adjoint_next = adjoint_temp + TIME_STEP * (DIFFUSION * laplace + transport) + misfit
    inside = face_masks(NY, NR)
    weights = [0.5 * (viscosity + visc_near[k]) * inside[k] for k in range(6)]
    diagonal = MASS_TERM + sum(weights)

    def apply(vector):
        result = []
        for comp in range(3):
            near = neighbours(vector[comp], edge_table, pole_table)
            total = diagonal * vector[comp]
            for k in range(6):
                total = total - weights[k] * near[k]
            result.append(total)
        return jnp.stack(result)

    right = forcing.at[2].add(BUOYANCY * adjoint_next)
    solution = jnp.zeros_like(right)
    residual = right
    precond = residual / diagonal
    direction = precond
    product_now = jnp.sum(residual * precond)
    for step in range(ITERS):
        image = apply(direction)
        step_size = product_now / jnp.sum(direction * image)
        solution = solution + step_size * direction
        residual = residual - step_size * image
        precond = residual / diagonal
        product_next = jnp.sum(residual * precond)
        direction = precond + (product_next / product_now) * direction
        product_now = product_next
    return solution, residual, adjoint_next
```

```python
import functools

import jax
import jax.numpy as jnp
from jax import lax
from jax.experimental import pallas as pl
from jax.experimental.pallas import tpu as pltpu
from jax.sharding import PartitionSpec as P

ITERS = 3
TIME_STEP = 0.1
DIFFUSION = 1.0
MASS_TERM = 0.5
BUOYANCY = 1.0
CENTERS = (0.0, 0.45, -0.45, 0.75, -0.75, 0.95, -0.95)
CHUNK = 32
SPLITS = ((0, 1), (1, 2), (2, 3))


def rows_around(load, start, total):
    low, high = max(start - 8, 0), min(start + CHUNK + 8, total)
    block = load(low, high)
    at = start - low
    after = pltpu.roll(block, high - low - 1, 0)[at : at + CHUNK]
    before = pltpu.roll(block, 1, 0)[at : at + CHUNK]
    return block[at : at + CHUNK], after, before


def layers_around(block):
    count = block.shape[1]
    return pltpu.roll(block, count - 1, 1), pltpu.roll(block, 1, 1)


def split3(value):
    top = value.astype(jnp.bfloat16)
    rest = value - top.astype(jnp.float32)
    middle = rest.astype(jnp.bfloat16)
    bottom = (rest - middle.astype(jnp.float32)).astype(jnp.bfloat16)
    return [top, middle, bottom]


def fold_matrix(edge_ref, pole_ref):
    group, tile = lax.axis_index("diamond"), lax.axis_index("tile")
    final = lax.axis_size("tile") - 1
    count = edge_ref.shape[1]
    rows = lax.broadcasted_iota(jnp.int32, (count, count), 0)
    same = lax.broadcasted_iota(jnp.int32, (1, count), 1)
    edge = jnp.where(group == 0, edge_ref[1:2], edge_ref[0:1])
    pole = jnp.where(group == 0, pole_ref[1:2], pole_ref[0:1])
    line = jnp.where(tile == 0, pole, jnp.where(tile == final, edge, same))
    return (rows == line).astype(jnp.bfloat16)


def unfold(matrix_ref, far_ref, out_ref):
    layers = far_ref.shape[2]
    for at in range(far_ref.shape[0]):
        pieces = jnp.concatenate(split3(far_ref[at]), axis=1)
        moved = jnp.dot(matrix_ref[...], pieces, preferred_element_type=jnp.float32)
        out_ref[at] = (
            moved[:, :layers] + moved[:, layers : 2 * layers] + moved[:, 2 * layers :]
        )


def local_kernel(
    temp_hbm, misfit_hbm, visc_hbm, velocity_hbm, forcing_hbm, edge_hbm, pole_hbm,
    half_ref, side_ref, base_ref, right_ref, part_ref, speed_ref, matrix_ref,
    temp_ref, misfit_ref, visc_ref, velocity_ref, edge_ref, pole_ref, sems,
):
    sources = [visc_hbm, temp_hbm, edge_hbm, pole_hbm, velocity_hbm, misfit_hbm, forcing_hbm]
    targets = [visc_ref, temp_ref, edge_ref, pole_ref, velocity_ref, misfit_ref, right_ref]
    copies = [pltpu.make_async_copy(s, t, sems.at[i]) for i, (s, t) in enumerate(zip(sources, targets))]
    for copy in copies:
        copy.start()
    odd = lax.rem(lax.axis_index("tile"), 2)
    half = jnp.where(odd == 0, 0.5, -0.5).astype(jnp.float32)
    total, layers = temp_ref.shape
    for copy in copies:
        copy.wait()
    matrix_ref[...] = fold_matrix(edge_ref, pole_ref)
    for start in range(0, total, CHUNK):
        here = slice(start, start + CHUNK)
        visc, visc_after, visc_before = rows_around(lambda a, b: visc_ref[a:b], start, total)
        temp, temp_after, temp_before = rows_around(lambda a, b: temp_ref[a:b], start, total)
        place = start + lax.broadcasted_iota(jnp.int32, (CHUNK, layers), 0)
        layer = lax.broadcasted_iota(jnp.int32, (CHUNK, layers), 1)
        inside = [place < total - 1, place > 0, layer < layers - 1, layer > 0]
        visc_near = [visc_after, visc_before, *layers_around(visc)]
        temp_near = [temp_after, temp_before, *layers_around(temp)]
        zero = jnp.zeros_like(visc)
        weights = [jnp.where(m, 0.5 * (visc + v), zero) for m, v in zip(inside, visc_near)]
        temps = [jnp.where(m, t, zero) for m, t in zip(inside, temp_near)]
        half_ref[here] = 0.5 * visc
        for k in range(4):
            side_ref[k, here] = weights[k]
        base_ref[here] = MASS_TERM + sum(weights)
        transport = 0.5 * (
            velocity_ref[1, here] * (temps[0] - temps[1]) + velocity_ref[2, here] * (temps[2] - temps[3])
        )
        laplace = sum(temps) - 6.0 * temp
        part_ref[here] = temp + TIME_STEP * (DIFFUSION * laplace + transport) + misfit_ref[here]
        speed_ref[here] = half * velocity_ref[0, here]


def prepare_kernel(
    half_ref, side_ref, base_ref, right_ref, part_ref, speed_ref, matrix_ref,
    visc_near_ref, temp_near_ref, visc_far_ref, temp_far_ref,
    next_ref, weights_ref, diagonal_ref, *refs,
):
    *first_refs, moved_visc_ref, moved_temp_ref = refs
    unfold(matrix_ref, visc_far_ref, moved_visc_ref)
    unfold(matrix_ref, temp_far_ref, moved_temp_ref)
    for start in range(0, half_ref.shape[0], CHUNK):
        here = slice(start, start + CHUNK)
        near, far = temp_near_ref[0, here], moved_temp_ref[0, here]
        adjoint_next = part_ref[here] + TIME_STEP * (
            DIFFUSION * (near + far) + speed_ref[here] * (near - far)
        )
        next_ref[here] = adjoint_next
        visc = half_ref[here]
        weights = [visc + 0.5 * visc_near_ref[0, here], visc + 0.5 * moved_visc_ref[0, here]]
        diagonal = base_ref[here] + weights[0] + weights[1]
        diagonal_ref[here] = diagonal
        inverse = 1.0 / diagonal
        weights += [side_ref[k, here] for k in range(4)]
        for k in range(6):
            weights_ref[k, here] = weights[k] * inverse
        for (low, high), first_ref in zip(SPLITS, first_refs):
            for at in range(low, high):
                right = right_ref[at, here]
                if at == 2:
                    right = right + BUOYANCY * adjoint_next
                first_ref[at - low, here] = right * inverse


def average(start, at, field_ref, near_ref, moved_ref, weights):
    here = slice(start, start + CHUNK)
    mid, after, before = rows_around(lambda a, b: field_ref[at, a:b], start, field_ref.shape[1])
    around = [near_ref[at, here], moved_ref[at, here], after, before, *layers_around(mid)]
    return sum(w * v for w, v in zip(weights, around))


def apply_kernel(far_ref, near_ref, field_ref, weights_ref, matrix_ref, after_ref, out_ref, moved_ref):
    unfold(matrix_ref, far_ref, moved_ref)
    for start in range(0, field_ref.shape[1], CHUNK):
        here = slice(start, start + CHUNK)
        weights = [weights_ref[k, here] for k in range(6)]
        for at in range(field_ref.shape[0]):
            out_ref[at, here] = average(start, at, field_ref, near_ref, moved_ref, weights)


def fold8(value):
    return jnp.sum(value.reshape(value.shape[0] // 8, 8, value.shape[1]), axis=0)


def moment_lanes(k):
    row = lax.broadcasted_iota(jnp.int32, (8, 128), 0)
    lane = lax.broadcasted_iota(jnp.int32, (8, 128), 1)
    return lane == row + 8 * k


def place_moment(k, sums):
    rows = [jnp.sum(s, axis=0, keepdims=True) for s in sums]
    rows += [rows[0]] * (8 - len(rows))
    column = jnp.sum(jnp.concatenate(rows, axis=0), axis=1, keepdims=True)
    return jnp.where(moment_lanes(k), column, 0.0)


def early_kernel(diagonal_ref, *refs):
    moments_ref, left_ref, shift_ref = refs[-3:]
    total, layers = diagonal_ref.shape
    sums = [[jnp.zeros((8, layers), jnp.float32) for _ in CENTERS] for _ in range(5)]
    for i, (low, high) in enumerate(SPLITS):
        y0_ref, y1_ref, y2_ref = refs[3 * i : 3 * i + 3]
        for start in range(0, total, CHUNK):
            here = slice(start, start + CHUNK)
            diagonal = diagonal_ref[here]
            for at in range(high - low):
                y0, y1, y2 = y0_ref[at, here], y1_ref[at, here], y2_ref[at, here]
                d0 = diagonal * y0
                m0 = fold8(d0 * y0)
                for j, center in enumerate(CENTERS):
                    q1 = y1 - center * y0
                    t2 = y2 - center * y1
                    q2 = t2 - center * q1
                    d1, d2 = diagonal * q1, diagonal * q2
                    left_ref[j, low + at, here] = d2
                    shift_ref[j, low + at, here] = center * (y2 + t2 + q2)
                    sums[0][j] += m0
                    sums[1][j] += fold8(d0 * q1)
                    sums[2][j] += fold8(d1 * q1)
                    sums[3][j] += fold8(d1 * q2)
                    sums[4][j] += fold8(d2 * q2)
    moments_ref[...] = sum(place_moment(k, sums[k]) for k in range(5))


def powers(center, y0, y1, y2, y3):
    q1 = y1 - center * y0
    t2 = y2 - center * y1
    q2 = t2 - center * q1
    q3 = (y3 - center * y2 - center * t2) - center * q2
    return q1, q2, q3


def last_kernel(
    low, far_ref, near_ref, field_ref, weights_ref, matrix_ref, earlier_ref, left_ref, shift_ref,
    out_ref, moments_ref, moved_ref,
):
    unfold(matrix_ref, far_ref, moved_ref)
    total, layers = field_ref.shape[1:]
    sums = [jnp.zeros((8, layers), jnp.float32) for _ in CENTERS]
    for start in range(0, total, CHUNK):
        here = slice(start, start + CHUNK)
        weights = [weights_ref[k, here] for k in range(6)]
        for at in range(field_ref.shape[0]):
            y3 = average(start, at, field_ref, near_ref, moved_ref, weights)
            out_ref[at, here] = y3
            for j in range(len(CENTERS)):
                sums[j] += fold8(left_ref[j, low + at, here] * (y3 - shift_ref[j, low + at, here]))
    message = earlier_ref[...] + place_moment(5, sums)
    if len(moments_ref.shape) == 2:
        moments_ref[...] = message
    else:
        row = jnp.sum(message, axis=0, keepdims=True)
        for device in range(moments_ref.shape[0]):
            moments_ref[device] = row


def inner(left, right, moments, shift=0):
    total = 0.0
    for i, a in enumerate(left):
        for j, b in enumerate(right):
            total = total + (a * b) * moments[i + j + shift]
    return total


def axpy(scale, left, right):
    count = max(len(left), len(right))
    result = []
    for i in range(count):
        if i >= len(left):
            result.append(right[i])
        elif i >= len(right):
            result.append(scale * left[i])
        else:
            result.append(scale * left[i] + right[i])
    return result


def recurrence(moments, centers):
    def operator(poly):
        result = [(1.0 - centers) * a for a in poly] + [jnp.zeros_like(centers)]
        for i, a in enumerate(poly):
            result[i + 1] = result[i + 1] - a
        return result

    one = jnp.ones_like(centers)
    residual, direction, answer = [one], [one], []
    product_now = moments[0]
    for step in range(ITERS):
        image = operator(direction)
        step_size = product_now / inner(direction, image, moments)
        answer = axpy(step_size, direction, answer)
        residual = axpy(-step_size, image, residual)
        if step + 1 < ITERS:
            product_next = inner(residual, residual, moments)
            direction = axpy(product_next / product_now, direction, residual)
            product_now = product_next
    return answer, residual


def finish_kernel(moments_ref, diagonal_ref, *refs):
    solution_ref, residual_ref = refs[-2:]
    streams = [refs[4 * i : 4 * i + 4] for i in range(len(SPLITS))]
    rows = [moments_ref[device] for device in range(moments_ref.shape[0])]
    while len(rows) > 1:
        rows = [a + b for a, b in zip(rows[::2], rows[1::2])]
    row = jnp.broadcast_to(rows[0], (8, 128))
    moments = [jnp.sum(jnp.where(moment_lanes(k), row, 0.0), axis=1, keepdims=True) for k in range(6)]
    place = lax.broadcasted_iota(jnp.int32, (8, 1), 0)
    centers = jnp.zeros((8, 1), jnp.float32)
    for j, center in enumerate(CENTERS):
        centers = jnp.where(place == j, center, centers)
    answer, residual = recurrence(moments, centers)
    packed = [centers, *answer, *residual]
    mean = centers[0:1] + moments[1][0:1] / moments[0][0:1]
    best = jnp.abs(mean - centers[0:1])
    chosen = [p[0:1] for p in packed]
    for j in range(1, len(CENTERS)):
        away = jnp.abs(mean - centers[j : j + 1])
        better = away < best
        best = jnp.where(better, away, best)
        chosen = [jnp.where(better, p[j : j + 1], c) for p, c in zip(packed, chosen)]
    total, layers = diagonal_ref.shape
    chosen = [jnp.broadcast_to(c, (CHUNK, layers)) for c in chosen]
    center, answer, residual = chosen[0], chosen[1:4], chosen[4:8]
    for start in range(0, total, CHUNK):
        here = slice(start, start + CHUNK)
        diagonal = diagonal_ref[here]
        for (low, high), stream in zip(SPLITS, streams):
            for at in range(high - low):
                values = [ref[at, here] for ref in stream]
                q1, q2, q3 = powers(center, *values)
                solution_ref[low + at, here] = answer[0] * values[0] + answer[1] * q1 + answer[2] * q2
                residual_ref[low + at, here] = diagonal * (
                    residual[0] * values[0] + residual[1] * q1 + residual[2] * q2 + residual[3] * q3
                )


def call(kernel, out_shapes, *args, scratch=(), place=pltpu.VMEM):
    whole = pl.BlockSpec(memory_space=pltpu.VMEM)
    if place is pltpu.HBM:
        args = [pltpu.with_memory_space_constraint(a, place) for a in args]
    outs = [o if isinstance(o, jax.ShapeDtypeStruct) else jax.ShapeDtypeStruct(o, jnp.float32) for o in out_shapes]
    return pl.pallas_call(
        kernel,
        out_shape=outs,
        in_specs=[pl.BlockSpec(memory_space=place)] * len(args),
        out_specs=[whole] * len(out_shapes),
        scratch_shapes=[pltpu.VMEM(s, jnp.float32) if isinstance(s, tuple) else s for s in scratch],
        compiler_params=pltpu.CompilerParams(vmem_limit_bytes=24 * 2**20),
    )(*args)


def ring_pairs(groups, tiles):
    beside = [(g * tiles + i, g * tiles + (i ^ 1)) for g in range(groups) for i in range(tiles)]
    across = []
    for g in range(groups):
        for i in range(tiles):
            j = i - 1 if i % 2 == 0 else i + 1
            if j < 0 or j >= tiles:
                across.append((g * tiles + i, (1 - g) * tiles + i))
            else:
                across.append((g * tiles + i, g * tiles + j))
    return beside, across


NAMES = ("diamond", "tile")


def exchange(value):
    beside, across = ring_pairs(lax.axis_size("diamond"), lax.axis_size("tile"))
    far = lax.ppermute(value, NAMES, across)
    near = lax.ppermute(value, NAMES, beside)
    return near, far


def body(adjoint_temp, misfit, viscosity, velocity, forcing, edge_table, pole_table):
    rows, layers = adjoint_temp.shape[2:]
    devices = lax.axis_size("diamond") * lax.axis_size("tile")
    flat, triple = (rows, layers), (3, rows, layers)
    temp, source, visc = (v.reshape(flat) for v in (adjoint_temp, misfit, viscosity))
    visc_near, visc_far = exchange(visc[None])
    temp_near, temp_far = exchange(temp[None])
    table = pltpu.VMEM(edge_table.shape, edge_table.dtype)
    half, side, base, right, part, speed, matrix = call(
        local_kernel,
        [flat, (4, *flat), flat, triple, flat, flat, jax.ShapeDtypeStruct((rows, rows), jnp.bfloat16)],
        temp, source, visc, velocity.reshape(triple), forcing.reshape(triple), edge_table, pole_table,
        scratch=[flat, flat, flat, triple, table, table, pltpu.SemaphoreType.DMA((7,))],
        place=pltpu.HBM,
    )
    shapes = [(high - low, rows, layers) for low, high in SPLITS]
    adjoint_next, weights, diagonal, *first = call(
        prepare_kernel, [flat, (6, *flat), flat, *shapes],
        half, side, base, right, part, speed, matrix, visc_near, temp_near, visc_far, temp_far,
        scratch=[(1, *flat), (1, *flat)],
    )
    streams = [[field] for field in first]
    swapped = [exchange(field) for field in first]
    latest = first[-1]
    for step in range(ITERS - 1):
        for i, shape in enumerate(shapes):
            near, far = swapped[i]
            (latest,) = call(
                apply_kernel, [shape], far, near, streams[i][-1], weights, matrix, latest, scratch=[shape]
            )
            swapped[i] = exchange(latest)
            streams[i].append(latest)
    many = (len(CENTERS), *triple)
    moments, left, shift = call(
        early_kernel, [(8, 128), many, many], diagonal, *[field for stream in streams for field in stream]
    )
    for i, shape in enumerate(shapes):
        near, far = swapped[i]
        sums = (8, 128) if i + 1 < len(shapes) else (devices, 1, 128)
        field, moments = call(
            functools.partial(last_kernel, SPLITS[i][0]), [shape, sums],
            far, near, streams[i][-1], weights, matrix, moments, left, shift, scratch=[shape],
        )
        streams[i].append(field)
    moments = lax.all_to_all(moments, NAMES, 0, 0)
    fields = [field for stream in streams for field in stream]
    answer, residual = call(finish_kernel, [triple, triple], moments, diagonal, *fields)
    whole = (3, 1, 1, rows, layers)
    return answer.reshape(whole), residual.reshape(whole), adjoint_next.reshape(adjoint_temp.shape)


def solution(mesh):
    flat = P("diamond", "tile", None, None)
    triple = P(None, "diamond", "tile", None, None)
    return jax.shard_map(
        body,
        mesh=mesh,
        in_specs=(flat, flat, flat, triple, triple, P(), P()),
        out_specs=(triple, triple, flat),
        check_vma=False,
    )
```

```python
import functools

import jax
import jax.numpy as jnp
from jax import lax
from jax.experimental import pallas as pl
from jax.experimental.pallas import tpu as pltpu
from jax.sharding import PartitionSpec as P

ITERS = 3
TIME_STEP = 0.1
DIFFUSION = 1.0
MASS_TERM = 0.5
BUOYANCY = 1.0
CENTERS = (0.0, 0.45, -0.45, 0.75, -0.75, 0.95, -0.95)
CHUNK = 32
SPLITS = ((0, 1), (1, 2), (2, 3))


def rows_around(load, start, total):
    low, high = max(start - 8, 0), min(start + CHUNK + 8, total)
    block = load(low, high)
    at = start - low
    after = pltpu.roll(block, high - low - 1, 0)[at : at + CHUNK]
    before = pltpu.roll(block, 1, 0)[at : at + CHUNK]
    return block[at : at + CHUNK], after, before


def layers_around(block):
    count = block.shape[1]
    return pltpu.roll(block, count - 1, 1), pltpu.roll(block, 1, 1)


def split3(value):
    top = value.astype(jnp.bfloat16)
    rest = value - top.astype(jnp.float32)
    middle = rest.astype(jnp.bfloat16)
    bottom = (rest - middle.astype(jnp.float32)).astype(jnp.bfloat16)
    return [top, middle, bottom]


def fold_matrix(edge_ref, pole_ref):
    group, tile = lax.axis_index("diamond"), lax.axis_index("tile")
    final = lax.axis_size("tile") - 1
    count = edge_ref.shape[1]
    rows = lax.broadcasted_iota(jnp.int32, (count, count), 0)
    same = lax.broadcasted_iota(jnp.int32, (1, count), 1)
    edge = jnp.where(group == 0, edge_ref[1:2], edge_ref[0:1])
    pole = jnp.where(group == 0, pole_ref[1:2], pole_ref[0:1])
    line = jnp.where(tile == 0, pole, jnp.where(tile == final, edge, same))
    return (rows == line).astype(jnp.bfloat16)


def unfold(matrix_ref, far_ref, out_ref):
    layers = far_ref.shape[2]
    for at in range(far_ref.shape[0]):
        pieces = jnp.concatenate(split3(far_ref[at]), axis=1)
        moved = jnp.dot(matrix_ref[...], pieces, preferred_element_type=jnp.float32)
        out_ref[at] = (
            moved[:, :layers] + moved[:, layers : 2 * layers] + moved[:, 2 * layers :]
        )


def local_kernel(
    temp_hbm, misfit_hbm, visc_hbm, velocity_hbm, forcing_hbm, edge_hbm, pole_hbm,
    half_ref, side_ref, base_ref, right_ref, part_ref, speed_ref, matrix_ref,
    temp_ref, misfit_ref, visc_ref, velocity_ref, edge_ref, pole_ref, sems,
):
    sources = [visc_hbm, temp_hbm, edge_hbm, pole_hbm, velocity_hbm, misfit_hbm, forcing_hbm]
    targets = [visc_ref, temp_ref, edge_ref, pole_ref, velocity_ref, misfit_ref, right_ref]
    copies = [pltpu.make_async_copy(s, t, sems.at[i]) for i, (s, t) in enumerate(zip(sources, targets))]
    for copy in copies:
        copy.start()
    odd = lax.rem(lax.axis_index("tile"), 2)
    half = jnp.where(odd == 0, 0.5, -0.5).astype(jnp.float32)
    total, layers = temp_ref.shape
    for copy in copies:
        copy.wait()
    matrix_ref[...] = fold_matrix(edge_ref, pole_ref)
    for start in range(0, total, CHUNK):
        here = slice(start, start + CHUNK)
        visc, visc_after, visc_before = rows_around(lambda a, b: visc_ref[a:b], start, total)
        temp, temp_after, temp_before = rows_around(lambda a, b: temp_ref[a:b], start, total)
        place = start + lax.broadcasted_iota(jnp.int32, (CHUNK, layers), 0)
        layer = lax.broadcasted_iota(jnp.int32, (CHUNK, layers), 1)
        inside = [place < total - 1, place > 0, layer < layers - 1, layer > 0]
        visc_near = [visc_after, visc_before, *layers_around(visc)]
        temp_near = [temp_after, temp_before, *layers_around(temp)]
        zero = jnp.zeros_like(visc)
        weights = [jnp.where(m, 0.5 * (visc + v), zero) for m, v in zip(inside, visc_near)]
        temps = [jnp.where(m, t, zero) for m, t in zip(inside, temp_near)]
        half_ref[here] = 0.5 * visc
        for k in range(4):
            side_ref[k, here] = weights[k]
        base_ref[here] = MASS_TERM + sum(weights)
        transport = 0.5 * (
            velocity_ref[1, here] * (temps[0] - temps[1]) + velocity_ref[2, here] * (temps[2] - temps[3])
        )
        laplace = sum(temps) - 6.0 * temp
        part_ref[here] = temp + TIME_STEP * (DIFFUSION * laplace + transport) + misfit_ref[here]
        speed_ref[here] = half * velocity_ref[0, here]


def weigh_kernel(
    far_ref, near_ref, half_ref, side_ref, base_ref, right_ref, matrix_ref,
    weights_ref, diagonal_ref, inverse_ref, *refs,
):
    *first_refs, moved_ref = refs
    unfold(matrix_ref, far_ref, moved_ref)
    for start in range(0, half_ref.shape[0], CHUNK):
        here = slice(start, start + CHUNK)
        visc = half_ref[here]
        weights = [visc + 0.5 * near_ref[0, here], visc + 0.5 * moved_ref[0, here]]
        diagonal = base_ref[here] + weights[0] + weights[1]
        diagonal_ref[here] = diagonal
        inverse = 1.0 / diagonal
        inverse_ref[here] = inverse
        for (low, high), first_ref in zip(SPLITS, first_refs):
            for at in range(low, high):
                first_ref[at - low, here] = right_ref[at, here] * inverse
        weights += [side_ref[k, here] for k in range(4)]
        for k in range(6):
            weights_ref[k, here] = weights[k] * inverse


def step_kernel(
    far_ref, near_ref, right_ref, part_ref, speed_ref, inverse_ref, matrix_ref, next_ref, first_ref, moved_ref
):
    unfold(matrix_ref, far_ref, moved_ref)
    for start in range(0, part_ref.shape[0], CHUNK):
        here = slice(start, start + CHUNK)
        near, far = near_ref[0, here], moved_ref[0, here]
        adjoint_next = part_ref[here] + TIME_STEP * (
            DIFFUSION * (near + far) + speed_ref[here] * (near - far)
        )
        next_ref[here] = adjoint_next
        first_ref[0, here] = (right_ref[2, here] + BUOYANCY * adjoint_next) * inverse_ref[here]


def average(start, at, field_ref, near_ref, moved_ref, weights):
    here = slice(start, start + CHUNK)
    mid, after, before = rows_around(lambda a, b: field_ref[at, a:b], start, field_ref.shape[1])
    around = [near_ref[at, here], moved_ref[at, here], after, before, *layers_around(mid)]
    return sum(w * v for w, v in zip(weights, around))


def apply_kernel(far_ref, near_ref, field_ref, weights_ref, matrix_ref, out_ref, moved_ref):
    unfold(matrix_ref, far_ref, moved_ref)
    for start in range(0, field_ref.shape[1], CHUNK):
        here = slice(start, start + CHUNK)
        weights = [weights_ref[k, here] for k in range(6)]
        for at in range(field_ref.shape[0]):
            out_ref[at, here] = average(start, at, field_ref, near_ref, moved_ref, weights)


def fold8(value):
    return jnp.sum(value.reshape(value.shape[0] // 8, 8, value.shape[1]), axis=0)


def moment_lanes(k):
    row = lax.broadcasted_iota(jnp.int32, (8, 128), 0)
    lane = lax.broadcasted_iota(jnp.int32, (8, 128), 1)
    return lane == row + 8 * k


def place_moment(k, sums):
    rows = [jnp.sum(s, axis=0, keepdims=True) for s in sums]
    rows += [rows[0]] * (8 - len(rows))
    column = jnp.sum(jnp.concatenate(rows, axis=0), axis=1, keepdims=True)
    return jnp.where(moment_lanes(k), column, 0.0)


def early_kernel(diagonal_ref, *refs):
    moments_ref, left_ref, shift_ref = refs[-3:]
    total, layers = diagonal_ref.shape
    sums = [[jnp.zeros((8, layers), jnp.float32) for _ in CENTERS] for _ in range(5)]
    for i, (low, high) in enumerate(SPLITS):
        y0_ref, y1_ref, y2_ref = refs[3 * i : 3 * i + 3]
        for start in range(0, total, CHUNK):
            here = slice(start, start + CHUNK)
            diagonal = diagonal_ref[here]
            for at in range(high - low):
                y0, y1, y2 = y0_ref[at, here], y1_ref[at, here], y2_ref[at, here]
                d0 = diagonal * y0
                m0 = fold8(d0 * y0)
                for j, center in enumerate(CENTERS):
                    q1 = y1 - center * y0
                    t2 = y2 - center * y1
                    q2 = t2 - center * q1
                    d1, d2 = diagonal * q1, diagonal * q2
                    left_ref[j, low + at, here] = d2
                    shift_ref[j, low + at, here] = center * (y2 + t2 + q2)
                    sums[0][j] += m0
                    sums[1][j] += fold8(d0 * q1)
                    sums[2][j] += fold8(d1 * q1)
                    sums[3][j] += fold8(d1 * q2)
                    sums[4][j] += fold8(d2 * q2)
    moments_ref[...] = sum(place_moment(k, sums[k]) for k in range(5))


def powers(center, y0, y1, y2, y3):
    q1 = y1 - center * y0
    t2 = y2 - center * y1
    q2 = t2 - center * q1
    q3 = (y3 - center * y2 - center * t2) - center * q2
    return q1, q2, q3


def last_kernel(
    low, far_ref, near_ref, field_ref, weights_ref, matrix_ref, earlier_ref, left_ref, shift_ref,
    out_ref, moments_ref, moved_ref,
):
    unfold(matrix_ref, far_ref, moved_ref)
    total, layers = field_ref.shape[1:]
    sums = [jnp.zeros((8, layers), jnp.float32) for _ in CENTERS]
    for start in range(0, total, CHUNK):
        here = slice(start, start + CHUNK)
        weights = [weights_ref[k, here] for k in range(6)]
        for at in range(field_ref.shape[0]):
            y3 = average(start, at, field_ref, near_ref, moved_ref, weights)
            out_ref[at, here] = y3
            for j in range(len(CENTERS)):
                sums[j] += fold8(left_ref[j, low + at, here] * (y3 - shift_ref[j, low + at, here]))
    message = earlier_ref[...] + place_moment(5, sums)
    if len(moments_ref.shape) == 2:
        moments_ref[...] = message
    else:
        row = jnp.sum(message, axis=0, keepdims=True)
        for device in range(moments_ref.shape[0]):
            moments_ref[device] = row


def inner(left, right, moments, shift=0):
    total = 0.0
    for i, a in enumerate(left):
        for j, b in enumerate(right):
            total = total + (a * b) * moments[i + j + shift]
    return total


def axpy(scale, left, right):
    count = max(len(left), len(right))
    result = []
    for i in range(count):
        if i >= len(left):
            result.append(right[i])
        elif i >= len(right):
            result.append(scale * left[i])
        else:
            result.append(scale * left[i] + right[i])
    return result


def recurrence(moments, centers):
    def operator(poly):
        result = [(1.0 - centers) * a for a in poly] + [jnp.zeros_like(centers)]
        for i, a in enumerate(poly):
            result[i + 1] = result[i + 1] - a
        return result

    one = jnp.ones_like(centers)
    residual, direction, answer = [one], [one], []
    product_now = moments[0]
    for step in range(ITERS):
        image = operator(direction)
        step_size = product_now / inner(direction, image, moments)
        answer = axpy(step_size, direction, answer)
        residual = axpy(-step_size, image, residual)
        if step + 1 < ITERS:
            product_next = inner(residual, residual, moments)
            direction = axpy(product_next / product_now, direction, residual)
            product_now = product_next
    return answer, residual


def finish_kernel(moments_ref, diagonal_ref, *refs):
    solution_ref, residual_ref = refs[-2:]
    streams = [refs[4 * i : 4 * i + 4] for i in range(len(SPLITS))]
    rows = [moments_ref[device] for device in range(moments_ref.shape[0])]
    while len(rows) > 1:
        rows = [a + b for a, b in zip(rows[::2], rows[1::2])]
    row = jnp.broadcast_to(rows[0], (8, 128))
    moments = [jnp.sum(jnp.where(moment_lanes(k), row, 0.0), axis=1, keepdims=True) for k in range(6)]
    place = lax.broadcasted_iota(jnp.int32, (8, 1), 0)
    centers = jnp.zeros((8, 1), jnp.float32)
    for j, center in enumerate(CENTERS):
        centers = jnp.where(place == j, center, centers)
    answer, residual = recurrence(moments, centers)
    packed = [centers, *answer, *residual]
    mean = centers[0:1] + moments[1][0:1] / moments[0][0:1]
    best = jnp.abs(mean - centers[0:1])
    chosen = [p[0:1] for p in packed]
    for j in range(1, len(CENTERS)):
        away = jnp.abs(mean - centers[j : j + 1])
        better = away < best
        best = jnp.where(better, away, best)
        chosen = [jnp.where(better, p[j : j + 1], c) for p, c in zip(packed, chosen)]
    total, layers = diagonal_ref.shape
    chosen = [jnp.broadcast_to(c, (CHUNK, layers)) for c in chosen]
    center, answer, residual = chosen[0], chosen[1:4], chosen[4:8]
    for start in range(0, total, CHUNK):
        here = slice(start, start + CHUNK)
        diagonal = diagonal_ref[here]
        for (low, high), stream in zip(SPLITS, streams):
            for at in range(high - low):
                values = [ref[at, here] for ref in stream]
                q1, q2, q3 = powers(center, *values)
                solution_ref[low + at, here] = answer[0] * values[0] + answer[1] * q1 + answer[2] * q2
                residual_ref[low + at, here] = diagonal * (
                    residual[0] * values[0] + residual[1] * q1 + residual[2] * q2 + residual[3] * q3
                )


def call(kernel, out_shapes, *args, scratch=(), place=pltpu.VMEM):
    whole = pl.BlockSpec(memory_space=pltpu.VMEM)
    if place is pltpu.HBM:
        args = [pltpu.with_memory_space_constraint(a, place) for a in args]
    outs = [o if isinstance(o, jax.ShapeDtypeStruct) else jax.ShapeDtypeStruct(o, jnp.float32) for o in out_shapes]
    return pl.pallas_call(
        kernel,
        out_shape=outs,
        in_specs=[pl.BlockSpec(memory_space=place)] * len(args),
        out_specs=[whole] * len(out_shapes),
        scratch_shapes=[pltpu.VMEM(s, jnp.float32) if isinstance(s, tuple) else s for s in scratch],
        compiler_params=pltpu.CompilerParams(vmem_limit_bytes=24 * 2**20),
    )(*args)


def ring_pairs(groups, tiles):
    beside = [(g * tiles + i, g * tiles + (i ^ 1)) for g in range(groups) for i in range(tiles)]
    across = []
    for g in range(groups):
        for i in range(tiles):
            j = i - 1 if i % 2 == 0 else i + 1
            if j < 0 or j >= tiles:
                across.append((g * tiles + i, (1 - g) * tiles + i))
            else:
                across.append((g * tiles + i, g * tiles + j))
    return beside, across


NAMES = ("diamond", "tile")


def exchange(value):
    beside, across = ring_pairs(lax.axis_size("diamond"), lax.axis_size("tile"))
    far = lax.ppermute(value, NAMES, across)
    near = lax.ppermute(value, NAMES, beside)
    return near, far


def body(adjoint_temp, misfit, viscosity, velocity, forcing, edge_table, pole_table):
    rows, layers = adjoint_temp.shape[2:]
    devices = lax.axis_size("diamond") * lax.axis_size("tile")
    flat, triple = (rows, layers), (3, rows, layers)
    temp, source, visc = (v.reshape(flat) for v in (adjoint_temp, misfit, viscosity))
    visc_near, visc_far = exchange(visc[None])
    temp_near, temp_far = exchange(temp[None])
    table = pltpu.VMEM(edge_table.shape, edge_table.dtype)
    half, side, base, right, part, speed, matrix = call(
        local_kernel,
        [flat, (4, *flat), flat, triple, flat, flat, jax.ShapeDtypeStruct((rows, rows), jnp.bfloat16)],
        temp, source, visc, velocity.reshape(triple), forcing.reshape(triple), edge_table, pole_table,
        scratch=[flat, flat, flat, triple, table, table, pltpu.SemaphoreType.DMA((7,))],
        place=pltpu.HBM,
    )
    shapes = [(high - low, rows, layers) for low, high in SPLITS]
    weights, diagonal, inverse, *first = call(
        weigh_kernel, [(6, *flat), flat, flat, *shapes[:-1]],
        visc_far, visc_near, half, side, base, right, matrix, scratch=[(1, *flat)],
    )
    adjoint_next, *rest = call(
        step_kernel, [flat, shapes[-1]],
        temp_far, temp_near, right, part, speed, inverse, matrix, scratch=[(1, *flat)],
    )
    first += rest
    streams = [[field] for field in first]
    swapped = [exchange(field) for field in first]
    for step in range(ITERS - 1):
        for i, shape in enumerate(shapes):
            near, far = swapped[i]
            (field,) = call(apply_kernel, [shape], far, near, streams[i][-1], weights, matrix, scratch=[shape])
            swapped[i] = exchange(field)
            streams[i].append(field)
    many = (len(CENTERS), *triple)
    moments, left, shift = call(
        early_kernel, [(8, 128), many, many], diagonal, *[field for stream in streams for field in stream]
    )
    for i, shape in enumerate(shapes):
        near, far = swapped[i]
        sums = (8, 128) if i + 1 < len(shapes) else (devices, 1, 128)
        field, moments = call(
            functools.partial(last_kernel, SPLITS[i][0]), [shape, sums],
            far, near, streams[i][-1], weights, matrix, moments, left, shift, scratch=[shape],
        )
        streams[i].append(field)
    moments = lax.all_to_all(moments, NAMES, 0, 0)
    fields = [field for stream in streams for field in stream]
    answer, residual = call(finish_kernel, [triple, triple], moments, diagonal, *fields)
    whole = (3, 1, 1, rows, layers)
    return answer.reshape(whole), residual.reshape(whole), adjoint_next.reshape(adjoint_temp.shape)


def solution(mesh):
    flat = P("diamond", "tile", None, None)
    triple = P(None, "diamond", "tile", None, None)
    return jax.shard_map(
        body,
        mesh=mesh,
        in_specs=(flat, flat, flat, triple, triple, P(), P()),
        out_specs=(triple, triple, flat),
        check_vma=False,
    )
```

```python
import functools

import jax
import jax.numpy as jnp
from jax import lax
from jax.experimental import pallas as pl
from jax.experimental.pallas import tpu as pltpu
from jax.sharding import PartitionSpec as P

ITERS = 3
TIME_STEP = 0.1
DIFFUSION = 1.0
MASS_TERM = 0.5
BUOYANCY = 1.0
CENTERS = (0.0, 0.45, -0.45, 0.75, -0.75, 0.95, -0.95)
CHUNK = 32
SPLITS = ((0, 1), (1, 2), (2, 3))


def rows_around(load, start, total):
    low, high = max(start - 8, 0), min(start + CHUNK + 8, total)
    block = load(low, high)
    at = start - low
    after = pltpu.roll(block, high - low - 1, 0)[at : at + CHUNK]
    before = pltpu.roll(block, 1, 0)[at : at + CHUNK]
    return block[at : at + CHUNK], after, before


def layers_around(block):
    count = block.shape[1]
    return pltpu.roll(block, count - 1, 1), pltpu.roll(block, 1, 1)


def split3(value):
    top = value.astype(jnp.bfloat16)
    rest = value - top.astype(jnp.float32)
    middle = rest.astype(jnp.bfloat16)
    bottom = (rest - middle.astype(jnp.float32)).astype(jnp.bfloat16)
    return [top, middle, bottom]


def fold_matrix(edge_ref, pole_ref):
    group, tile = lax.axis_index("diamond"), lax.axis_index("tile")
    final = lax.axis_size("tile") - 1
    count = edge_ref.shape[1]
    rows = lax.broadcasted_iota(jnp.int32, (count, count), 0)
    same = lax.broadcasted_iota(jnp.int32, (1, count), 1)
    edge = jnp.where(group == 0, edge_ref[1:2], edge_ref[0:1])
    pole = jnp.where(group == 0, pole_ref[1:2], pole_ref[0:1])
    line = jnp.where(tile == 0, pole, jnp.where(tile == final, edge, same))
    return (rows == line).astype(jnp.bfloat16)


def unfold(matrix_ref, far_ref, out_ref):
    layers = far_ref.shape[2]
    for at in range(far_ref.shape[0]):
        pieces = jnp.concatenate(split3(far_ref[at]), axis=1)
        moved = jnp.dot(matrix_ref[...], pieces, preferred_element_type=jnp.float32)
        out_ref[at] = (
            moved[:, :layers] + moved[:, layers : 2 * layers] + moved[:, 2 * layers :]
        )


def local_kernel(
    temp_hbm, misfit_hbm, visc_hbm, velocity_hbm, forcing_hbm, edge_hbm, pole_hbm,
    half_ref, side_ref, base_ref, right_ref, part_ref, speed_ref, matrix_ref, temp_ref,
    misfit_ref, visc_ref, velocity_ref, edge_ref, pole_ref, sems,
):
    sources = [visc_hbm, temp_hbm, edge_hbm, pole_hbm, velocity_hbm, misfit_hbm, forcing_hbm]
    targets = [visc_ref, temp_ref, edge_ref, pole_ref, velocity_ref, misfit_ref, right_ref]
    copies = [pltpu.make_async_copy(s, t, sems.at[i]) for i, (s, t) in enumerate(zip(sources, targets))]
    for copy in copies:
        copy.start()
    odd = lax.rem(lax.axis_index("tile"), 2)
    half = jnp.where(odd == 0, 0.5, -0.5).astype(jnp.float32)
    total, layers = temp_ref.shape
    for copy in copies:
        copy.wait()
    matrix_ref[...] = fold_matrix(edge_ref, pole_ref)
    for start in range(0, total, CHUNK):
        here = slice(start, start + CHUNK)
        visc, visc_after, visc_before = rows_around(lambda a, b: visc_ref[a:b], start, total)
        temp, temp_after, temp_before = rows_around(lambda a, b: temp_ref[a:b], start, total)
        place = start + lax.broadcasted_iota(jnp.int32, (CHUNK, layers), 0)
        layer = lax.broadcasted_iota(jnp.int32, (CHUNK, layers), 1)
        inside = [place < total - 1, place > 0, layer < layers - 1, layer > 0]
        visc_near = [visc_after, visc_before, *layers_around(visc)]
        temp_near = [temp_after, temp_before, *layers_around(temp)]
        zero = jnp.zeros_like(visc)
        weights = [jnp.where(m, 0.5 * (visc + v), zero) for m, v in zip(inside, visc_near)]
        temps = [jnp.where(m, t, zero) for m, t in zip(inside, temp_near)]
        half_ref[here] = 0.5 * visc
        for k in range(4):
            side_ref[k, here] = weights[k]
        base_ref[here] = MASS_TERM + sum(weights)
        transport = 0.5 * (
            velocity_ref[1, here] * (temps[0] - temps[1]) + velocity_ref[2, here] * (temps[2] - temps[3])
        )
        laplace = sum(temps) - 6.0 * temp
        part_ref[here] = temp + TIME_STEP * (DIFFUSION * laplace + transport) + misfit_ref[here]
        speed_ref[here] = half * velocity_ref[0, here]


def weigh_kernel(
    far_ref, near_ref, half_ref, side_ref, base_ref, right_ref, matrix_ref,
    weights_ref, diagonal_ref, inverse_ref, *refs,
):
    *first_refs, moved_ref = refs
    unfold(matrix_ref, far_ref, moved_ref)
    for start in range(0, half_ref.shape[0], CHUNK):
        here = slice(start, start + CHUNK)
        visc = half_ref[here]
        weights = [visc + 0.5 * near_ref[0, here], visc + 0.5 * moved_ref[0, here]]
        diagonal = base_ref[here] + weights[0] + weights[1]
        diagonal_ref[here] = diagonal
        inverse = 1.0 / diagonal
        inverse_ref[here] = inverse
        for (low, high), first_ref in zip(SPLITS, first_refs):
            for at in range(low, high):
                first_ref[at - low, here] = right_ref[at, here] * inverse
        weights += [side_ref[k, here] for k in range(4)]
        for k in range(6):
            weights_ref[k, here] = weights[k] * inverse


def step_kernel(
    far_ref, near_ref, right_ref, part_ref, speed_ref, inverse_ref, matrix_ref, next_ref, first_ref, moved_ref
):
    unfold(matrix_ref, far_ref, moved_ref)
    for start in range(0, part_ref.shape[0], CHUNK):
        here = slice(start, start + CHUNK)
        near, far = near_ref[0, here], moved_ref[0, here]
        adjoint_next = part_ref[here] + TIME_STEP * (
            DIFFUSION * (near + far) + speed_ref[here] * (near - far)
        )
        next_ref[here] = adjoint_next
        first_ref[0, here] = (right_ref[2, here] + BUOYANCY * adjoint_next) * inverse_ref[here]


def average(start, at, field_ref, near_ref, moved_ref, weights):
    here = slice(start, start + CHUNK)
    mid, after, before = rows_around(lambda a, b: field_ref[at, a:b], start, field_ref.shape[1])
    around = [near_ref[at, here], moved_ref[at, here], after, before, *layers_around(mid)]
    return sum(w * v for w, v in zip(weights, around))


def apply_kernel(far_ref, near_ref, field_ref, weights_ref, matrix_ref, out_ref, moved_ref):
    unfold(matrix_ref, far_ref, moved_ref)
    for start in range(0, field_ref.shape[1], CHUNK):
        here = slice(start, start + CHUNK)
        weights = [weights_ref[k, here] for k in range(6)]
        for at in range(field_ref.shape[0]):
            out_ref[at, here] = average(start, at, field_ref, near_ref, moved_ref, weights)


def fold8(value):
    return jnp.sum(value.reshape(value.shape[0] // 8, 8, value.shape[1]), axis=0)


def moment_lanes(k):
    row = lax.broadcasted_iota(jnp.int32, (8, 128), 0)
    lane = lax.broadcasted_iota(jnp.int32, (8, 128), 1)
    return lane == row + 8 * k


def place_moment(k, sums):
    rows = [jnp.sum(s, axis=0, keepdims=True) for s in sums]
    rows += [rows[0]] * (8 - len(rows))
    column = jnp.sum(jnp.concatenate(rows, axis=0), axis=1, keepdims=True)
    return jnp.where(moment_lanes(k), column, 0.0)


def early_kernel(diagonal_ref, *refs):
    moments_ref, left_ref, shift_ref = refs[-3:]
    total, layers = diagonal_ref.shape
    sums = [[jnp.zeros((8, layers), jnp.float32) for _ in CENTERS] for _ in range(5)]
    for i, (low, high) in enumerate(SPLITS):
        y0_ref, y1_ref, y2_ref = refs[3 * i : 3 * i + 3]
        for start in range(0, total, CHUNK):
            here = slice(start, start + CHUNK)
            diagonal = diagonal_ref[here]
            for at in range(high - low):
                y0, y1, y2 = y0_ref[at, here], y1_ref[at, here], y2_ref[at, here]
                d0 = diagonal * y0
                m0 = fold8(d0 * y0)
                for j, center in enumerate(CENTERS):
                    q1 = y1 - center * y0
                    t2 = y2 - center * y1
                    q2 = t2 - center * q1
                    d1, d2 = diagonal * q1, diagonal * q2
                    left_ref[j, low + at, here] = d2
                    shift_ref[j, low + at, here] = center * (y2 + t2 + q2)
                    sums[0][j] += m0
                    sums[1][j] += fold8(d0 * q1)
                    sums[2][j] += fold8(d1 * q1)
                    sums[3][j] += fold8(d1 * q2)
                    sums[4][j] += fold8(d2 * q2)
    moments_ref[...] = sum(place_moment(k, sums[k]) for k in range(5))


def powers(center, y0, y1, y2, y3):
    q1 = y1 - center * y0
    t2 = y2 - center * y1
    q2 = t2 - center * q1
    q3 = (y3 - center * y2 - center * t2) - center * q2
    return q1, q2, q3


def last_kernel(
    low, far_ref, near_ref, field_ref, weights_ref, matrix_ref, earlier_ref, left_ref, shift_ref,
    out_ref, moments_ref, moved_ref,
):
    unfold(matrix_ref, far_ref, moved_ref)
    total, layers = field_ref.shape[1:]
    sums = [jnp.zeros((8, layers), jnp.float32) for _ in CENTERS]
    for start in range(0, total, CHUNK):
        here = slice(start, start + CHUNK)
        weights = [weights_ref[k, here] for k in range(6)]
        for at in range(field_ref.shape[0]):
            y3 = average(start, at, field_ref, near_ref, moved_ref, weights)
            out_ref[at, here] = y3
            for j in range(len(CENTERS)):
                sums[j] += fold8(left_ref[j, low + at, here] * (y3 - shift_ref[j, low + at, here]))
    message = earlier_ref[...] + place_moment(5, sums)
    if len(moments_ref.shape) == 2:
        moments_ref[...] = message
    else:
        row = jnp.sum(message, axis=0, keepdims=True)
        for device in range(moments_ref.shape[0]):
            moments_ref[device] = row


def inner(left, right, moments, shift=0):
    total = 0.0
    for i, a in enumerate(left):
        for j, b in enumerate(right):
            total = total + (a * b) * moments[i + j + shift]
    return total


def axpy(scale, left, right):
    count = max(len(left), len(right))
    result = []
    for i in range(count):
        if i >= len(left):
            result.append(right[i])
        elif i >= len(right):
            result.append(scale * left[i])
        else:
            result.append(scale * left[i] + right[i])
    return result


def recurrence(moments, centers):
    def operator(poly):
        result = [(1.0 - centers) * a for a in poly] + [jnp.zeros_like(centers)]
        for i, a in enumerate(poly):
            result[i + 1] = result[i + 1] - a
        return result

    one = jnp.ones_like(centers)
    residual, direction, answer = [one], [one], []
    product_now = moments[0]
    for step in range(ITERS):
        image = operator(direction)
        step_size = product_now / inner(direction, image, moments)
        answer = axpy(step_size, direction, answer)
        residual = axpy(-step_size, image, residual)
        if step + 1 < ITERS:
            product_next = inner(residual, residual, moments)
            direction = axpy(product_next / product_now, direction, residual)
            product_now = product_next
    return answer, residual


def finish_kernel(moments_ref, diagonal_ref, *refs):
    *refs, solution_hbm, residual_hbm, solution_ref, residual_ref, sems = refs
    streams = [refs[4 * i : 4 * i + 4] for i in range(len(SPLITS))]
    rows = [moments_ref[device] for device in range(moments_ref.shape[0])]
    while len(rows) > 1:
        rows = [a + b for a, b in zip(rows[::2], rows[1::2])]
    row = jnp.broadcast_to(rows[0], (8, 128))
    moments = [jnp.sum(jnp.where(moment_lanes(k), row, 0.0), axis=1, keepdims=True) for k in range(6)]
    place = lax.broadcasted_iota(jnp.int32, (8, 1), 0)
    centers = jnp.zeros((8, 1), jnp.float32)
    for j, center in enumerate(CENTERS):
        centers = jnp.where(place == j, center, centers)
    answer, residual = recurrence(moments, centers)
    packed = [centers, *answer, *residual]
    mean = centers[0:1] + moments[1][0:1] / moments[0][0:1]
    best = jnp.abs(mean - centers[0:1])
    chosen = [p[0:1] for p in packed]
    for j in range(1, len(CENTERS)):
        away = jnp.abs(mean - centers[j : j + 1])
        better = away < best
        best = jnp.where(better, away, best)
        chosen = [jnp.where(better, p[j : j + 1], c) for p, c in zip(packed, chosen)]
    total, layers = diagonal_ref.shape
    chosen = [jnp.broadcast_to(c, (CHUNK, layers)) for c in chosen]
    center, answer, residual = chosen[0], chosen[1:4], chosen[4:8]
    copies = []
    for (low, high), stream in zip(SPLITS, streams):
        for at in range(high - low):
            for start in range(0, total, CHUNK):
                here = slice(start, start + CHUNK)
                values = [ref[at, here] for ref in stream]
                q1, q2, q3 = powers(center, *values)
                solution_ref[low + at, here] = answer[0] * values[0] + answer[1] * q1 + answer[2] * q2
                residual_ref[low + at, here] = diagonal_ref[here] * (
                    residual[0] * values[0] + residual[1] * q1 + residual[2] * q2 + residual[3] * q3
                )
            for k, (source, target) in enumerate(((solution_ref, solution_hbm), (residual_ref, residual_hbm))):
                copies.append(pltpu.make_async_copy(source.at[low + at], target.at[low + at], sems.at[k, low + at]))
                copies[-1].start()
    for copy in copies:
        copy.wait()


def call(kernel, out_shapes, *args, scratch=(), place=pltpu.VMEM, out_place=pltpu.VMEM):
    if place is pltpu.HBM:
        args = [pltpu.with_memory_space_constraint(a, place) for a in args]
    outs = [o if isinstance(o, jax.ShapeDtypeStruct) else jax.ShapeDtypeStruct(o, jnp.float32) for o in out_shapes]
    return pl.pallas_call(
        kernel,
        out_shape=outs,
        in_specs=[pl.BlockSpec(memory_space=place)] * len(args),
        out_specs=[pl.BlockSpec(memory_space=out_place)] * len(out_shapes),
        scratch_shapes=[pltpu.VMEM(s, jnp.float32) if isinstance(s, tuple) else s for s in scratch],
        compiler_params=pltpu.CompilerParams(vmem_limit_bytes=24 * 2**20),
    )(*args)


def ring_pairs(groups, tiles):
    beside = [(g * tiles + i, g * tiles + (i ^ 1)) for g in range(groups) for i in range(tiles)]
    across = []
    for g in range(groups):
        for i in range(tiles):
            j = i - 1 if i % 2 == 0 else i + 1
            if j < 0 or j >= tiles:
                across.append((g * tiles + i, (1 - g) * tiles + i))
            else:
                across.append((g * tiles + i, g * tiles + j))
    return beside, across


NAMES = ("diamond", "tile")


def exchange(value):
    beside, across = ring_pairs(lax.axis_size("diamond"), lax.axis_size("tile"))
    far = lax.ppermute(value, NAMES, across)
    near = lax.ppermute(value, NAMES, beside)
    return near, far


def body(adjoint_temp, misfit, viscosity, velocity, forcing, edge_table, pole_table):
    rows, layers = adjoint_temp.shape[2:]
    devices = lax.axis_size("diamond") * lax.axis_size("tile")
    flat, triple = (rows, layers), (3, rows, layers)
    temp, source, visc = (v.reshape(flat) for v in (adjoint_temp, misfit, viscosity))
    visc_near, visc_far = exchange(visc[None])
    table = pltpu.VMEM(edge_table.shape, edge_table.dtype)
    half, side, base, right, part, speed, matrix, sent = call(
        local_kernel,
        [flat, (4, *flat), flat, triple, flat, flat, jax.ShapeDtypeStruct((rows, rows), jnp.bfloat16), flat],
        temp, source, visc, velocity.reshape(triple), forcing.reshape(triple), edge_table, pole_table,
        scratch=[flat, flat, triple, table, table, pltpu.SemaphoreType.DMA((7,))],
        place=pltpu.HBM,
    )
    temp_near, temp_far = exchange(sent[None])
    shapes = [(high - low, rows, layers) for low, high in SPLITS]
    weights, diagonal, inverse, *first = call(
        weigh_kernel, [(6, *flat), flat, flat, *shapes[:-1]],
        visc_far, visc_near, half, side, base, right, matrix, scratch=[(1, *flat)],
    )
    adjoint_next, *rest = call(
        step_kernel, [flat, shapes[-1]],
        temp_far, temp_near, right, part, speed, inverse, matrix, scratch=[(1, *flat)],
    )
    first += rest
    streams = [[field] for field in first]
    swapped = [exchange(field) for field in first]
    for step in range(ITERS - 1):
        for i, shape in enumerate(shapes):
            near, far = swapped[i]
            (field,) = call(apply_kernel, [shape], far, near, streams[i][-1], weights, matrix, scratch=[shape])
            swapped[i] = exchange(field)
            streams[i].append(field)
    many = (len(CENTERS), *triple)
    moments, left, shift = call(
        early_kernel, [(8, 128), many, many], diagonal, *[field for stream in streams for field in stream]
    )
    for i, shape in enumerate(shapes):
        near, far = swapped[i]
        sums = (8, 128) if i + 1 < len(shapes) else (devices, 1, 128)
        field, moments = call(
            functools.partial(last_kernel, SPLITS[i][0]), [shape, sums],
            far, near, streams[i][-1], weights, matrix, moments, left, shift, scratch=[shape],
        )
        streams[i].append(field)
    moments = lax.all_to_all(moments, NAMES, 0, 0)
    fields = [field for stream in streams for field in stream]
    answer, residual = call(
        finish_kernel, [triple, triple], moments, diagonal, *fields,
        scratch=[triple, triple, pltpu.SemaphoreType.DMA((2, 3))], out_place=pltpu.HBM,
    )
    whole = (3, 1, 1, rows, layers)
    return answer.reshape(whole), residual.reshape(whole), adjoint_next.reshape(adjoint_temp.shape)


def solution(mesh):
    flat = P("diamond", "tile", None, None)
    triple = P(None, "diamond", "tile", None, None)
    return jax.shard_map(
        body,
        mesh=mesh,
        in_specs=(flat, flat, flat, triple, triple, P(), P()),
        out_specs=(triple, triple, flat),
        check_vma=False,
    )
```

```python
import functools

import jax
import jax.numpy as jnp
from jax import lax
from jax.experimental import pallas as pl
from jax.experimental.pallas import tpu as pltpu
from jax.sharding import PartitionSpec as P

ITERS = 3
TIME_STEP = 0.1
DIFFUSION = 1.0
MASS_TERM = 0.5
BUOYANCY = 1.0
CENTERS = (0.0, 0.45, -0.45, 0.75, -0.75, 0.95, -0.95)
CHUNK = 32
SPLITS = ((0, 1), (1, 2), (2, 3))


def tile_index():
    return 2 * lax.axis_index("chip") + lax.axis_index("core")


def tile_count():
    return 2 * lax.axis_size("chip")


def rows_around(load, start, total):
    low, high = max(start - 8, 0), min(start + CHUNK + 8, total)
    block = load(low, high)
    at = start - low
    after = pltpu.roll(block, high - low - 1, 0)[at : at + CHUNK]
    before = pltpu.roll(block, 1, 0)[at : at + CHUNK]
    return block[at : at + CHUNK], after, before


def layers_around(block):
    count = block.shape[1]
    return pltpu.roll(block, count - 1, 1), pltpu.roll(block, 1, 1)


def split3(value):
    top = value.astype(jnp.bfloat16)
    rest = value - top.astype(jnp.float32)
    middle = rest.astype(jnp.bfloat16)
    bottom = (rest - middle.astype(jnp.float32)).astype(jnp.bfloat16)
    return [top, middle, bottom]


def fold_matrix(edge_ref, pole_ref):
    group, tile = lax.axis_index("diamond"), tile_index()
    final = tile_count() - 1
    count = edge_ref.shape[1]
    rows = lax.broadcasted_iota(jnp.int32, (count, count), 0)
    same = lax.broadcasted_iota(jnp.int32, (1, count), 1)
    edge = jnp.where(group == 0, edge_ref[1:2], edge_ref[0:1])
    pole = jnp.where(group == 0, pole_ref[1:2], pole_ref[0:1])
    line = jnp.where(tile == 0, pole, jnp.where(tile == final, edge, same))
    return (rows == line).astype(jnp.bfloat16)


def unfold(matrix_ref, far_ref, out_ref):
    layers = far_ref.shape[2]
    for at in range(far_ref.shape[0]):
        pieces = jnp.concatenate(split3(far_ref[at]), axis=1)
        moved = jnp.dot(matrix_ref[...], pieces, preferred_element_type=jnp.float32)
        out_ref[at] = (
            moved[:, :layers] + moved[:, layers : 2 * layers] + moved[:, 2 * layers :]
        )


def local_kernel(
    temp_hbm, misfit_hbm, visc_hbm, velocity_hbm, forcing_hbm, edge_hbm, pole_hbm,
    half_ref, side_ref, base_ref, right_ref, part_ref, speed_ref, matrix_ref, temp_ref,
    misfit_ref, visc_ref, velocity_ref, edge_ref, pole_ref, sems,
):
    sources = [visc_hbm, temp_hbm, edge_hbm, pole_hbm, velocity_hbm, misfit_hbm, forcing_hbm]
    targets = [visc_ref, temp_ref, edge_ref, pole_ref, velocity_ref, misfit_ref, right_ref]
    copies = [pltpu.make_async_copy(s, t, sems.at[i]) for i, (s, t) in enumerate(zip(sources, targets))]
    for copy in copies:
        copy.start()
    odd = lax.axis_index("core")
    half = jnp.where(odd == 0, 0.5, -0.5).astype(jnp.float32)
    total, layers = temp_ref.shape
    for copy in copies:
        copy.wait()
    matrix_ref[...] = fold_matrix(edge_ref, pole_ref)
    for start in range(0, total, CHUNK):
        here = slice(start, start + CHUNK)
        visc, visc_after, visc_before = rows_around(lambda a, b: visc_ref[a:b], start, total)
        temp, temp_after, temp_before = rows_around(lambda a, b: temp_ref[a:b], start, total)
        place = start + lax.broadcasted_iota(jnp.int32, (CHUNK, layers), 0)
        layer = lax.broadcasted_iota(jnp.int32, (CHUNK, layers), 1)
        inside = [place < total - 1, place > 0, layer < layers - 1, layer > 0]
        visc_near = [visc_after, visc_before, *layers_around(visc)]
        temp_near = [temp_after, temp_before, *layers_around(temp)]
        zero = jnp.zeros_like(visc)
        weights = [jnp.where(m, 0.5 * (visc + v), zero) for m, v in zip(inside, visc_near)]
        temps = [jnp.where(m, t, zero) for m, t in zip(inside, temp_near)]
        half_ref[here] = 0.5 * visc
        for k in range(4):
            side_ref[k, here] = weights[k]
        base_ref[here] = MASS_TERM + sum(weights)
        transport = 0.5 * (
            velocity_ref[1, here] * (temps[0] - temps[1]) + velocity_ref[2, here] * (temps[2] - temps[3])
        )
        laplace = sum(temps) - 6.0 * temp
        part_ref[here] = temp + TIME_STEP * (DIFFUSION * laplace + transport) + misfit_ref[here]
        speed_ref[here] = half * velocity_ref[0, here]


def weigh_kernel(
    far_ref, near_ref, half_ref, side_ref, base_ref, right_ref, matrix_ref,
    weights_ref, diagonal_ref, inverse_ref, *refs,
):
    *first_refs, moved_ref = refs
    unfold(matrix_ref, far_ref, moved_ref)
    for start in range(0, half_ref.shape[0], CHUNK):
        here = slice(start, start + CHUNK)
        visc = half_ref[here]
        weights = [visc + 0.5 * near_ref[0, here], visc + 0.5 * moved_ref[0, here]]
        diagonal = base_ref[here] + weights[0] + weights[1]
        diagonal_ref[here] = diagonal
        inverse = 1.0 / diagonal
        inverse_ref[here] = inverse
        for (low, high), first_ref in zip(SPLITS, first_refs):
            for at in range(low, high):
                first_ref[at - low, here] = right_ref[at, here] * inverse
        weights += [side_ref[k, here] for k in range(4)]
        for k in range(6):
            weights_ref[k, here] = weights[k] * inverse


def step_kernel(
    far_ref, near_ref, right_ref, part_ref, speed_ref, inverse_ref, matrix_ref, next_ref, first_ref, moved_ref
):
    unfold(matrix_ref, far_ref, moved_ref)
    for start in range(0, part_ref.shape[0], CHUNK):
        here = slice(start, start + CHUNK)
        near, far = near_ref[0, here], moved_ref[0, here]
        adjoint_next = part_ref[here] + TIME_STEP * (
            DIFFUSION * (near + far) + speed_ref[here] * (near - far)
        )
        next_ref[here] = adjoint_next
        first_ref[0, here] = (right_ref[2, here] + BUOYANCY * adjoint_next) * inverse_ref[here]


def average(start, at, field_ref, near_ref, moved_ref, weights):
    here = slice(start, start + CHUNK)
    mid, after, before = rows_around(lambda a, b: field_ref[at, a:b], start, field_ref.shape[1])
    around = [near_ref[at, here], moved_ref[at, here], after, before, *layers_around(mid)]
    return sum(w * v for w, v in zip(weights, around))


def apply_kernel(far_ref, near_ref, field_ref, weights_ref, matrix_ref, out_ref, moved_ref):
    unfold(matrix_ref, far_ref, moved_ref)
    for start in range(0, field_ref.shape[1], CHUNK):
        here = slice(start, start + CHUNK)
        weights = [weights_ref[k, here] for k in range(6)]
        for at in range(field_ref.shape[0]):
            out_ref[at, here] = average(start, at, field_ref, near_ref, moved_ref, weights)


def fold8(value):
    return jnp.sum(value.reshape(value.shape[0] // 8, 8, value.shape[1]), axis=0)


def moment_lanes(k):
    row = lax.broadcasted_iota(jnp.int32, (8, 128), 0)
    lane = lax.broadcasted_iota(jnp.int32, (8, 128), 1)
    return lane == row + 8 * k


def place_moment(k, sums):
    rows = [jnp.sum(s, axis=0, keepdims=True) for s in sums]
    rows += [rows[0]] * (8 - len(rows))
    column = jnp.sum(jnp.concatenate(rows, axis=0), axis=1, keepdims=True)
    return jnp.where(moment_lanes(k), column, 0.0)


def early_kernel(diagonal_ref, *refs):
    moments_ref, left_ref, shift_ref = refs[-3:]
    total, layers = diagonal_ref.shape
    sums = [[jnp.zeros((8, layers), jnp.float32) for _ in CENTERS] for _ in range(5)]
    for i, (low, high) in enumerate(SPLITS):
        y0_ref, y1_ref, y2_ref = refs[3 * i : 3 * i + 3]
        for start in range(0, total, CHUNK):
            here = slice(start, start + CHUNK)
            diagonal = diagonal_ref[here]
            for at in range(high - low):
                y0, y1, y2 = y0_ref[at, here], y1_ref[at, here], y2_ref[at, here]
                d0 = diagonal * y0
                m0 = fold8(d0 * y0)
                for j, center in enumerate(CENTERS):
                    q1 = y1 - center * y0
                    t2 = y2 - center * y1
                    q2 = t2 - center * q1
                    d1, d2 = diagonal * q1, diagonal * q2
                    left_ref[j, low + at, here] = d2
                    shift_ref[j, low + at, here] = center * (y2 + t2 + q2)
                    sums[0][j] += m0
                    sums[1][j] += fold8(d0 * q1)
                    sums[2][j] += fold8(d1 * q1)
                    sums[3][j] += fold8(d1 * q2)
                    sums[4][j] += fold8(d2 * q2)
    moments_ref[...] = sum(place_moment(k, sums[k]) for k in range(5))


def powers(center, y0, y1, y2, y3):
    q1 = y1 - center * y0
    t2 = y2 - center * y1
    q2 = t2 - center * q1
    q3 = (y3 - center * y2 - center * t2) - center * q2
    return q1, q2, q3


def last_kernel(
    low, far_ref, near_ref, field_ref, weights_ref, matrix_ref, earlier_ref, left_ref, shift_ref,
    out_ref, moments_ref, moved_ref,
):
    unfold(matrix_ref, far_ref, moved_ref)
    total, layers = field_ref.shape[1:]
    sums = [jnp.zeros((8, layers), jnp.float32) for _ in CENTERS]
    for start in range(0, total, CHUNK):
        here = slice(start, start + CHUNK)
        weights = [weights_ref[k, here] for k in range(6)]
        for at in range(field_ref.shape[0]):
            y3 = average(start, at, field_ref, near_ref, moved_ref, weights)
            out_ref[at, here] = y3
            for j in range(len(CENTERS)):
                sums[j] += fold8(left_ref[j, low + at, here] * (y3 - shift_ref[j, low + at, here]))
    message = earlier_ref[...] + place_moment(5, sums)
    moments_ref[...] = jnp.sum(message, axis=0, keepdims=True) if moments_ref.shape[0] == 1 else message


def inner(left, right, moments, shift=0):
    total = 0.0
    for i, a in enumerate(left):
        for j, b in enumerate(right):
            total = total + (a * b) * moments[i + j + shift]
    return total


def axpy(scale, left, right):
    count = max(len(left), len(right))
    result = []
    for i in range(count):
        if i >= len(left):
            result.append(right[i])
        elif i >= len(right):
            result.append(scale * left[i])
        else:
            result.append(scale * left[i] + right[i])
    return result


def recurrence(moments, centers):
    def operator(poly):
        result = [(1.0 - centers) * a for a in poly] + [jnp.zeros_like(centers)]
        for i, a in enumerate(poly):
            result[i + 1] = result[i + 1] - a
        return result

    one = jnp.ones_like(centers)
    residual, direction, answer = [one], [one], []
    product_now = moments[0]
    for step in range(ITERS):
        image = operator(direction)
        step_size = product_now / inner(direction, image, moments)
        answer = axpy(step_size, direction, answer)
        residual = axpy(-step_size, image, residual)
        if step + 1 < ITERS:
            product_next = inner(residual, residual, moments)
            direction = axpy(product_next / product_now, direction, residual)
            product_now = product_next
    return answer, residual


def finish_kernel(moments_ref, diagonal_ref, next_ref, *refs):
    *refs, solution_hbm, residual_hbm, next_hbm, solution_ref, residual_ref, sems, next_sem = refs
    copies = [pltpu.make_async_copy(next_ref, next_hbm, next_sem)]
    copies[0].start()
    streams = [refs[4 * i : 4 * i + 4] for i in range(len(SPLITS))]
    rows = [moments_ref[device] for device in range(moments_ref.shape[0])]
    while len(rows) > 1:
        rows = [a + b for a, b in zip(rows[::2], rows[1::2])]
    row = jnp.broadcast_to(rows[0], (8, 128))
    moments = [jnp.sum(jnp.where(moment_lanes(k), row, 0.0), axis=1, keepdims=True) for k in range(6)]
    place = lax.broadcasted_iota(jnp.int32, (8, 1), 0)
    centers = jnp.zeros((8, 1), jnp.float32)
    for j, center in enumerate(CENTERS):
        centers = jnp.where(place == j, center, centers)
    answer, residual = recurrence(moments, centers)
    packed = [centers, *answer, *residual]
    mean = centers[0:1] + moments[1][0:1] / moments[0][0:1]
    best = jnp.abs(mean - centers[0:1])
    chosen = [p[0:1] for p in packed]
    for j in range(1, len(CENTERS)):
        away = jnp.abs(mean - centers[j : j + 1])
        better = away < best
        best = jnp.where(better, away, best)
        chosen = [jnp.where(better, p[j : j + 1], c) for p, c in zip(packed, chosen)]
    total, layers = diagonal_ref.shape
    chosen = [jnp.broadcast_to(c, (CHUNK, layers)) for c in chosen]
    center, answer, residual = chosen[0], chosen[1:4], chosen[4:8]
    for (low, high), stream in zip(SPLITS, streams):
        for at in range(high - low):
            for start in range(0, total, CHUNK):
                here = slice(start, start + CHUNK)
                values = [ref[at, here] for ref in stream]
                q1, q2, q3 = powers(center, *values)
                solution_ref[low + at, here] = answer[0] * values[0] + answer[1] * q1 + answer[2] * q2
                residual_ref[low + at, here] = diagonal_ref[here] * (
                    residual[0] * values[0] + residual[1] * q1 + residual[2] * q2 + residual[3] * q3
                )
            for k, (source, target) in enumerate(((solution_ref, solution_hbm), (residual_ref, residual_hbm))):
                copies.append(pltpu.make_async_copy(source.at[low + at], target.at[low + at], sems.at[k, low + at]))
                copies[-1].start()
    for copy in copies:
        copy.wait()


def call(kernel, out_shapes, *args, scratch=(), place=pltpu.VMEM, out_place=pltpu.VMEM):
    if place is pltpu.HBM:
        args = [pltpu.with_memory_space_constraint(a, place) for a in args]
    outs = [o if isinstance(o, jax.ShapeDtypeStruct) else jax.ShapeDtypeStruct(o, jnp.float32) for o in out_shapes]
    return pl.pallas_call(
        kernel,
        out_shape=outs,
        in_specs=[pl.BlockSpec(memory_space=place)] * len(args),
        out_specs=[pl.BlockSpec(memory_space=out_place)] * len(out_shapes),
        scratch_shapes=[pltpu.VMEM(s, jnp.float32) if isinstance(s, tuple) else s for s in scratch],
        compiler_params=pltpu.CompilerParams(vmem_limit_bytes=24 * 2**20),
    )(*args)


def ring_pairs(groups, tiles):
    beside = [(g * tiles + i, g * tiles + (i ^ 1)) for g in range(groups) for i in range(tiles)]
    across = []
    for g in range(groups):
        for i in range(tiles):
            j = i - 1 if i % 2 == 0 else i + 1
            if j < 0 or j >= tiles:
                across.append((g * tiles + i, (1 - g) * tiles + i))
            else:
                across.append((g * tiles + i, g * tiles + j))
    return beside, across


NAMES = ("diamond", "chip", "core")


def exchange(value):
    beside, across = ring_pairs(lax.axis_size("diamond"), tile_count())
    far = lax.ppermute(value, NAMES, across)
    near = lax.ppermute(value, NAMES, beside)
    return near, far


def body(adjoint_temp, misfit, viscosity, velocity, forcing, edge_table, pole_table):
    rows, layers = adjoint_temp.shape[2:]
    chips = lax.axis_size("diamond") * lax.axis_size("chip")
    flat, triple = (rows, layers), (3, rows, layers)
    temp, source, visc = (v.reshape(flat) for v in (adjoint_temp, misfit, viscosity))
    visc_near, visc_far = exchange(visc[None])
    table = pltpu.VMEM(edge_table.shape, edge_table.dtype)
    half, side, base, right, part, speed, matrix, sent = call(
        local_kernel,
        [flat, (4, *flat), flat, triple, flat, flat, jax.ShapeDtypeStruct((rows, rows), jnp.bfloat16), flat],
        temp, source, visc, velocity.reshape(triple), forcing.reshape(triple), edge_table, pole_table,
        scratch=[flat, flat, triple, table, table, pltpu.SemaphoreType.DMA((7,))],
        place=pltpu.HBM,
    )
    temp_near, temp_far = exchange(sent[None])
    shapes = [(high - low, rows, layers) for low, high in SPLITS]
    weights, diagonal, inverse, *first = call(
        weigh_kernel, [(6, *flat), flat, flat, *shapes[:-1]],
        visc_far, visc_near, half, side, base, right, matrix, scratch=[(1, *flat)],
    )
    adjoint_next, *rest = call(
        step_kernel, [flat, shapes[-1]],
        temp_far, temp_near, right, part, speed, inverse, matrix, scratch=[(1, *flat)],
    )
    first += rest
    streams = [[field] for field in first]
    swapped = [exchange(field) for field in first]
    for step in range(ITERS - 1):
        for i, shape in enumerate(shapes):
            near, far = swapped[i]
            (field,) = call(apply_kernel, [shape], far, near, streams[i][-1], weights, matrix, scratch=[shape])
            swapped[i] = exchange(field)
            streams[i].append(field)
    many = (len(CENTERS), *triple)
    moments, left, shift = call(
        early_kernel, [(8, 128), many, many], diagonal, *[field for stream in streams for field in stream]
    )
    for i, shape in enumerate(shapes):
        near, far = swapped[i]
        sums = (8 if i + 1 < len(shapes) else 1, 128)
        field, moments = call(
            functools.partial(last_kernel, SPLITS[i][0]), [shape, sums],
            far, near, streams[i][-1], weights, matrix, moments, left, shift, scratch=[shape],
        )
        streams[i].append(field)
    moments = moments + lax.ppermute(moments, "core", [(0, 1), (1, 0)])
    moments = lax.all_to_all(jnp.broadcast_to(moments, (chips, 1, 128)), NAMES[:2], 0, 0)
    fields = [field for stream in streams for field in stream]
    answer, residual, adjoint_next = call(
        finish_kernel, [triple, triple, flat], moments, diagonal, adjoint_next, *fields,
        scratch=[triple, triple, pltpu.SemaphoreType.DMA((2, 3)), pltpu.SemaphoreType.DMA], out_place=pltpu.HBM,
    )
    whole = (3, 1, 1, rows, layers)
    return answer.reshape(whole), residual.reshape(whole), adjoint_next.reshape(adjoint_temp.shape)


def solution(mesh):
    groups, tiles = mesh.devices.shape
    mesh = jax.sharding.Mesh(mesh.devices.reshape(groups, tiles // 2, 2), NAMES)
    flat = P("diamond", ("chip", "core"), None, None)
    triple = P(None, "diamond", ("chip", "core"), None, None)
    return jax.shard_map(
        body,
        mesh=mesh,
        in_specs=(flat, flat, flat, triple, triple, P(), P()),
        out_specs=(triple, triple, flat),
        check_vma=False,
    )
```

```python
import functools

import jax
import jax.numpy as jnp
from jax import lax
from jax.experimental import pallas as pl
from jax.experimental.pallas import tpu as pltpu
from jax.sharding import PartitionSpec as P

ITERS = 3
TIME_STEP = 0.1
DIFFUSION = 1.0
MASS_TERM = 0.5
BUOYANCY = 1.0
CENTERS = (0.0, 0.45, -0.45, 0.75, -0.75, 0.95, -0.95)
CHUNK = 32
SPLITS = ((0, 1), (1, 2), (2, 3))


def rows_around(load, start, total):
    low, high = max(start - 8, 0), min(start + CHUNK + 8, total)
    block = load(low, high)
    at = start - low
    after = pltpu.roll(block, high - low - 1, 0)[at : at + CHUNK]
    before = pltpu.roll(block, 1, 0)[at : at + CHUNK]
    return block[at : at + CHUNK], after, before


def layers_around(block):
    count = block.shape[1]
    return pltpu.roll(block, count - 1, 1), pltpu.roll(block, 1, 1)


def split3(value):
    top = value.astype(jnp.bfloat16)
    rest = value - top.astype(jnp.float32)
    middle = rest.astype(jnp.bfloat16)
    bottom = (rest - middle.astype(jnp.float32)).astype(jnp.bfloat16)
    return [top, middle, bottom]


def fold_matrix(edge_ref, pole_ref):
    group, tile = lax.axis_index("diamond"), lax.axis_index("tile")
    final = lax.axis_size("tile") - 1
    count = edge_ref.shape[1]
    rows = lax.broadcasted_iota(jnp.int32, (count, count), 0)
    same = lax.broadcasted_iota(jnp.int32, (1, count), 1)
    edge = jnp.where(group == 0, edge_ref[1:2], edge_ref[0:1])
    pole = jnp.where(group == 0, pole_ref[1:2], pole_ref[0:1])
    line = jnp.where(tile == 0, pole, jnp.where(tile == final, edge, same))
    return (rows == line).astype(jnp.bfloat16)


def unfold(matrix_ref, far_ref, out_ref):
    layers = far_ref.shape[2]
    for at in range(far_ref.shape[0]):
        pieces = jnp.concatenate(split3(far_ref[at]), axis=1)
        moved = jnp.dot(matrix_ref[...], pieces, preferred_element_type=jnp.float32)
        out_ref[at] = (
            moved[:, :layers] + moved[:, layers : 2 * layers] + moved[:, 2 * layers :]
        )


def local_kernel(
    temp_hbm, misfit_hbm, visc_hbm, velocity_hbm, forcing_hbm, edge_hbm, pole_hbm,
    half_ref, side_ref, base_ref, right_ref, part_ref, speed_ref, matrix_ref, temp_ref,
    misfit_ref, visc_ref, velocity_ref, edge_ref, pole_ref, sems,
):
    sources = [visc_hbm, temp_hbm, edge_hbm, pole_hbm, velocity_hbm, misfit_hbm, forcing_hbm]
    targets = [visc_ref, temp_ref, edge_ref, pole_ref, velocity_ref, misfit_ref, right_ref]
    copies = [pltpu.make_async_copy(s, t, sems.at[i]) for i, (s, t) in enumerate(zip(sources, targets))]
    for copy in copies:
        copy.start()
    odd = lax.rem(lax.axis_index("tile"), 2)
    half = jnp.where(odd == 0, 0.5, -0.5).astype(jnp.float32)
    total, layers = temp_ref.shape
    for copy in copies:
        copy.wait()
    matrix_ref[...] = fold_matrix(edge_ref, pole_ref)
    for start in range(0, total, CHUNK):
        here = slice(start, start + CHUNK)
        visc, visc_after, visc_before = rows_around(lambda a, b: visc_ref[a:b], start, total)
        temp, temp_after, temp_before = rows_around(lambda a, b: temp_ref[a:b], start, total)
        place = start + lax.broadcasted_iota(jnp.int32, (CHUNK, layers), 0)
        layer = lax.broadcasted_iota(jnp.int32, (CHUNK, layers), 1)
        inside = [place < total - 1, place > 0, layer < layers - 1, layer > 0]
        visc_near = [visc_after, visc_before, *layers_around(visc)]
        temp_near = [temp_after, temp_before, *layers_around(temp)]
        zero = jnp.zeros_like(visc)
        weights = [jnp.where(m, 0.5 * (visc + v), zero) for m, v in zip(inside, visc_near)]
        temps = [jnp.where(m, t, zero) for m, t in zip(inside, temp_near)]
        half_ref[here] = 0.5 * visc
        for k in range(4):
            side_ref[k, here] = weights[k]
        base_ref[here] = MASS_TERM + sum(weights)
        transport = 0.5 * (
            velocity_ref[1, here] * (temps[0] - temps[1]) + velocity_ref[2, here] * (temps[2] - temps[3])
        )
        laplace = sum(temps) - 6.0 * temp
        part_ref[here] = temp + TIME_STEP * (DIFFUSION * laplace + transport) + misfit_ref[here]
        speed_ref[here] = half * velocity_ref[0, here]


def weigh_kernel(
    far_ref, near_ref, half_ref, side_ref, base_ref, right_ref, matrix_ref,
    weights_ref, diagonal_ref, inverse_ref, *refs,
):
    *first_refs, moved_ref = refs
    unfold(matrix_ref, far_ref, moved_ref)
    for start in range(0, half_ref.shape[0], CHUNK):
        here = slice(start, start + CHUNK)
        visc = half_ref[here]
        weights = [visc + 0.5 * near_ref[0, here], visc + 0.5 * moved_ref[0, here]]
        diagonal = base_ref[here] + weights[0] + weights[1]
        diagonal_ref[here] = diagonal
        inverse = 1.0 / diagonal
        inverse_ref[here] = inverse
        for (low, high), first_ref in zip(SPLITS, first_refs):
            for at in range(low, high):
                first_ref[at - low, here] = right_ref[at, here] * inverse
        weights += [side_ref[k, here] for k in range(4)]
        for k in range(6):
            weights_ref[k, here] = weights[k] * inverse


def step_kernel(
    far_ref, near_ref, right_ref, part_ref, speed_ref, inverse_ref, matrix_ref, next_ref, first_ref, moved_ref
):
    unfold(matrix_ref, far_ref, moved_ref)
    for start in range(0, part_ref.shape[0], CHUNK):
        here = slice(start, start + CHUNK)
        near, far = near_ref[0, here], moved_ref[0, here]
        adjoint_next = part_ref[here] + TIME_STEP * (
            DIFFUSION * (near + far) + speed_ref[here] * (near - far)
        )
        next_ref[here] = adjoint_next
        first_ref[0, here] = (right_ref[2, here] + BUOYANCY * adjoint_next) * inverse_ref[here]


def average(start, at, field_ref, near_ref, moved_ref, weights):
    here = slice(start, start + CHUNK)
    mid, after, before = rows_around(lambda a, b: field_ref[at, a:b], start, field_ref.shape[1])
    around = [near_ref[at, here], moved_ref[at, here], after, before, *layers_around(mid)]
    return sum(w * v for w, v in zip(weights, around))


def apply_kernel(far_ref, near_ref, field_ref, weights_ref, matrix_ref, out_ref, moved_ref):
    unfold(matrix_ref, far_ref, moved_ref)
    for start in range(0, field_ref.shape[1], CHUNK):
        here = slice(start, start + CHUNK)
        weights = [weights_ref[k, here] for k in range(6)]
        for at in range(field_ref.shape[0]):
            out_ref[at, here] = average(start, at, field_ref, near_ref, moved_ref, weights)


def fold8(value):
    return jnp.sum(value.reshape(value.shape[0] // 8, 8, value.shape[1]), axis=0)


def moment_lanes(k):
    row = lax.broadcasted_iota(jnp.int32, (8, 128), 0)
    lane = lax.broadcasted_iota(jnp.int32, (8, 128), 1)
    return lane == row + 8 * k


def place_moment(k, sums):
    rows = [jnp.sum(s, axis=0, keepdims=True) for s in sums]
    rows += [rows[0]] * (8 - len(rows))
    column = jnp.sum(jnp.concatenate(rows, axis=0), axis=1, keepdims=True)
    return jnp.where(moment_lanes(k), column, 0.0)


def early_kernel(diagonal_ref, *refs):
    moments_ref, left_ref, shift_ref = refs[-3:]
    total, layers = diagonal_ref.shape
    sums = [[jnp.zeros((8, layers), jnp.float32) for _ in CENTERS] for _ in range(5)]
    for i, (low, high) in enumerate(SPLITS):
        y0_ref, y1_ref, y2_ref = refs[3 * i : 3 * i + 3]
        for start in range(0, total, CHUNK):
            here = slice(start, start + CHUNK)
            diagonal = diagonal_ref[here]
            for at in range(high - low):
                y0, y1, y2 = y0_ref[at, here], y1_ref[at, here], y2_ref[at, here]
                d0 = diagonal * y0
                m0 = fold8(d0 * y0)
                for j, center in enumerate(CENTERS):
                    q1 = y1 - center * y0
                    t2 = y2 - center * y1
                    q2 = t2 - center * q1
                    d1, d2 = diagonal * q1, diagonal * q2
                    left_ref[j, low + at, here] = d2
                    shift_ref[j, low + at, here] = center * (y2 + t2 + q2)
                    sums[0][j] += m0
                    sums[1][j] += fold8(d0 * q1)
                    sums[2][j] += fold8(d1 * q1)
                    sums[3][j] += fold8(d1 * q2)
                    sums[4][j] += fold8(d2 * q2)
    moments_ref[...] = sum(place_moment(k, sums[k]) for k in range(5))


def powers(center, y0, y1, y2, y3):
    q1 = y1 - center * y0
    t2 = y2 - center * y1
    q2 = t2 - center * q1
    q3 = (y3 - center * y2 - center * t2) - center * q2
    return q1, q2, q3


def last_kernel(
    low, far_ref, near_ref, field_ref, weights_ref, matrix_ref, earlier_ref, left_ref, shift_ref,
    out_ref, moments_ref, moved_ref,
):
    unfold(matrix_ref, far_ref, moved_ref)
    total, layers = field_ref.shape[1:]
    sums = [jnp.zeros((8, layers), jnp.float32) for _ in CENTERS]
    for start in range(0, total, CHUNK):
        here = slice(start, start + CHUNK)
        weights = [weights_ref[k, here] for k in range(6)]
        for at in range(field_ref.shape[0]):
            y3 = average(start, at, field_ref, near_ref, moved_ref, weights)
            out_ref[at, here] = y3
            for j in range(len(CENTERS)):
                sums[j] += fold8(left_ref[j, low + at, here] * (y3 - shift_ref[j, low + at, here]))
    message = earlier_ref[...] + place_moment(5, sums)
    if len(moments_ref.shape) == 2:
        moments_ref[...] = message
    else:
        row = jnp.sum(message, axis=0, keepdims=True)
        for device in range(moments_ref.shape[0]):
            moments_ref[device] = row


def inner(left, right, moments, shift=0):
    total = 0.0
    for i, a in enumerate(left):
        for j, b in enumerate(right):
            total = total + (a * b) * moments[i + j + shift]
    return total


def axpy(scale, left, right):
    count = max(len(left), len(right))
    result = []
    for i in range(count):
        if i >= len(left):
            result.append(right[i])
        elif i >= len(right):
            result.append(scale * left[i])
        else:
            result.append(scale * left[i] + right[i])
    return result


def recurrence(moments, centers):
    def operator(poly):
        result = [(1.0 - centers) * a for a in poly] + [jnp.zeros_like(centers)]
        for i, a in enumerate(poly):
            result[i + 1] = result[i + 1] - a
        return result

    one = jnp.ones_like(centers)
    residual, direction, answer = [one], [one], []
    product_now = moments[0]
    for step in range(ITERS):
        image = operator(direction)
        step_size = product_now / inner(direction, image, moments)
        answer = axpy(step_size, direction, answer)
        residual = axpy(-step_size, image, residual)
        if step + 1 < ITERS:
            product_next = inner(residual, residual, moments)
            direction = axpy(product_next / product_now, direction, residual)
            product_now = product_next
    return answer, residual


def finish_kernel(moments_ref, diagonal_ref, next_ref, *refs):
    *refs, solution_hbm, residual_hbm, next_hbm, solution_ref, residual_ref, sems, next_sem = refs
    copies = [pltpu.make_async_copy(next_ref, next_hbm, next_sem)]
    copies[0].start()
    streams = [refs[4 * i : 4 * i + 4] for i in range(len(SPLITS))]
    rows = [moments_ref[device] for device in range(moments_ref.shape[0])]
    while len(rows) > 1:
        rows = [a + b for a, b in zip(rows[::2], rows[1::2])]
    row = jnp.broadcast_to(rows[0], (8, 128))
    moments = [jnp.sum(jnp.where(moment_lanes(k), row, 0.0), axis=1, keepdims=True) for k in range(6)]
    place = lax.broadcasted_iota(jnp.int32, (8, 1), 0)
    centers = jnp.zeros((8, 1), jnp.float32)
    for j, center in enumerate(CENTERS):
        centers = jnp.where(place == j, center, centers)
    answer, residual = recurrence(moments, centers)
    packed = [centers, *answer, *residual]
    mean = centers[0:1] + moments[1][0:1] / moments[0][0:1]
    best = jnp.abs(mean - centers[0:1])
    chosen = [p[0:1] for p in packed]
    for j in range(1, len(CENTERS)):
        away = jnp.abs(mean - centers[j : j + 1])
        better = away < best
        best = jnp.where(better, away, best)
        chosen = [jnp.where(better, p[j : j + 1], c) for p, c in zip(packed, chosen)]
    total, layers = diagonal_ref.shape
    chosen = [jnp.broadcast_to(c, (CHUNK, layers)) for c in chosen]
    center, answer, residual = chosen[0], chosen[1:4], chosen[4:8]
    for (low, high), stream in zip(SPLITS, streams):
        for at in range(high - low):
            for start in range(0, total, CHUNK):
                here = slice(start, start + CHUNK)
                values = [ref[at, here] for ref in stream]
                q1, q2, q3 = powers(center, *values)
                solution_ref[low + at, here] = answer[0] * values[0] + answer[1] * q1 + answer[2] * q2
                residual_ref[low + at, here] = diagonal_ref[here] * (
                    residual[0] * values[0] + residual[1] * q1 + residual[2] * q2 + residual[3] * q3
                )
            for k, (source, target) in enumerate(((solution_ref, solution_hbm), (residual_ref, residual_hbm))):
                copies.append(pltpu.make_async_copy(source.at[low + at], target.at[low + at], sems.at[k, low + at]))
                copies[-1].start()
    for copy in copies:
        copy.wait()


def call(kernel, out_shapes, *args, scratch=(), place=pltpu.VMEM, out_place=pltpu.VMEM):
    if place is pltpu.HBM:
        args = [pltpu.with_memory_space_constraint(a, place) for a in args]
    outs = [o if isinstance(o, jax.ShapeDtypeStruct) else jax.ShapeDtypeStruct(o, jnp.float32) for o in out_shapes]
    return pl.pallas_call(
        kernel,
        out_shape=outs,
        in_specs=[pl.BlockSpec(memory_space=place)] * len(args),
        out_specs=[pl.BlockSpec(memory_space=out_place)] * len(out_shapes),
        scratch_shapes=[pltpu.VMEM(s, jnp.float32) if isinstance(s, tuple) else s for s in scratch],
        compiler_params=pltpu.CompilerParams(vmem_limit_bytes=24 * 2**20),
    )(*args)


def ring_pairs(groups, tiles):
    beside = [(g * tiles + i, g * tiles + (i ^ 1)) for g in range(groups) for i in range(tiles)]
    across = []
    for g in range(groups):
        for i in range(tiles):
            j = i - 1 if i % 2 == 0 else i + 1
            if j < 0 or j >= tiles:
                across.append((g * tiles + i, (1 - g) * tiles + i))
            else:
                across.append((g * tiles + i, g * tiles + j))
    return beside, across


NAMES = ("diamond", "tile")


def exchange(value):
    beside, across = ring_pairs(lax.axis_size("diamond"), lax.axis_size("tile"))
    far = lax.ppermute(value, NAMES, across)
    near = lax.ppermute(value, NAMES, beside)
    return near, far


def body(adjoint_temp, misfit, viscosity, velocity, forcing, edge_table, pole_table):
    rows, layers = adjoint_temp.shape[2:]
    devices = lax.axis_size("diamond") * lax.axis_size("tile")
    flat, triple = (rows, layers), (3, rows, layers)
    temp, source, visc = (v.reshape(flat) for v in (adjoint_temp, misfit, viscosity))
    visc_near, visc_far = exchange(visc[None])
    table = pltpu.VMEM(edge_table.shape, edge_table.dtype)
    half, side, base, right, part, speed, matrix, sent = call(
        local_kernel,
        [flat, (4, *flat), flat, triple, flat, flat, jax.ShapeDtypeStruct((rows, rows), jnp.bfloat16), flat],
        temp, source, visc, velocity.reshape(triple), forcing.reshape(triple), edge_table, pole_table,
        scratch=[flat, flat, triple, table, table, pltpu.SemaphoreType.DMA((7,))],
        place=pltpu.HBM,
    )
    temp_near, temp_far = exchange(sent[None])
    shapes = [(high - low, rows, layers) for low, high in SPLITS]
    weights, diagonal, inverse, *first = call(
        weigh_kernel, [(6, *flat), flat, flat, *shapes[:-1]],
        visc_far, visc_near, half, side, base, right, matrix, scratch=[(1, *flat)],
    )
    adjoint_next, *rest = call(
        step_kernel, [flat, shapes[-1]],
        temp_far, temp_near, right, part, speed, inverse, matrix, scratch=[(1, *flat)],
    )
    first += rest
    streams = [[field] for field in first]
    swapped = [exchange(field) for field in first]
    for step in range(ITERS - 1):
        for i, shape in enumerate(shapes):
            near, far = swapped[i]
            (field,) = call(apply_kernel, [shape], far, near, streams[i][-1], weights, matrix, scratch=[shape])
            swapped[i] = exchange(field)
            streams[i].append(field)
    many = (len(CENTERS), *triple)
    moments, left, shift = call(
        early_kernel, [(8, 128), many, many], diagonal, *[field for stream in streams for field in stream]
    )
    for i, shape in enumerate(shapes):
        near, far = swapped[i]
        sums = (8, 128) if i + 1 < len(shapes) else (devices, 1, 128)
        field, moments = call(
            functools.partial(last_kernel, SPLITS[i][0]), [shape, sums],
            far, near, streams[i][-1], weights, matrix, moments, left, shift, scratch=[shape],
        )
        streams[i].append(field)
    moments = lax.all_to_all(moments, NAMES, 0, 0)
    fields = [field for stream in streams for field in stream]
    answer, residual, adjoint_next = call(
        finish_kernel, [triple, triple, flat], moments, diagonal, adjoint_next, *fields,
        scratch=[triple, triple, pltpu.SemaphoreType.DMA((2, 3)), pltpu.SemaphoreType.DMA], out_place=pltpu.HBM,
    )
    whole = (3, 1, 1, rows, layers)
    return answer.reshape(whole), residual.reshape(whole), adjoint_next.reshape(adjoint_temp.shape)


def solution(mesh):
    flat = P("diamond", "tile", None, None)
    triple = P(None, "diamond", "tile", None, None)
    return jax.shard_map(
        body,
        mesh=mesh,
        in_specs=(flat, flat, flat, triple, triple, P(), P()),
        out_specs=(triple, triple, flat),
        check_vma=False,
    )
```

```python
import functools

import jax
import jax.numpy as jnp
from jax import lax
from jax.experimental import pallas as pl
from jax.experimental.pallas import tpu as pltpu
from jax.sharding import PartitionSpec as P

ITERS = 3
TIME_STEP = 0.1
DIFFUSION = 1.0
MASS_TERM = 0.5
BUOYANCY = 1.0
CENTERS = (0.0, 0.45, -0.45, 0.75, -0.75, 0.95, -0.95)
CHUNK = 32
SPLITS = ((0, 1), (1, 2), (2, 3))


def rows_around(load, start, total):
    low, high = max(start - 8, 0), min(start + CHUNK + 8, total)
    block = load(low, high)
    at = start - low
    after = pltpu.roll(block, high - low - 1, 0)[at : at + CHUNK]
    before = pltpu.roll(block, 1, 0)[at : at + CHUNK]
    return block[at : at + CHUNK], after, before


def layers_around(block):
    count = block.shape[1]
    return pltpu.roll(block, count - 1, 1), pltpu.roll(block, 1, 1)


def split3(value):
    top = value.astype(jnp.bfloat16)
    rest = value - top.astype(jnp.float32)
    middle = rest.astype(jnp.bfloat16)
    bottom = (rest - middle.astype(jnp.float32)).astype(jnp.bfloat16)
    return [top, middle, bottom]


def fold_matrix(edge_ref, pole_ref):
    group, tile = lax.axis_index("diamond"), lax.axis_index("tile")
    final = lax.axis_size("tile") - 1
    count = edge_ref.shape[1]
    rows = lax.broadcasted_iota(jnp.int32, (count, count), 0)
    same = lax.broadcasted_iota(jnp.int32, (1, count), 1)
    edge = jnp.where(group == 0, edge_ref[1:2], edge_ref[0:1])
    pole = jnp.where(group == 0, pole_ref[1:2], pole_ref[0:1])
    line = jnp.where(tile == 0, pole, jnp.where(tile == final, edge, same))
    return (rows == line).astype(jnp.bfloat16)


def unfold(matrix_ref, far_ref, out_ref):
    layers = far_ref.shape[2]
    for at in range(far_ref.shape[0]):
        pieces = jnp.concatenate(split3(far_ref[at]), axis=1)
        moved = jnp.dot(matrix_ref[...], pieces, preferred_element_type=jnp.float32)
        out_ref[at] = (
            moved[:, :layers] + moved[:, layers : 2 * layers] + moved[:, 2 * layers :]
        )


def local_kernel(
    temp_hbm, misfit_hbm, visc_hbm, velocity_hbm, forcing_hbm, edge_hbm, pole_hbm,
    half_ref, side_ref, base_ref, right_ref, part_ref, speed_ref, matrix_ref, temp_ref,
    misfit_ref, visc_ref, velocity_ref, edge_ref, pole_ref, sems,
):
    sources = [visc_hbm, temp_hbm, edge_hbm, pole_hbm, velocity_hbm, misfit_hbm, forcing_hbm]
    targets = [visc_ref, temp_ref, edge_ref, pole_ref, velocity_ref, misfit_ref, right_ref]
    copies = [pltpu.make_async_copy(s, t, sems.at[i]) for i, (s, t) in enumerate(zip(sources, targets))]
    for copy in copies:
        copy.start()
    odd = lax.rem(lax.axis_index("tile"), 2)
    half = jnp.where(odd == 0, 0.5, -0.5).astype(jnp.float32)
    total, layers = temp_ref.shape
    for copy in copies:
        copy.wait()
    matrix_ref[...] = fold_matrix(edge_ref, pole_ref)
    for start in range(0, total, CHUNK):
        here = slice(start, start + CHUNK)
        visc, visc_after, visc_before = rows_around(lambda a, b: visc_ref[a:b], start, total)
        temp, temp_after, temp_before = rows_around(lambda a, b: temp_ref[a:b], start, total)
        place = start + lax.broadcasted_iota(jnp.int32, (CHUNK, layers), 0)
        layer = lax.broadcasted_iota(jnp.int32, (CHUNK, layers), 1)
        inside = [place < total - 1, place > 0, layer < layers - 1, layer > 0]
        visc_near = [visc_after, visc_before, *layers_around(visc)]
        temp_near = [temp_after, temp_before, *layers_around(temp)]
        zero = jnp.zeros_like(visc)
        weights = [jnp.where(m, 0.5 * (visc + v), zero) for m, v in zip(inside, visc_near)]
        temps = [jnp.where(m, t, zero) for m, t in zip(inside, temp_near)]
        half_ref[here] = 0.5 * visc
        for k in range(4):
            side_ref[k, here] = weights[k]
        base_ref[here] = MASS_TERM + sum(weights)
        transport = 0.5 * (
            velocity_ref[1, here] * (temps[0] - temps[1]) + velocity_ref[2, here] * (temps[2] - temps[3])
        )
        laplace = sum(temps) - 6.0 * temp
        part_ref[here] = temp + TIME_STEP * (DIFFUSION * laplace + transport) + misfit_ref[here]
        speed_ref[here] = half * velocity_ref[0, here]


def weigh_kernel(
    far_ref, near_ref, half_ref, side_ref, base_ref, right_ref, matrix_ref,
    weights_ref, diagonal_ref, inverse_ref, *refs,
):
    *first_refs, moved_ref = refs
    unfold(matrix_ref, far_ref, moved_ref)
    for start in range(0, half_ref.shape[0], CHUNK):
        here = slice(start, start + CHUNK)
        visc = half_ref[here]
        weights = [visc + 0.5 * near_ref[0, here], visc + 0.5 * moved_ref[0, here]]
        diagonal = base_ref[here] + weights[0] + weights[1]
        diagonal_ref[here] = diagonal
        inverse = 1.0 / diagonal
        inverse_ref[here] = inverse
        for (low, high), first_ref in zip(SPLITS, first_refs):
            for at in range(low, high):
                first_ref[at - low, here] = right_ref[at, here] * inverse
        weights += [side_ref[k, here] for k in range(4)]
        for k in range(6):
            weights_ref[k, here] = weights[k] * inverse


def step_kernel(
    far_ref, near_ref, right_ref, part_ref, speed_ref, inverse_ref, matrix_ref, next_ref, first_ref, moved_ref
):
    unfold(matrix_ref, far_ref, moved_ref)
    for start in range(0, part_ref.shape[0], CHUNK):
        here = slice(start, start + CHUNK)
        near, far = near_ref[0, here], moved_ref[0, here]
        adjoint_next = part_ref[here] + TIME_STEP * (
            DIFFUSION * (near + far) + speed_ref[here] * (near - far)
        )
        next_ref[here] = adjoint_next
        first_ref[0, here] = (right_ref[2, here] + BUOYANCY * adjoint_next) * inverse_ref[here]


def average(start, at, field_ref, near_ref, moved_ref, weights):
    here = slice(start, start + CHUNK)
    mid, after, before = rows_around(lambda a, b: field_ref[at, a:b], start, field_ref.shape[1])
    around = [near_ref[at, here], moved_ref[at, here], after, before, *layers_around(mid)]
    return sum(w * v for w, v in zip(weights, around))


def apply_kernel(far_ref, near_ref, field_ref, weights_ref, matrix_ref, after_ref, out_ref, moved_ref):
    unfold(matrix_ref, far_ref, moved_ref)
    for start in range(0, field_ref.shape[1], CHUNK):
        here = slice(start, start + CHUNK)
        weights = [weights_ref[k, here] for k in range(6)]
        for at in range(field_ref.shape[0]):
            out_ref[at, here] = average(start, at, field_ref, near_ref, moved_ref, weights)


def fold8(value):
    return jnp.sum(value.reshape(value.shape[0] // 8, 8, value.shape[1]), axis=0)


def moment_lanes(k):
    row = lax.broadcasted_iota(jnp.int32, (8, 128), 0)
    lane = lax.broadcasted_iota(jnp.int32, (8, 128), 1)
    return lane == row + 8 * k


def place_moment(k, sums):
    rows = [jnp.sum(s, axis=0, keepdims=True) for s in sums]
    rows += [rows[0]] * (8 - len(rows))
    column = jnp.sum(jnp.concatenate(rows, axis=0), axis=1, keepdims=True)
    return jnp.where(moment_lanes(k), column, 0.0)


def early_kernel(diagonal_ref, *refs):
    moments_ref, left_ref, shift_ref = refs[-3:]
    total, layers = diagonal_ref.shape
    sums = [[jnp.zeros((8, layers), jnp.float32) for _ in CENTERS] for _ in range(5)]
    for i, (low, high) in enumerate(SPLITS):
        y0_ref, y1_ref, y2_ref = refs[3 * i : 3 * i + 3]
        for start in range(0, total, CHUNK):
            here = slice(start, start + CHUNK)
            diagonal = diagonal_ref[here]
            for at in range(high - low):
                y0, y1, y2 = y0_ref[at, here], y1_ref[at, here], y2_ref[at, here]
                d0 = diagonal * y0
                m0 = fold8(d0 * y0)
                for j, center in enumerate(CENTERS):
                    q1 = y1 - center * y0
                    t2 = y2 - center * y1
                    q2 = t2 - center * q1
                    d1, d2 = diagonal * q1, diagonal * q2
                    left_ref[j, low + at, here] = d2
                    shift_ref[j, low + at, here] = center * (y2 + t2 + q2)
                    sums[0][j] += m0
                    sums[1][j] += fold8(d0 * q1)
                    sums[2][j] += fold8(d1 * q1)
                    sums[3][j] += fold8(d1 * q2)
                    sums[4][j] += fold8(d2 * q2)
    moments_ref[...] = sum(place_moment(k, sums[k]) for k in range(5))


def powers(center, y0, y1, y2, y3):
    q1 = y1 - center * y0
    t2 = y2 - center * y1
    q2 = t2 - center * q1
    q3 = (y3 - center * y2 - center * t2) - center * q2
    return q1, q2, q3


def last_kernel(
    low, far_ref, near_ref, field_ref, weights_ref, matrix_ref, earlier_ref, left_ref, shift_ref,
    out_ref, moments_ref, moved_ref,
):
    unfold(matrix_ref, far_ref, moved_ref)
    total, layers = field_ref.shape[1:]
    sums = [jnp.zeros((8, layers), jnp.float32) for _ in CENTERS]
    for start in range(0, total, CHUNK):
        here = slice(start, start + CHUNK)
        weights = [weights_ref[k, here] for k in range(6)]
        for at in range(field_ref.shape[0]):
            y3 = average(start, at, field_ref, near_ref, moved_ref, weights)
            out_ref[at, here] = y3
            for j in range(len(CENTERS)):
                sums[j] += fold8(left_ref[j, low + at, here] * (y3 - shift_ref[j, low + at, here]))
    message = earlier_ref[...] + place_moment(5, sums)
    if len(moments_ref.shape) == 2:
        moments_ref[...] = message
    else:
        row = jnp.sum(message, axis=0, keepdims=True)
        for device in range(moments_ref.shape[0]):
            moments_ref[device] = row


def inner(left, right, moments, shift=0):
    total = 0.0
    for i, a in enumerate(left):
        for j, b in enumerate(right):
            total = total + (a * b) * moments[i + j + shift]
    return total


def axpy(scale, left, right):
    count = max(len(left), len(right))
    result = []
    for i in range(count):
        if i >= len(left):
            result.append(right[i])
        elif i >= len(right):
            result.append(scale * left[i])
        else:
            result.append(scale * left[i] + right[i])
    return result


def recurrence(moments, centers):
    def operator(poly):
        result = [(1.0 - centers) * a for a in poly] + [jnp.zeros_like(centers)]
        for i, a in enumerate(poly):
            result[i + 1] = result[i + 1] - a
        return result

    one = jnp.ones_like(centers)
    residual, direction, answer = [one], [one], []
    product_now = moments[0]
    for step in range(ITERS):
        image = operator(direction)
        step_size = product_now / inner(direction, image, moments)
        answer = axpy(step_size, direction, answer)
        residual = axpy(-step_size, image, residual)
        if step + 1 < ITERS:
            product_next = inner(residual, residual, moments)
            direction = axpy(product_next / product_now, direction, residual)
            product_now = product_next
    return answer, residual


def finish_kernel(moments_ref, diagonal_ref, next_ref, *refs):
    *refs, solution_hbm, residual_hbm, next_hbm, solution_ref, residual_ref, sems, next_sem = refs
    copies = [pltpu.make_async_copy(next_ref, next_hbm, next_sem)]
    copies[0].start()
    streams = [refs[4 * i : 4 * i + 4] for i in range(len(SPLITS))]
    rows = [moments_ref[device] for device in range(moments_ref.shape[0])]
    while len(rows) > 1:
        rows = [a + b for a, b in zip(rows[::2], rows[1::2])]
    row = jnp.broadcast_to(rows[0], (8, 128))
    moments = [jnp.sum(jnp.where(moment_lanes(k), row, 0.0), axis=1, keepdims=True) for k in range(6)]
    place = lax.broadcasted_iota(jnp.int32, (8, 1), 0)
    centers = jnp.zeros((8, 1), jnp.float32)
    for j, center in enumerate(CENTERS):
        centers = jnp.where(place == j, center, centers)
    answer, residual = recurrence(moments, centers)
    packed = [centers, *answer, *residual]
    mean = centers[0:1] + moments[1][0:1] / moments[0][0:1]
    best = jnp.abs(mean - centers[0:1])
    chosen = [p[0:1] for p in packed]
    for j in range(1, len(CENTERS)):
        away = jnp.abs(mean - centers[j : j + 1])
        better = away < best
        best = jnp.where(better, away, best)
        chosen = [jnp.where(better, p[j : j + 1], c) for p, c in zip(packed, chosen)]
    total, layers = diagonal_ref.shape
    chosen = [jnp.broadcast_to(c, (CHUNK, layers)) for c in chosen]
    center, answer, residual = chosen[0], chosen[1:4], chosen[4:8]
    for (low, high), stream in zip(SPLITS, streams):
        for at in range(high - low):
            for start in range(0, total, CHUNK):
                here = slice(start, start + CHUNK)
                values = [ref[at, here] for ref in stream]
                q1, q2, q3 = powers(center, *values)
                solution_ref[low + at, here] = answer[0] * values[0] + answer[1] * q1 + answer[2] * q2
                residual_ref[low + at, here] = diagonal_ref[here] * (
                    residual[0] * values[0] + residual[1] * q1 + residual[2] * q2 + residual[3] * q3
                )
            for k, (source, target) in enumerate(((solution_ref, solution_hbm), (residual_ref, residual_hbm))):
                copies.append(pltpu.make_async_copy(source.at[low + at], target.at[low + at], sems.at[k, low + at]))
                copies[-1].start()
    for copy in copies:
        copy.wait()


def call(kernel, out_shapes, *args, scratch=(), place=pltpu.VMEM, out_place=pltpu.VMEM):
    if place is pltpu.HBM:
        args = [pltpu.with_memory_space_constraint(a, place) for a in args]
    outs = [o if isinstance(o, jax.ShapeDtypeStruct) else jax.ShapeDtypeStruct(o, jnp.float32) for o in out_shapes]
    return pl.pallas_call(
        kernel,
        out_shape=outs,
        in_specs=[pl.BlockSpec(memory_space=place)] * len(args),
        out_specs=[pl.BlockSpec(memory_space=out_place)] * len(out_shapes),
        scratch_shapes=[pltpu.VMEM(s, jnp.float32) if isinstance(s, tuple) else s for s in scratch],
        compiler_params=pltpu.CompilerParams(vmem_limit_bytes=24 * 2**20),
    )(*args)


def ring_pairs(groups, tiles):
    beside = [(g * tiles + i, g * tiles + (i ^ 1)) for g in range(groups) for i in range(tiles)]
    across = []
    for g in range(groups):
        for i in range(tiles):
            j = i - 1 if i % 2 == 0 else i + 1
            if j < 0 or j >= tiles:
                across.append((g * tiles + i, (1 - g) * tiles + i))
            else:
                across.append((g * tiles + i, g * tiles + j))
    return beside, across


NAMES = ("diamond", "tile")


def exchange(value):
    beside, across = ring_pairs(lax.axis_size("diamond"), lax.axis_size("tile"))
    far = lax.ppermute(value, NAMES, across)
    near = lax.ppermute(value, NAMES, beside)
    return near, far


def body(adjoint_temp, misfit, viscosity, velocity, forcing, edge_table, pole_table):
    rows, layers = adjoint_temp.shape[2:]
    devices = lax.axis_size("diamond") * lax.axis_size("tile")
    flat, triple = (rows, layers), (3, rows, layers)
    temp, source, visc = (v.reshape(flat) for v in (adjoint_temp, misfit, viscosity))
    visc_near, visc_far = exchange(visc[None])
    table = pltpu.VMEM(edge_table.shape, edge_table.dtype)
    half, side, base, right, part, speed, matrix, sent = call(
        local_kernel,
        [flat, (4, *flat), flat, triple, flat, flat, jax.ShapeDtypeStruct((rows, rows), jnp.bfloat16), flat],
        temp, source, visc, velocity.reshape(triple), forcing.reshape(triple), edge_table, pole_table,
        scratch=[flat, flat, triple, table, table, pltpu.SemaphoreType.DMA((7,))],
        place=pltpu.HBM,
    )
    temp_near, temp_far = exchange(sent[None])
    shapes = [(high - low, rows, layers) for low, high in SPLITS]
    weights, diagonal, inverse, *first = call(
        weigh_kernel, [(6, *flat), flat, flat, *shapes[:-1]],
        visc_far, visc_near, half, side, base, right, matrix, scratch=[(1, *flat)],
    )
    adjoint_next, *rest = call(
        step_kernel, [flat, shapes[-1]],
        temp_far, temp_near, right, part, speed, inverse, matrix, scratch=[(1, *flat)],
    )
    first += rest
    streams = [[field] for field in first]
    swapped = [exchange(field) for field in first]
    for step in range(ITERS - 1):
        for i, shape in enumerate(shapes):
            near, far = swapped[i]
            after = swapped[0][0] if step + 2 == ITERS and i + 1 == len(shapes) else near
            (field,) = call(apply_kernel, [shape], far, near, streams[i][-1], weights, matrix, after, scratch=[shape])
            swapped[i] = exchange(field)
            streams[i].append(field)
    many = (len(CENTERS), *triple)
    moments, left, shift = call(
        early_kernel, [(8, 128), many, many], diagonal, *[field for stream in streams for field in stream]
    )
    for i, shape in enumerate(shapes):
        near, far = swapped[i]
        sums = (8, 128) if i + 1 < len(shapes) else (devices, 1, 128)
        field, moments = call(
            functools.partial(last_kernel, SPLITS[i][0]), [shape, sums],
            far, near, streams[i][-1], weights, matrix, moments, left, shift, scratch=[shape],
        )
        streams[i].append(field)
    moments = lax.all_to_all(moments, NAMES, 0, 0)
    fields = [field for stream in streams for field in stream]
    answer, residual, adjoint_next = call(
        finish_kernel, [triple, triple, flat], moments, diagonal, adjoint_next, *fields,
        scratch=[triple, triple, pltpu.SemaphoreType.DMA((2, 3)), pltpu.SemaphoreType.DMA], out_place=pltpu.HBM,
    )
    whole = (3, 1, 1, rows, layers)
    return answer.reshape(whole), residual.reshape(whole), adjoint_next.reshape(adjoint_temp.shape)


def solution(mesh):
    flat = P("diamond", "tile", None, None)
    triple = P(None, "diamond", "tile", None, None)
    return jax.shard_map(
        body,
        mesh=mesh,
        in_specs=(flat, flat, flat, triple, triple, P(), P()),
        out_specs=(triple, triple, flat),
        check_vma=False,
    )
```

```python
import jax
import jax.numpy as jnp
from jax import lax
from jax.experimental import pallas as pl
from jax.experimental.pallas import tpu as pltpu
from jax.sharding import PartitionSpec as P

ITERS = 3
TIME_STEP = 0.1
DIFFUSION = 1.0
MASS_TERM = 0.5
BUOYANCY = 1.0
CENTERS = (0.0, 0.45, -0.45, 0.75, -0.75, 0.95, -0.95)
CHUNK = 32
SPLITS = ((0, 1), (1, 2), (2, 3))


def rows_around(load, start, total):
    low, high = max(start - 8, 0), min(start + CHUNK + 8, total)
    block = load(low, high)
    at = start - low
    after = pltpu.roll(block, high - low - 1, 0)[at : at + CHUNK]
    before = pltpu.roll(block, 1, 0)[at : at + CHUNK]
    return block[at : at + CHUNK], after, before


def layers_around(block):
    count = block.shape[1]
    return pltpu.roll(block, count - 1, 1), pltpu.roll(block, 1, 1)


def sides(load, start, total):
    mid, after, before = rows_around(load, start, total)
    place = start + lax.broadcasted_iota(jnp.int32, mid.shape, 0)
    layer = lax.broadcasted_iota(jnp.int32, mid.shape, 1)
    inside = [place < total - 1, place > 0, layer < mid.shape[1] - 1, layer > 0]
    return mid, [after, before, *layers_around(mid)], inside


def split3(value):
    top = value.astype(jnp.bfloat16)
    rest = value - top.astype(jnp.float32)
    middle = rest.astype(jnp.bfloat16)
    bottom = (rest - middle.astype(jnp.float32)).astype(jnp.bfloat16)
    return [top, middle, bottom]


def fold_matrix(edge_ref, pole_ref, kind):
    group, tile = lax.axis_index("diamond"), lax.axis_index("tile")
    last = lax.axis_size("tile") - 1
    count = edge_ref.shape[1]
    rows = lax.broadcasted_iota(jnp.int32, (count, count), 0)
    same = lax.broadcasted_iota(jnp.int32, (1, count), 1)
    side = 1 - group if kind == 1 else group
    skip = 2 if kind == 2 else 0
    edge = jnp.where(side == 0, edge_ref[1:2], edge_ref[0:1])
    pole = jnp.where(side == 0, pole_ref[1:2], pole_ref[0:1])
    line = jnp.where(tile == skip, pole, jnp.where(tile == last - skip, edge, same))
    return (rows == line).astype(jnp.bfloat16)


def unfold(matrix_ref, far_ref, out_ref):
    layers = far_ref.shape[2]
    for at in range(far_ref.shape[0]):
        pieces = jnp.concatenate(split3(far_ref[at]), axis=1)
        moved = jnp.dot(matrix_ref[...], pieces, preferred_element_type=jnp.float32)
        out_ref[at] = (
            moved[:, :layers] + moved[:, layers : 2 * layers] + moved[:, 2 * layers :]
        )


def local_kernel(
    temp_hbm, misfit_hbm, visc_hbm, velocity_hbm, forcing_hbm, edge_hbm, pole_hbm,
    half_ref, side_ref, base_ref, right_ref, part_ref, speed_ref, matrix_ref, back_ref, ahead_ref, temp_ref,
    misfit_ref, visc_ref, velocity_ref, edge_ref, pole_ref, sems,
):
    sources = [visc_hbm, temp_hbm, edge_hbm, pole_hbm, velocity_hbm, misfit_hbm, forcing_hbm]
    targets = [visc_ref, temp_ref, edge_ref, pole_ref, velocity_ref, misfit_ref, right_ref]
    copies = [pltpu.make_async_copy(s, t, sems.at[i]) for i, (s, t) in enumerate(zip(sources, targets))]
    for copy in copies:
        copy.start()
    odd = lax.rem(lax.axis_index("tile"), 2)
    half = jnp.where(odd == 0, 0.5, -0.5).astype(jnp.float32)
    total, layers = temp_ref.shape
    for copy in copies:
        copy.wait()
    for kind, ref in enumerate((matrix_ref, back_ref, ahead_ref)):
        ref[...] = fold_matrix(edge_ref, pole_ref, kind)
    for start in range(0, total, CHUNK):
        here = slice(start, start + CHUNK)
        visc, visc_near, inside = sides(lambda a, b: visc_ref[a:b], start, total)
        temp, temp_near, _ = sides(lambda a, b: temp_ref[a:b], start, total)
        zero = jnp.zeros_like(visc)
        weights = [jnp.where(m, 0.5 * (visc + v), zero) for m, v in zip(inside, visc_near)]
        temps = [jnp.where(m, t, zero) for m, t in zip(inside, temp_near)]
        half_ref[0, here] = 0.5 * visc
        for k in range(4):
            side_ref[k, here] = weights[k]
        base_ref[here] = MASS_TERM + sum(weights)
        transport = 0.5 * (
            velocity_ref[1, here] * (temps[0] - temps[1]) + velocity_ref[2, here] * (temps[2] - temps[3])
        )
        laplace = sum(temps) - 6.0 * temp
        part_ref[here] = temp + TIME_STEP * (DIFFUSION * laplace + transport) + misfit_ref[here]
        speed_ref[here] = half * velocity_ref[0, here]


def weigh_kernel(
    far_ref, near_ref, half_ref, side_ref, base_ref, matrix_ref,
    weights_ref, diagonal_ref, inverse_ref, moved_ref,
):
    unfold(matrix_ref, far_ref, moved_ref)
    for start in range(0, half_ref.shape[1], CHUNK):
        here = slice(start, start + CHUNK)
        visc = half_ref[0, here]
        weights = [visc + 0.5 * near_ref[0, here], visc + 0.5 * moved_ref[0, here]]
        diagonal = base_ref[here] + weights[0] + weights[1]
        diagonal_ref[here] = diagonal
        inverse = 1.0 / diagonal
        inverse_ref[here] = inverse
        weights += [side_ref[k, here] for k in range(4)]
        for k in range(6):
            weights_ref[k, here] = weights[k] * inverse


def step_kernel(
    far_ref, near_ref, right_ref, part_ref, speed_ref, inverse_ref, matrix_ref, next_ref, *refs
):
    *first_refs, moved_ref = refs
    unfold(matrix_ref, far_ref, moved_ref)
    for start in range(0, part_ref.shape[0], CHUNK):
        here = slice(start, start + CHUNK)
        near, far = near_ref[0, here], moved_ref[0, here]
        adjoint_next = part_ref[here] + TIME_STEP * (
            DIFFUSION * (near + far) + speed_ref[here] * (near - far)
        )
        next_ref[here] = adjoint_next
        inverse = inverse_ref[here]
        first_refs[0][0, here] = right_ref[0, here] * inverse
        first_refs[1][0, here] = right_ref[1, here] * inverse
        first_refs[2][0, here] = (right_ref[2, here] + BUOYANCY * adjoint_next) * inverse


def average(start, at, field_ref, near_ref, moved_ref, weights):
    here = slice(start, start + CHUNK)
    mid, after, before = rows_around(lambda a, b: field_ref[at, a:b], start, field_ref.shape[1])
    around = [near_ref[at, here], moved_ref[at, here], after, before, *layers_around(mid)]
    return sum(w * v for w, v in zip(weights, around))


def apply_rows(field_ref, near_ref, moved_ref, weights_ref, out_ref):
    for start in range(0, field_ref.shape[1], CHUNK):
        here = slice(start, start + CHUNK)
        weights = [weights_ref[k, here] for k in range(6)]
        for at in range(field_ref.shape[0]):
            out_ref[at, here] = average(start, at, field_ref, near_ref, moved_ref, weights)


def deep_weigh_kernel(
    second_ref, third_ref, first_ref, half_ref, back_ref, ahead_ref, after_ref, first_weights_ref, second_weights_ref, *moved_refs
):
    unfold(back_ref, half_ref, moved_refs[0])
    unfold(ahead_ref, third_ref, moved_refs[1])
    total = half_ref.shape[1]
    for start in range(0, total, CHUNK):
        here = slice(start, start + CHUNK)
        between = 0.5 * (first_ref[0, here] + second_ref[0, here])
        beyond = (moved_refs[0][0, here], 0.5 * moved_refs[1][0, here])
        outs = (first_weights_ref, second_weights_ref)
        for row_ref, other, out_ref in zip((first_ref, second_ref), beyond, outs):
            visc, near, inside = sides(lambda a, b: row_ref[0, a:b], start, total)
            weights = [between, 0.5 * visc + other]
            weights += [jnp.where(m, 0.5 * (visc + v), jnp.zeros_like(visc)) for m, v in zip(inside, near)]
            inverse = 1.0 / (MASS_TERM + sum(weights))
            for k in range(6):
                out_ref[k, here] = weights[k] * inverse


def deep_first_kernel(
    first_ref, second_ref, third_ref, near_ref, field_ref, weights_ref, first_weights_ref, second_weights_ref,
    matrix_ref, back_ref, ahead_ref, after_ref, out_ref, out_first_ref, out_second_ref, moved_ref,
):
    unfold(matrix_ref, first_ref, moved_ref)
    apply_rows(field_ref, near_ref, moved_ref, weights_ref, out_ref)
    unfold(back_ref, field_ref, moved_ref)
    apply_rows(first_ref, second_ref, moved_ref, first_weights_ref, out_first_ref)
    unfold(ahead_ref, third_ref, moved_ref)
    apply_rows(second_ref, first_ref, moved_ref, second_weights_ref, out_second_ref)


def deep_second_kernel(
    first_ref, second_ref, near_ref, field_ref, weights_ref, first_weights_ref, matrix_ref, back_ref, after_ref,
    out_ref, out_first_ref, moved_ref,
):
    unfold(matrix_ref, first_ref, moved_ref)
    apply_rows(field_ref, near_ref, moved_ref, weights_ref, out_ref)
    unfold(back_ref, field_ref, moved_ref)
    apply_rows(first_ref, second_ref, moved_ref, first_weights_ref, out_first_ref)


def fold8(value):
    return jnp.sum(value.reshape(value.shape[0] // 8, 8, value.shape[1]), axis=0)


def moment_lanes(k):
    row = lax.broadcasted_iota(jnp.int32, (8, 128), 0)
    lane = lax.broadcasted_iota(jnp.int32, (8, 128), 1)
    return lane == row + 8 * k


def place_moment(k, sums):
    rows = [jnp.sum(s, axis=0, keepdims=True) for s in sums]
    rows += [rows[0]] * (8 - len(rows))
    column = jnp.sum(jnp.concatenate(rows, axis=0), axis=1, keepdims=True)
    return jnp.where(moment_lanes(k), column, 0.0)


def early_kernel(diagonal_ref, y0_ref, y1_ref, y2_ref, moments_ref, left_ref, shift_ref):
    total, layers = diagonal_ref.shape
    sums = [[jnp.zeros((8, layers), jnp.float32) for _ in CENTERS] for _ in range(5)]
    for start in range(0, total, CHUNK):
        here = slice(start, start + CHUNK)
        diagonal = diagonal_ref[here]
        for at in range(y0_ref.shape[0]):
            y0, y1, y2 = y0_ref[at, here], y1_ref[at, here], y2_ref[at, here]
            d0 = diagonal * y0
            m0 = fold8(d0 * y0)
            for j, center in enumerate(CENTERS):
                q1 = y1 - center * y0
                t2 = y2 - center * y1
                q2 = t2 - center * q1
                d1, d2 = diagonal * q1, diagonal * q2
                left_ref[j, at, here] = d2
                shift_ref[j, at, here] = center * (y2 + t2 + q2)
                sums[0][j] += m0
                sums[1][j] += fold8(d0 * q1)
                sums[2][j] += fold8(d1 * q1)
                sums[3][j] += fold8(d1 * q2)
                sums[4][j] += fold8(d2 * q2)
    moments_ref[...] = sum(place_moment(k, sums[k]) for k in range(5))


def powers(center, y0, y1, y2, y3):
    q1 = y1 - center * y0
    t2 = y2 - center * y1
    q2 = t2 - center * q1
    q3 = (y3 - center * y2 - center * t2) - center * q2
    return q1, q2, q3


def last_kernel(
    far_ref, near_ref, field_ref, weights_ref, matrix_ref, earlier_ref, left_ref, shift_ref,
    out_ref, moments_ref, moved_ref,
):
    unfold(matrix_ref, far_ref, moved_ref)
    total, layers = field_ref.shape[1:]
    sums = [jnp.zeros((8, layers), jnp.float32) for _ in CENTERS]
    for start in range(0, total, CHUNK):
        here = slice(start, start + CHUNK)
        weights = [weights_ref[k, here] for k in range(6)]
        for at in range(field_ref.shape[0]):
            y3 = average(start, at, field_ref, near_ref, moved_ref, weights)
            out_ref[at, here] = y3
            for j in range(len(CENTERS)):
                sums[j] += fold8(left_ref[j, at, here] * (y3 - shift_ref[j, at, here]))
    message = earlier_ref[...] + place_moment(5, sums)
    if len(moments_ref.shape) == 2:
        moments_ref[...] = message
    else:
        row = jnp.sum(message, axis=0, keepdims=True)
        for device in range(moments_ref.shape[0]):
            moments_ref[device] = row


def inner(left, right, moments, shift=0):
    total = 0.0
    for i, a in enumerate(left):
        for j, b in enumerate(right):
            total = total + (a * b) * moments[i + j + shift]
    return total


def axpy(scale, left, right):
    count = max(len(left), len(right))
    result = []
    for i in range(count):
        if i >= len(left):
            result.append(right[i])
        elif i >= len(right):
            result.append(scale * left[i])
        else:
            result.append(scale * left[i] + right[i])
    return result


def recurrence(moments, centers):
    def operator(poly):
        result = [(1.0 - centers) * a for a in poly] + [jnp.zeros_like(centers)]
        for i, a in enumerate(poly):
            result[i + 1] = result[i + 1] - a
        return result

    one = jnp.ones_like(centers)
    residual, direction, answer = [one], [one], []
    product_now = moments[0]
    for step in range(ITERS):
        image = operator(direction)
        step_size = product_now / inner(direction, image, moments)
        answer = axpy(step_size, direction, answer)
        residual = axpy(-step_size, image, residual)
        if step + 1 < ITERS:
            product_next = inner(residual, residual, moments)
            direction = axpy(product_next / product_now, direction, residual)
            product_now = product_next
    return answer, residual


def finish_kernel(moments_ref, diagonal_ref, next_ref, *refs):
    *refs, solution_hbm, residual_hbm, next_hbm, solution_ref, residual_ref, sems, next_sem = refs
    copies = [pltpu.make_async_copy(next_ref, next_hbm, next_sem)]
    copies[0].start()
    streams = [refs[4 * i : 4 * i + 4] for i in range(len(SPLITS))]
    rows = [moments_ref[device] for device in range(moments_ref.shape[0])]
    while len(rows) > 1:
        rows = [a + b for a, b in zip(rows[::2], rows[1::2])]
    row = jnp.broadcast_to(rows[0], (8, 128))
    moments = [jnp.sum(jnp.where(moment_lanes(k), row, 0.0), axis=1, keepdims=True) for k in range(6)]
    place = lax.broadcasted_iota(jnp.int32, (8, 1), 0)
    centers = jnp.zeros((8, 1), jnp.float32)
    for j, center in enumerate(CENTERS):
        centers = jnp.where(place == j, center, centers)
    answer, residual = recurrence(moments, centers)
    packed = [centers, *answer, *residual]
    mean = centers[0:1] + moments[1][0:1] / moments[0][0:1]
    best = jnp.abs(mean - centers[0:1])
    chosen = [p[0:1] for p in packed]
    for j in range(1, len(CENTERS)):
        away = jnp.abs(mean - centers[j : j + 1])
        better = away < best
        best = jnp.where(better, away, best)
        chosen = [jnp.where(better, p[j : j + 1], c) for p, c in zip(packed, chosen)]
    total, layers = diagonal_ref.shape
    chosen = [jnp.broadcast_to(c, (CHUNK, layers)) for c in chosen]
    center, answer, residual = chosen[0], chosen[1:4], chosen[4:8]
    for (low, high), stream in zip(SPLITS, streams):
        for at in range(high - low):
            for start in range(0, total, CHUNK):
                here = slice(start, start + CHUNK)
                values = [ref[at, here] for ref in stream]
                q1, q2, q3 = powers(center, *values)
                solution_ref[low + at, here] = answer[0] * values[0] + answer[1] * q1 + answer[2] * q2
                residual_ref[low + at, here] = diagonal_ref[here] * (
                    residual[0] * values[0] + residual[1] * q1 + residual[2] * q2 + residual[3] * q3
                )
            for k, (source, target) in enumerate(((solution_ref, solution_hbm), (residual_ref, residual_hbm))):
                copies.append(pltpu.make_async_copy(source.at[low + at], target.at[low + at], sems.at[k, low + at]))
                copies[-1].start()
    for copy in copies:
        copy.wait()


def call(kernel, out_shapes, *args, scratch=(), place=pltpu.VMEM, out_place=pltpu.VMEM):
    if place is pltpu.HBM:
        args = [pltpu.with_memory_space_constraint(a, place) for a in args]
    outs = [o if isinstance(o, jax.ShapeDtypeStruct) else jax.ShapeDtypeStruct(o, jnp.float32) for o in out_shapes]
    return pl.pallas_call(
        kernel,
        out_shape=outs,
        in_specs=[pl.BlockSpec(memory_space=place)] * len(args),
        out_specs=[pl.BlockSpec(memory_space=out_place)] * len(out_shapes),
        scratch_shapes=[pltpu.VMEM(s, jnp.float32) if isinstance(s, tuple) else s for s in scratch],
        compiler_params=pltpu.CompilerParams(vmem_limit_bytes=24 * 2**20),
    )(*args)


def ring_pairs(groups, tiles):
    beside = [(g * tiles + i, g * tiles + (i ^ 1)) for g in range(groups) for i in range(tiles)]
    across = []
    for g in range(groups):
        for i in range(tiles):
            j = i - 1 if i % 2 == 0 else i + 1
            if j < 0 or j >= tiles:
                across.append((g * tiles + i, (1 - g) * tiles + i))
            else:
                across.append((g * tiles + i, g * tiles + j))
    return beside, across


NAMES = ("diamond", "tile")


def neighbour(value):
    beside, _ = ring_pairs(lax.axis_size("diamond"), lax.axis_size("tile"))
    return lax.ppermute(value, NAMES, beside)


def far_row(value, distance):
    tiles = lax.axis_size("tile")
    size = lax.axis_size("diamond") * tiles
    device = [i if i < tiles else tiles + size - 1 - i for i in range(size)]
    pairs = []
    for place in range(size):
        source = (place - distance if place % 2 == 0 else place + distance) % size
        pairs.append((device[source], device[place]))
    return lax.ppermute(value, NAMES, sorted(pairs))


def exchange(value):
    return neighbour(value), far_row(value, 1)


def body(adjoint_temp, misfit, viscosity, velocity, forcing, edge_table, pole_table):
    rows, layers = adjoint_temp.shape[2:]
    devices = lax.axis_size("diamond") * lax.axis_size("tile")
    flat, triple, single, double = (rows, layers), (3, rows, layers), (1, rows, layers), (2, rows, layers)
    temp, source, visc = (v.reshape(flat) for v in (adjoint_temp, misfit, viscosity))
    visc_near, visc_far = exchange(visc[None])
    visc_second, visc_third = far_row(visc[None], 2), far_row(visc[None], 3)
    table = pltpu.VMEM(edge_table.shape, edge_table.dtype)
    square = jax.ShapeDtypeStruct((rows, rows), jnp.bfloat16)
    half, side, base, right, part, speed, matrix, back, ahead, sent = call(
        local_kernel, [single, (4, *flat), flat, triple, flat, flat, square, square, square, flat],
        temp, source, visc, velocity.reshape(triple), forcing.reshape(triple), edge_table, pole_table,
        scratch=[flat, flat, triple, table, table, pltpu.SemaphoreType.DMA((7,))],
        place=pltpu.HBM,
    )
    temp_near, temp_far = exchange(sent[None])
    weights, diagonal, inverse = call(
        weigh_kernel, [(6, *flat), flat, flat],
        visc_far, visc_near, half, side, base, matrix, scratch=[single],
    )
    adjoint_next, *first = call(
        step_kernel, [flat, single, single, single],
        temp_far, temp_near, right, part, speed, inverse, matrix, scratch=[single],
    )
    halos = [[far_row(y, 1), far_row(y, 2), far_row(y, 3), neighbour(y)] for y in first]
    deep = call(
        deep_weigh_kernel, [(6, *flat)] * 2,
        visc_second, visc_third, visc_far, half, back, ahead, first[0], scratch=[single, single],
    )
    streams = [[y] for y in first]
    many = (len(CENTERS), *single)

    def one(i, after):
        y1, first_row, second_row = call(
            deep_first_kernel, [single] * 3,
            *halos[i], first[i], weights, *deep, matrix, back, ahead, after, scratch=[single],
        )
        streams[i].append(y1)
        return first_row, second_row, neighbour(y1)

    def two(i, rows_near, after):
        y2, first_row = call(
            deep_second_kernel, [single] * 2,
            *rows_near, streams[i][1], weights, deep[0], matrix, back, after, scratch=[single],
        )
        streams[i].append(y2)
        return first_row, neighbour(y2)

    def early(i):
        return call(early_kernel, [(8, 128), many, many], diagonal, *streams[i])

    a = one(0, weights)
    b = one(1, streams[0][1])
    a = two(0, a, streams[1][1])
    early_a = early(0)
    c = one(2, early_a[0])
    b = two(1, b, streams[2][1])
    c = two(2, c, streams[1][2])
    early_b, early_c = early(1), early(2)
    moments = early_a[0] + early_b[0] + early_c[0]
    for i, (swapped, prepared) in enumerate(((a, early_a), (b, early_b), (c, early_c))):
        field, moments = call(
            last_kernel, [single, (devices, 1, 128) if i == 2 else (8, 128)],
            *swapped, streams[i][2], weights, matrix, moments, *prepared[1:], scratch=[single],
        )
        streams[i].append(field)
    moments = lax.all_to_all(moments, NAMES, 0, 0)
    answer, residual, adjoint_next = call(
        finish_kernel, [triple, triple, flat],
        moments, diagonal, adjoint_next, *[field for stream in streams for field in stream],
        scratch=[triple, triple, pltpu.SemaphoreType.DMA((2, 3)), pltpu.SemaphoreType.DMA], out_place=pltpu.HBM,
    )
    whole = (3, 1, 1, rows, layers)
    return answer.reshape(whole), residual.reshape(whole), adjoint_next.reshape(adjoint_temp.shape)


def solution(mesh):
    flat = P("diamond", "tile", None, None)
    triple = P(None, "diamond", "tile", None, None)
    return jax.shard_map(
        body,
        mesh=mesh,
        in_specs=(flat, flat, flat, triple, triple, P(), P()),
        out_specs=(triple, triple, flat),
        check_vma=False,
    )
```

```python
import functools

import jax
import jax.numpy as jnp
from jax import lax
from jax.experimental import pallas as pl
from jax.experimental.pallas import tpu as pltpu
from jax.sharding import PartitionSpec as P

ITERS = 3
TIME_STEP = 0.1
DIFFUSION = 1.0
MASS_TERM = 0.5
BUOYANCY = 1.0
CENTERS = (1.0, 0.55, 1.45, 0.25, 1.75, 0.05, 1.95)
CHUNK = 32
SPLITS = ((0, 1), (1, 2), (2, 3))


def rows_around(load, start, total):
    low, high = max(start - 8, 0), min(start + CHUNK + 8, total)
    block = load(low, high)
    at = start - low
    after = pltpu.roll(block, high - low - 1, 0)[at : at + CHUNK]
    before = pltpu.roll(block, 1, 0)[at : at + CHUNK]
    return block[at : at + CHUNK], after, before


def layers_around(block):
    count = block.shape[1]
    return pltpu.roll(block, count - 1, 1), pltpu.roll(block, 1, 1)


def split3(value):
    top = value.astype(jnp.bfloat16)
    rest = value - top.astype(jnp.float32)
    middle = rest.astype(jnp.bfloat16)
    bottom = (rest - middle.astype(jnp.float32)).astype(jnp.bfloat16)
    return [top, middle, bottom]


def fold_matrix(edge_ref, pole_ref):
    group, tile = lax.axis_index("diamond"), lax.axis_index("tile")
    final = lax.axis_size("tile") - 1
    count = edge_ref.shape[1]
    rows = lax.broadcasted_iota(jnp.int32, (count, count), 0)
    same = lax.broadcasted_iota(jnp.int32, (1, count), 1)
    edge = jnp.where(group == 0, edge_ref[1:2], edge_ref[0:1])
    pole = jnp.where(group == 0, pole_ref[1:2], pole_ref[0:1])
    line = jnp.where(tile == 0, pole, jnp.where(tile == final, edge, same))
    return (rows == line).astype(jnp.bfloat16)


def unfold(matrix_ref, far_ref, out_ref):
    layers = far_ref.shape[2]
    for at in range(far_ref.shape[0]):
        pieces = jnp.concatenate(split3(far_ref[at]), axis=1)
        moved = jnp.dot(matrix_ref[...], pieces, preferred_element_type=jnp.float32)
        out_ref[at] = (
            moved[:, :layers] + moved[:, layers : 2 * layers] + moved[:, 2 * layers :]
        )


def local_kernel(
    temp_hbm, misfit_hbm, visc_hbm, velocity_hbm, forcing_hbm, edge_hbm, pole_hbm,
    half_ref, side_ref, base_ref, right_ref, part_ref, speed_ref, matrix_ref, temp_ref,
    misfit_ref, visc_ref, velocity_ref, edge_ref, pole_ref, sems,
):
    sources = [visc_hbm, temp_hbm, edge_hbm, pole_hbm, velocity_hbm, misfit_hbm, forcing_hbm]
    targets = [visc_ref, temp_ref, edge_ref, pole_ref, velocity_ref, misfit_ref, right_ref]
    copies = [pltpu.make_async_copy(s, t, sems.at[i]) for i, (s, t) in enumerate(zip(sources, targets))]
    for copy in copies:
        copy.start()
    odd = lax.rem(lax.axis_index("tile"), 2)
    half = jnp.where(odd == 0, 0.5, -0.5).astype(jnp.float32)
    total, layers = temp_ref.shape
    for copy in copies:
        copy.wait()
    matrix_ref[...] = fold_matrix(edge_ref, pole_ref)
    for start in range(0, total, CHUNK):
        here = slice(start, start + CHUNK)
        visc, visc_after, visc_before = rows_around(lambda a, b: visc_ref[a:b], start, total)
        temp, temp_after, temp_before = rows_around(lambda a, b: temp_ref[a:b], start, total)
        place = start + lax.broadcasted_iota(jnp.int32, (CHUNK, layers), 0)
        layer = lax.broadcasted_iota(jnp.int32, (CHUNK, layers), 1)
        inside = [place < total - 1, place > 0, layer < layers - 1, layer > 0]
        visc_near = [visc_after, visc_before, *layers_around(visc)]
        temp_near = [temp_after, temp_before, *layers_around(temp)]
        zero = jnp.zeros_like(visc)
        weights = [jnp.where(m, 0.5 * (visc + v), zero) for m, v in zip(inside, visc_near)]
        temps = [jnp.where(m, t, zero) for m, t in zip(inside, temp_near)]
        half_ref[here] = 0.5 * visc
        for k in range(4):
            side_ref[k, here] = weights[k]
        base_ref[here] = MASS_TERM + sum(weights)
        transport = 0.5 * (
            velocity_ref[1, here] * (temps[0] - temps[1]) + velocity_ref[2, here] * (temps[2] - temps[3])
        )
        laplace = sum(temps) - 6.0 * temp
        part_ref[here] = temp + TIME_STEP * (DIFFUSION * laplace + transport) + misfit_ref[here]
        speed_ref[here] = half * velocity_ref[0, here]


def weigh_kernel(
    far_ref, near_ref, half_ref, side_ref, base_ref, right_ref, matrix_ref,
    weights_ref, diagonal_ref, inverse_ref, *refs,
):
    *first_refs, moved_ref = refs
    unfold(matrix_ref, far_ref, moved_ref)
    for start in range(0, half_ref.shape[0], CHUNK):
        here = slice(start, start + CHUNK)
        visc = half_ref[here]
        weights = [visc + 0.5 * near_ref[0, here], visc + 0.5 * moved_ref[0, here]]
        diagonal = base_ref[here] + weights[0] + weights[1]
        diagonal_ref[here] = diagonal
        inverse = 1.0 / diagonal
        inverse_ref[here] = inverse
        for (low, high), first_ref in zip(SPLITS, first_refs):
            for at in range(low, high):
                first_ref[at - low, here] = right_ref[at, here] * inverse
        weights += [side_ref[k, here] for k in range(4)]
        for k in range(6):
            weights_ref[k, here] = weights[k] * inverse


def step_kernel(
    far_ref, near_ref, right_ref, part_ref, speed_ref, inverse_ref, matrix_ref, next_ref, first_ref, moved_ref
):
    unfold(matrix_ref, far_ref, moved_ref)
    for start in range(0, part_ref.shape[0], CHUNK):
        here = slice(start, start + CHUNK)
        near, far = near_ref[0, here], moved_ref[0, here]
        adjoint_next = part_ref[here] + TIME_STEP * (
            DIFFUSION * (near + far) + speed_ref[here] * (near - far)
        )
        next_ref[here] = adjoint_next
        first_ref[0, here] = (right_ref[2, here] + BUOYANCY * adjoint_next) * inverse_ref[here]


def average(start, at, field_ref, near_ref, moved_ref, weights):
    here = slice(start, start + CHUNK)
    mid, after, before = rows_around(lambda a, b: field_ref[at, a:b], start, field_ref.shape[1])
    around = [near_ref[at, here], moved_ref[at, here], after, before, *layers_around(mid)]
    return mid - sum(w * v for w, v in zip(weights, around))


def apply_kernel(far_ref, near_ref, field_ref, weights_ref, matrix_ref, out_ref, moved_ref):
    unfold(matrix_ref, far_ref, moved_ref)
    for start in range(0, field_ref.shape[1], CHUNK):
        here = slice(start, start + CHUNK)
        weights = [weights_ref[k, here] for k in range(6)]
        for at in range(field_ref.shape[0]):
            out_ref[at, here] = average(start, at, field_ref, near_ref, moved_ref, weights)


def fold8(value):
    return jnp.sum(value.reshape(value.shape[0] // 8, 8, value.shape[1]), axis=0)


def moment_lanes(k):
    row = lax.broadcasted_iota(jnp.int32, (8, 128), 0)
    lane = lax.broadcasted_iota(jnp.int32, (8, 128), 1)
    return lane == row + 8 * k


def place_moment(k, sums):
    rows = [jnp.sum(s, axis=0, keepdims=True) for s in sums]
    rows += [rows[0]] * (8 - len(rows))
    column = jnp.sum(jnp.concatenate(rows, axis=0), axis=1, keepdims=True)
    return jnp.where(moment_lanes(k), column, 0.0)


def early_kernel(diagonal_ref, *refs):
    moments_ref, left_ref, shift_ref = refs[-3:]
    total, layers = diagonal_ref.shape
    sums = [[jnp.zeros((8, layers), jnp.float32) for _ in CENTERS] for _ in range(5)]
    for i, (low, high) in enumerate(SPLITS):
        y0_ref, y1_ref, y2_ref = refs[3 * i : 3 * i + 3]
        for start in range(0, total, CHUNK):
            here = slice(start, start + CHUNK)
            diagonal = diagonal_ref[here]
            for at in range(high - low):
                y0, y1, y2 = y0_ref[at, here], y1_ref[at, here], y2_ref[at, here]
                d0 = diagonal * y0
                m0 = fold8(d0 * y0)
                for j, center in enumerate(CENTERS):
                    q1 = y1 - center * y0
                    t2 = y2 - center * y1
                    q2 = t2 - center * q1
                    d1, d2 = diagonal * q1, diagonal * q2
                    left_ref[j, low + at, here] = d2
                    shift_ref[j, low + at, here] = center * (y2 + t2 + q2)
                    sums[0][j] += m0
                    sums[1][j] += fold8(d0 * q1)
                    sums[2][j] += fold8(d1 * q1)
                    sums[3][j] += fold8(d1 * q2)
                    sums[4][j] += fold8(d2 * q2)
    moments_ref[...] = sum(place_moment(k, sums[k]) for k in range(5))


def powers(center, y0, y1, y2, y3):
    q1 = y1 - center * y0
    t2 = y2 - center * y1
    q2 = t2 - center * q1
    q3 = (y3 - center * y2 - center * t2) - center * q2
    return q1, q2, q3


def last_kernel(
    low, far_ref, near_ref, field_ref, weights_ref, matrix_ref, earlier_ref, left_ref, shift_ref,
    out_ref, moments_ref, moved_ref,
):
    unfold(matrix_ref, far_ref, moved_ref)
    total, layers = field_ref.shape[1:]
    sums = [jnp.zeros((8, layers), jnp.float32) for _ in CENTERS]
    for start in range(0, total, CHUNK):
        here = slice(start, start + CHUNK)
        weights = [weights_ref[k, here] for k in range(6)]
        for at in range(field_ref.shape[0]):
            y3 = average(start, at, field_ref, near_ref, moved_ref, weights)
            out_ref[at, here] = y3
            for j in range(len(CENTERS)):
                sums[j] += fold8(left_ref[j, low + at, here] * (y3 - shift_ref[j, low + at, here]))
    message = earlier_ref[...] + place_moment(5, sums)
    if len(moments_ref.shape) == 2:
        moments_ref[...] = message
    else:
        row = jnp.sum(message, axis=0, keepdims=True)
        for device in range(moments_ref.shape[0]):
            moments_ref[device] = row


def inner(left, right, moments, shift=0):
    total = 0.0
    for i, a in enumerate(left):
        for j, b in enumerate(right):
            total = total + (a * b) * moments[i + j + shift]
    return total


def axpy(scale, left, right):
    count = max(len(left), len(right))
    result = []
    for i in range(count):
        if i >= len(left):
            result.append(right[i])
        elif i >= len(right):
            result.append(scale * left[i])
        else:
            result.append(scale * left[i] + right[i])
    return result


def recurrence(moments, centers):
    def operator(poly):
        result = [centers * a for a in poly] + [jnp.zeros_like(centers)]
        for i, a in enumerate(poly):
            result[i + 1] = result[i + 1] + a
        return result

    one = jnp.ones_like(centers)
    residual, direction, answer = [one], [one], []
    product_now = moments[0]
    for step in range(ITERS):
        image = operator(direction)
        step_size = product_now / inner(direction, image, moments)
        answer = axpy(step_size, direction, answer)
        residual = axpy(-step_size, image, residual)
        if step + 1 < ITERS:
            product_next = inner(residual, residual, moments)
            direction = axpy(product_next / product_now, direction, residual)
            product_now = product_next
    return answer, residual


def finish_kernel(moments_ref, diagonal_ref, *refs):
    *refs, solution_hbm, residual_hbm, solution_ref, residual_ref, sems = refs
    streams = [refs[4 * i : 4 * i + 4] for i in range(len(SPLITS))]
    rows = [moments_ref[device] for device in range(moments_ref.shape[0])]
    while len(rows) > 1:
        rows = [a + b for a, b in zip(rows[::2], rows[1::2])]
    row = jnp.broadcast_to(rows[0], (8, 128))
    moments = [jnp.sum(jnp.where(moment_lanes(k), row, 0.0), axis=1, keepdims=True) for k in range(6)]
    place = lax.broadcasted_iota(jnp.int32, (8, 1), 0)
    centers = jnp.zeros((8, 1), jnp.float32)
    for j, center in enumerate(CENTERS):
        centers = jnp.where(place == j, center, centers)
    answer, residual = recurrence(moments, centers)
    packed = [centers, *answer, *residual]
    mean = centers[0:1] + moments[1][0:1] / moments[0][0:1]
    best = jnp.abs(mean - centers[0:1])
    chosen = [p[0:1] for p in packed]
    for j in range(1, len(CENTERS)):
        away = jnp.abs(mean - centers[j : j + 1])
        better = away < best
        best = jnp.where(better, away, best)
        chosen = [jnp.where(better, p[j : j + 1], c) for p, c in zip(packed, chosen)]
    total, layers = diagonal_ref.shape
    chosen = [jnp.broadcast_to(c, (CHUNK, layers)) for c in chosen]
    center, answer, residual = chosen[0], chosen[1:4], chosen[4:8]
    copies = []
    for (low, high), stream in zip(SPLITS, streams):
        for at in range(high - low):
            for start in range(0, total, CHUNK):
                here = slice(start, start + CHUNK)
                values = [ref[at, here] for ref in stream]
                q1, q2, q3 = powers(center, *values)
                solution_ref[low + at, here] = answer[0] * values[0] + answer[1] * q1 + answer[2] * q2
                residual_ref[low + at, here] = diagonal_ref[here] * (
                    residual[0] * values[0] + residual[1] * q1 + residual[2] * q2 + residual[3] * q3
                )
            for k, (source, target) in enumerate(((solution_ref, solution_hbm), (residual_ref, residual_hbm))):
                copies.append(pltpu.make_async_copy(source.at[low + at], target.at[low + at], sems.at[k, low + at]))
                copies[-1].start()
    for copy in copies:
        copy.wait()


def call(kernel, out_shapes, *args, scratch=(), place=pltpu.VMEM, out_place=pltpu.VMEM):
    if place is pltpu.HBM:
        args = [pltpu.with_memory_space_constraint(a, place) for a in args]
    outs = [o if isinstance(o, jax.ShapeDtypeStruct) else jax.ShapeDtypeStruct(o, jnp.float32) for o in out_shapes]
    return pl.pallas_call(
        kernel,
        out_shape=outs,
        in_specs=[pl.BlockSpec(memory_space=place)] * len(args),
        out_specs=[pl.BlockSpec(memory_space=out_place)] * len(out_shapes),
        scratch_shapes=[pltpu.VMEM(s, jnp.float32) if isinstance(s, tuple) else s for s in scratch],
        compiler_params=pltpu.CompilerParams(vmem_limit_bytes=24 * 2**20),
    )(*args)


def ring_pairs(groups, tiles):
    beside = [(g * tiles + i, g * tiles + (i ^ 1)) for g in range(groups) for i in range(tiles)]
    across = []
    for g in range(groups):
        for i in range(tiles):
            j = i - 1 if i % 2 == 0 else i + 1
            if j < 0 or j >= tiles:
                across.append((g * tiles + i, (1 - g) * tiles + i))
            else:
                across.append((g * tiles + i, g * tiles + j))
    return beside, across


NAMES = ("diamond", "tile")


def exchange(value):
    beside, across = ring_pairs(lax.axis_size("diamond"), lax.axis_size("tile"))
    far = lax.ppermute(value, NAMES, across)
    near = lax.ppermute(value, NAMES, beside)
    return near, far


def body(adjoint_temp, misfit, viscosity, velocity, forcing, edge_table, pole_table):
    rows, layers = adjoint_temp.shape[2:]
    devices = lax.axis_size("diamond") * lax.axis_size("tile")
    flat, triple = (rows, layers), (3, rows, layers)
    temp, source, visc = (v.reshape(flat) for v in (adjoint_temp, misfit, viscosity))
    visc_near, visc_far = exchange(visc[None])
    table = pltpu.VMEM(edge_table.shape, edge_table.dtype)
    half, side, base, right, part, speed, matrix, sent = call(
        local_kernel,
        [flat, (4, *flat), flat, triple, flat, flat, jax.ShapeDtypeStruct((rows, rows), jnp.bfloat16), flat],
        temp, source, visc, velocity.reshape(triple), forcing.reshape(triple), edge_table, pole_table,
        scratch=[flat, flat, triple, table, table, pltpu.SemaphoreType.DMA((7,))],
        place=pltpu.HBM,
    )
    temp_near, temp_far = exchange(sent[None])
    shapes = [(high - low, rows, layers) for low, high in SPLITS]
    weights, diagonal, inverse, *first = call(
        weigh_kernel, [(6, *flat), flat, flat, *shapes[:-1]],
        visc_far, visc_near, half, side, base, right, matrix, scratch=[(1, *flat)],
    )
    adjoint_next, *rest = call(
        step_kernel, [flat, shapes[-1]],
        temp_far, temp_near, right, part, speed, inverse, matrix, scratch=[(1, *flat)],
    )
    first += rest
    streams = [[field] for field in first]
    swapped = [exchange(field) for field in first]
    for step in range(ITERS - 1):
        for i, shape in enumerate(shapes):
            near, far = swapped[i]
            (field,) = call(apply_kernel, [shape], far, near, streams[i][-1], weights, matrix, scratch=[shape])
            swapped[i] = exchange(field)
            streams[i].append(field)
    many = (len(CENTERS), *triple)
    moments, left, shift = call(
        early_kernel, [(8, 128), many, many], diagonal, *[field for stream in streams for field in stream]
    )
    for i, shape in enumerate(shapes):
        near, far = swapped[i]
        sums = (8, 128) if i + 1 < len(shapes) else (devices, 1, 128)
        field, moments = call(
            functools.partial(last_kernel, SPLITS[i][0]), [shape, sums],
            far, near, streams[i][-1], weights, matrix, moments, left, shift, scratch=[shape],
        )
        streams[i].append(field)
    moments = lax.all_to_all(moments, NAMES, 0, 0)
    fields = [field for stream in streams for field in stream]
    answer, residual = call(
        finish_kernel, [triple, triple], moments, diagonal, *fields,
        scratch=[triple, triple, pltpu.SemaphoreType.DMA((2, 3))], out_place=pltpu.HBM,
    )
    whole = (3, 1, 1, rows, layers)
    return answer.reshape(whole), residual.reshape(whole), adjoint_next.reshape(adjoint_temp.shape)


def solution(mesh):
    flat = P("diamond", "tile", None, None)
    triple = P(None, "diamond", "tile", None, None)
    return jax.shard_map(
        body,
        mesh=mesh,
        in_specs=(flat, flat, flat, triple, triple, P(), P()),
        out_specs=(triple, triple, flat),
        check_vma=False,
    )
```

```python
import functools

import jax
import jax.numpy as jnp
from jax import lax
from jax.experimental import pallas as pl
from jax.experimental.pallas import tpu as pltpu
from jax.sharding import PartitionSpec as P

ITERS = 3
TIME_STEP = 0.1
DIFFUSION = 1.0
MASS_TERM = 0.5
BUOYANCY = 1.0
CENTERS = (0.8, 0.4, 1.3, 0.05, 1.8)
CHUNK = 32
SPLITS = ((0, 1), (1, 2), (2, 3))


def rows_around(load, start, total):
    low, high = max(start - 8, 0), min(start + CHUNK + 8, total)
    block = load(low, high)
    at = start - low
    after = pltpu.roll(block, high - low - 1, 0)[at : at + CHUNK]
    before = pltpu.roll(block, 1, 0)[at : at + CHUNK]
    return block[at : at + CHUNK], after, before


def layers_around(block):
    count = block.shape[1]
    return pltpu.roll(block, count - 1, 1), pltpu.roll(block, 1, 1)


def split3(value):
    top = value.astype(jnp.bfloat16)
    rest = value - top.astype(jnp.float32)
    middle = rest.astype(jnp.bfloat16)
    bottom = (rest - middle.astype(jnp.float32)).astype(jnp.bfloat16)
    return [top, middle, bottom]


def fold_matrix(edge_ref, pole_ref):
    group, tile = lax.axis_index("diamond"), lax.axis_index("tile")
    final = lax.axis_size("tile") - 1
    count = edge_ref.shape[1]
    rows = lax.broadcasted_iota(jnp.int32, (count, count), 0)
    same = lax.broadcasted_iota(jnp.int32, (1, count), 1)
    edge = jnp.where(group == 0, edge_ref[1:2], edge_ref[0:1])
    pole = jnp.where(group == 0, pole_ref[1:2], pole_ref[0:1])
    line = jnp.where(tile == 0, pole, jnp.where(tile == final, edge, same))
    return (rows == line).astype(jnp.bfloat16)


def unfold(matrix_ref, far_ref, out_ref):
    layers = far_ref.shape[2]
    for at in range(far_ref.shape[0]):
        pieces = jnp.concatenate(split3(far_ref[at]), axis=1)
        moved = jnp.dot(matrix_ref[...], pieces, preferred_element_type=jnp.float32)
        out_ref[at] = (
            moved[:, :layers] + moved[:, layers : 2 * layers] + moved[:, 2 * layers :]
        )


def local_kernel(
    temp_hbm, misfit_hbm, visc_hbm, velocity_hbm, forcing_hbm, edge_hbm, pole_hbm,
    half_ref, side_ref, base_ref, right_ref, part_ref, speed_ref, matrix_ref, temp_ref,
    misfit_ref, visc_ref, velocity_ref, edge_ref, pole_ref, sems,
):
    sources = [visc_hbm, temp_hbm, edge_hbm, pole_hbm, velocity_hbm, misfit_hbm, forcing_hbm]
    targets = [visc_ref, temp_ref, edge_ref, pole_ref, velocity_ref, misfit_ref, right_ref]
    copies = [pltpu.make_async_copy(s, t, sems.at[i]) for i, (s, t) in enumerate(zip(sources, targets))]
    for copy in copies:
        copy.start()
    odd = lax.rem(lax.axis_index("tile"), 2)
    half = jnp.where(odd == 0, 0.5, -0.5).astype(jnp.float32)
    total, layers = temp_ref.shape
    for copy in copies:
        copy.wait()
    matrix_ref[...] = fold_matrix(edge_ref, pole_ref)
    for start in range(0, total, CHUNK):
        here = slice(start, start + CHUNK)
        visc, visc_after, visc_before = rows_around(lambda a, b: visc_ref[a:b], start, total)
        temp, temp_after, temp_before = rows_around(lambda a, b: temp_ref[a:b], start, total)
        place = start + lax.broadcasted_iota(jnp.int32, (CHUNK, layers), 0)
        layer = lax.broadcasted_iota(jnp.int32, (CHUNK, layers), 1)
        inside = [place < total - 1, place > 0, layer < layers - 1, layer > 0]
        visc_near = [visc_after, visc_before, *layers_around(visc)]
        temp_near = [temp_after, temp_before, *layers_around(temp)]
        zero = jnp.zeros_like(visc)
        weights = [jnp.where(m, 0.5 * (visc + v), zero) for m, v in zip(inside, visc_near)]
        temps = [jnp.where(m, t, zero) for m, t in zip(inside, temp_near)]
        half_ref[here] = 0.5 * visc
        for k in range(4):
            side_ref[k, here] = weights[k]
        base_ref[here] = MASS_TERM + sum(weights)
        transport = 0.5 * (
            velocity_ref[1, here] * (temps[0] - temps[1]) + velocity_ref[2, here] * (temps[2] - temps[3])
        )
        laplace = sum(temps) - 6.0 * temp
        part_ref[here] = temp + TIME_STEP * (DIFFUSION * laplace + transport) + misfit_ref[here]
        speed_ref[here] = half * velocity_ref[0, here]


def weigh_kernel(
    far_ref, near_ref, half_ref, side_ref, base_ref, right_ref, matrix_ref,
    weights_ref, diagonal_ref, inverse_ref, *refs,
):
    *first_refs, moved_ref = refs
    unfold(matrix_ref, far_ref, moved_ref)
    for start in range(0, half_ref.shape[0], CHUNK):
        here = slice(start, start + CHUNK)
        visc = half_ref[here]
        weights = [visc + 0.5 * near_ref[0, here], visc + 0.5 * moved_ref[0, here]]
        diagonal = base_ref[here] + weights[0] + weights[1]
        diagonal_ref[here] = diagonal
        inverse = 1.0 / diagonal
        inverse_ref[here] = inverse
        for (low, high), first_ref in zip(SPLITS, first_refs):
            for at in range(low, high):
                first_ref[at - low, here] = right_ref[at, here] * inverse
        weights += [side_ref[k, here] for k in range(4)]
        for k in range(6):
            weights_ref[k, here] = weights[k] * inverse


def step_kernel(
    far_ref, near_ref, right_ref, part_ref, speed_ref, inverse_ref, matrix_ref, next_ref, first_ref, moved_ref
):
    unfold(matrix_ref, far_ref, moved_ref)
    for start in range(0, part_ref.shape[0], CHUNK):
        here = slice(start, start + CHUNK)
        near, far = near_ref[0, here], moved_ref[0, here]
        adjoint_next = part_ref[here] + TIME_STEP * (
            DIFFUSION * (near + far) + speed_ref[here] * (near - far)
        )
        next_ref[here] = adjoint_next
        first_ref[0, here] = (right_ref[2, here] + BUOYANCY * adjoint_next) * inverse_ref[here]


def average(start, at, field_ref, near_ref, moved_ref, weights):
    here = slice(start, start + CHUNK)
    mid, after, before = rows_around(lambda a, b: field_ref[at, a:b], start, field_ref.shape[1])
    around = [near_ref[at, here], moved_ref[at, here], after, before, *layers_around(mid)]
    return mid - sum(w * v for w, v in zip(weights, around))


def apply_kernel(far_ref, near_ref, field_ref, weights_ref, matrix_ref, out_ref, moved_ref):
    unfold(matrix_ref, far_ref, moved_ref)
    for start in range(0, field_ref.shape[1], CHUNK):
        here = slice(start, start + CHUNK)
        weights = [weights_ref[k, here] for k in range(6)]
        for at in range(field_ref.shape[0]):
            out_ref[at, here] = average(start, at, field_ref, near_ref, moved_ref, weights)


def fold8(value):
    return jnp.sum(value.reshape(value.shape[0] // 8, 8, value.shape[1]), axis=0)


def moment_lanes(k):
    row = lax.broadcasted_iota(jnp.int32, (8, 128), 0)
    lane = lax.broadcasted_iota(jnp.int32, (8, 128), 1)
    return lane == row + 8 * k


def place_moment(k, sums):
    rows = [jnp.sum(s, axis=0, keepdims=True) for s in sums]
    rows += [rows[0]] * (8 - len(rows))
    column = jnp.sum(jnp.concatenate(rows, axis=0), axis=1, keepdims=True)
    return jnp.where(moment_lanes(k), column, 0.0)


def early_kernel(diagonal_ref, *refs):
    moments_ref, left_ref, shift_ref = refs[-3:]
    total, layers = diagonal_ref.shape
    sums = [[jnp.zeros((8, layers), jnp.float32) for _ in CENTERS] for _ in range(5)]
    for i, (low, high) in enumerate(SPLITS):
        y0_ref, y1_ref, y2_ref = refs[3 * i : 3 * i + 3]
        for start in range(0, total, CHUNK):
            here = slice(start, start + CHUNK)
            diagonal = diagonal_ref[here]
            for at in range(high - low):
                y0, y1, y2 = y0_ref[at, here], y1_ref[at, here], y2_ref[at, here]
                d0 = diagonal * y0
                m0 = fold8(d0 * y0)
                for j, center in enumerate(CENTERS):
                    q1 = y1 - center * y0
                    t2 = y2 - center * y1
                    q2 = t2 - center * q1
                    d1, d2 = diagonal * q1, diagonal * q2
                    left_ref[j, low + at, here] = d2
                    shift_ref[j, low + at, here] = center * (y2 + t2 + q2)
                    sums[0][j] += m0
                    sums[1][j] += fold8(d0 * q1)
                    sums[2][j] += fold8(d1 * q1)
                    sums[3][j] += fold8(d1 * q2)
                    sums[4][j] += fold8(d2 * q2)
    moments_ref[...] = sum(place_moment(k, sums[k]) for k in range(5))


def last_kernel(
    low, far_ref, near_ref, field_ref, weights_ref, matrix_ref, earlier_ref, left_ref, shift_ref,
    out_ref, moments_ref, moved_ref,
):
    unfold(matrix_ref, far_ref, moved_ref)
    total, layers = field_ref.shape[1:]
    sums = [jnp.zeros((8, layers), jnp.float32) for _ in CENTERS]
    for start in range(0, total, CHUNK):
        here = slice(start, start + CHUNK)
        weights = [weights_ref[k, here] for k in range(6)]
        for at in range(field_ref.shape[0]):
            y3 = average(start, at, field_ref, near_ref, moved_ref, weights)
            out_ref[at, here] = y3
            for j in range(len(CENTERS)):
                sums[j] += fold8(left_ref[j, low + at, here] * (y3 - shift_ref[j, low + at, here]))
    message = earlier_ref[...] + place_moment(5, sums)
    if len(moments_ref.shape) == 2:
        moments_ref[...] = message
    else:
        row = jnp.sum(message, axis=0, keepdims=True)
        for device in range(moments_ref.shape[0]):
            moments_ref[device] = row


def inner(left, right, moments, shift=0):
    total = 0.0
    for i, a in enumerate(left):
        for j, b in enumerate(right):
            total = total + (a * b) * moments[i + j + shift]
    return total


def axpy(scale, left, right):
    count = max(len(left), len(right))
    result = []
    for i in range(count):
        if i >= len(left):
            result.append(right[i])
        elif i >= len(right):
            result.append(scale * left[i])
        else:
            result.append(scale * left[i] + right[i])
    return result


def recurrence(moments, centers):
    def operator(poly):
        result = [centers * a for a in poly] + [jnp.zeros_like(centers)]
        for i, a in enumerate(poly):
            result[i + 1] = result[i + 1] + a
        return result

    one = jnp.ones_like(centers)
    residual, direction, answer = [one], [one], []
    product_now = moments[0]
    for step in range(ITERS):
        image = operator(direction)
        step_size = product_now / inner(direction, image, moments)
        answer = axpy(step_size, direction, answer)
        if step + 1 < ITERS:
            residual = axpy(-step_size, image, residual)
            product_next = inner(residual, residual, moments)
            direction = axpy(product_next / product_now, direction, residual)
            product_now = product_next
    return answer


def finish_kernel(moments_ref, diagonal_ref, *refs):
    *refs, solution_hbm, residual_hbm, solution_ref, residual_ref, sems = refs
    streams = [refs[4 * i : 4 * i + 4] for i in range(len(SPLITS))]
    rows = [moments_ref[device] for device in range(moments_ref.shape[0])]
    while len(rows) > 1:
        rows = [a + b for a, b in zip(rows[::2], rows[1::2])]
    row = jnp.broadcast_to(rows[0], (8, 128))
    moments = [jnp.sum(jnp.where(moment_lanes(k), row, 0.0), axis=1, keepdims=True) for k in range(6)]
    place = lax.broadcasted_iota(jnp.int32, (8, 1), 0)
    centers = jnp.zeros((8, 1), jnp.float32)
    for j, center in enumerate(CENTERS):
        centers = jnp.where(place == j, center, centers)
    a0, a1, a2 = recurrence(moments, centers)
    packed = [a0 - centers * (a1 - centers * a2), a1 - (2.0 * centers) * a2, a2]
    mean = centers[0:1] + moments[1][0:1] / moments[0][0:1]
    best = jnp.abs(mean - centers[0:1])
    chosen = [p[0:1] for p in packed]
    for j in range(1, len(CENTERS)):
        away = jnp.abs(mean - centers[j : j + 1])
        better = away < best
        best = jnp.where(better, away, best)
        chosen = [jnp.where(better, p[j : j + 1], c) for p, c in zip(packed, chosen)]
    total, layers = diagonal_ref.shape
    a0, a1, a2 = [jnp.broadcast_to(c, (CHUNK, layers)) for c in chosen]
    copies = []
    for (low, high), stream in zip(SPLITS, streams):
        for at in range(high - low):
            for start in range(0, total, CHUNK):
                here = slice(start, start + CHUNK)
                y0, y1, y2, y3 = [ref[at, here] for ref in stream]
                solution_ref[low + at, here] = a0 * y0 + a1 * y1 + a2 * y2
                residual_ref[low + at, here] = diagonal_ref[here] * (y0 - (a0 * y1 + a1 * y2 + a2 * y3))
            for k, (source, target) in enumerate(((solution_ref, solution_hbm), (residual_ref, residual_hbm))):
                copies.append(pltpu.make_async_copy(source.at[low + at], target.at[low + at], sems.at[k, low + at]))
                copies[-1].start()
    for copy in copies:
        copy.wait()


def call(kernel, out_shapes, *args, scratch=(), place=pltpu.VMEM, out_place=pltpu.VMEM):
    if place is pltpu.HBM:
        args = [pltpu.with_memory_space_constraint(a, place) for a in args]
    outs = [o if isinstance(o, jax.ShapeDtypeStruct) else jax.ShapeDtypeStruct(o, jnp.float32) for o in out_shapes]
    return pl.pallas_call(
        kernel,
        out_shape=outs,
        in_specs=[pl.BlockSpec(memory_space=place)] * len(args),
        out_specs=[pl.BlockSpec(memory_space=out_place)] * len(out_shapes),
        scratch_shapes=[pltpu.VMEM(s, jnp.float32) if isinstance(s, tuple) else s for s in scratch],
        compiler_params=pltpu.CompilerParams(vmem_limit_bytes=24 * 2**20),
    )(*args)


def ring_pairs(groups, tiles):
    beside = [(g * tiles + i, g * tiles + (i ^ 1)) for g in range(groups) for i in range(tiles)]
    across = []
    for g in range(groups):
        for i in range(tiles):
            j = i - 1 if i % 2 == 0 else i + 1
            if j < 0 or j >= tiles:
                across.append((g * tiles + i, (1 - g) * tiles + i))
            else:
                across.append((g * tiles + i, g * tiles + j))
    return beside, across


NAMES = ("diamond", "tile")


def exchange(value):
    beside, across = ring_pairs(lax.axis_size("diamond"), lax.axis_size("tile"))
    far = lax.ppermute(value, NAMES, across)
    near = lax.ppermute(value, NAMES, beside)
    return near, far


def body(adjoint_temp, misfit, viscosity, velocity, forcing, edge_table, pole_table):
    rows, layers = adjoint_temp.shape[2:]
    devices = lax.axis_size("diamond") * lax.axis_size("tile")
    flat, triple = (rows, layers), (3, rows, layers)
    temp, source, visc = (v.reshape(flat) for v in (adjoint_temp, misfit, viscosity))
    visc_near, visc_far = exchange(visc[None])
    table = pltpu.VMEM(edge_table.shape, edge_table.dtype)
    half, side, base, right, part, speed, matrix, sent = call(
        local_kernel,
        [flat, (4, *flat), flat, triple, flat, flat, jax.ShapeDtypeStruct((rows, rows), jnp.bfloat16), flat],
        temp, source, visc, velocity.reshape(triple), forcing.reshape(triple), edge_table, pole_table,
        scratch=[flat, flat, triple, table, table, pltpu.SemaphoreType.DMA((7,))],
        place=pltpu.HBM,
    )
    temp_near, temp_far = exchange(sent[None])
    shapes = [(high - low, rows, layers) for low, high in SPLITS]
    weights, diagonal, inverse, *first = call(
        weigh_kernel, [(6, *flat), flat, flat, *shapes[:-1]],
        visc_far, visc_near, half, side, base, right, matrix, scratch=[(1, *flat)],
    )
    adjoint_next, *rest = call(
        step_kernel, [flat, shapes[-1]],
        temp_far, temp_near, right, part, speed, inverse, matrix, scratch=[(1, *flat)],
    )
    first += rest
    streams = [[field] for field in first]
    swapped = [exchange(field) for field in first]
    for step in range(ITERS - 1):
        for i, shape in enumerate(shapes):
            near, far = swapped[i]
            (field,) = call(apply_kernel, [shape], far, near, streams[i][-1], weights, matrix, scratch=[shape])
            swapped[i] = exchange(field)
            streams[i].append(field)
    many = (len(CENTERS), *triple)
    moments, left, shift = call(
        early_kernel, [(8, 128), many, many], diagonal, *[field for stream in streams for field in stream]
    )
    for i, shape in enumerate(shapes):
        near, far = swapped[i]
        sums = (8, 128) if i + 1 < len(shapes) else (devices, 1, 128)
        field, moments = call(
            functools.partial(last_kernel, SPLITS[i][0]), [shape, sums],
            far, near, streams[i][-1], weights, matrix, moments, left, shift, scratch=[shape],
        )
        streams[i].append(field)
    moments = lax.all_to_all(moments, NAMES, 0, 0)
    fields = [field for stream in streams for field in stream]
    answer, residual = call(
        finish_kernel, [triple, triple], moments, diagonal, *fields,
        scratch=[triple, triple, pltpu.SemaphoreType.DMA((2, 3))], out_place=pltpu.HBM,
    )
    whole = (3, 1, 1, rows, layers)
    return answer.reshape(whole), residual.reshape(whole), adjoint_next.reshape(adjoint_temp.shape)


def solution(mesh):
    flat = P("diamond", "tile", None, None)
    triple = P(None, "diamond", "tile", None, None)
    return jax.shard_map(
        body,
        mesh=mesh,
        in_specs=(flat, flat, flat, triple, triple, P(), P()),
        out_specs=(triple, triple, flat),
        check_vma=False,
    )
```

```python
import functools

import jax
import jax.numpy as jnp
from jax import lax
from jax.experimental import pallas as pl
from jax.experimental.pallas import tpu as pltpu
from jax.sharding import PartitionSpec as P

ITERS = 3
TIME_STEP = 0.1
DIFFUSION = 1.0
MASS_TERM = 0.5
BUOYANCY = 1.0
CENTERS = (0.8, 0.4, 1.3, 0.05, 1.8)
CHUNK = 32
SPLITS = ((0, 1), (1, 2), (2, 3))


def rows_around(load, start, total):
    low, high = max(start - 8, 0), min(start + CHUNK + 8, total)
    block = load(low, high)
    at = start - low
    after = pltpu.roll(block, high - low - 1, 0)[at : at + CHUNK]
    before = pltpu.roll(block, 1, 0)[at : at + CHUNK]
    return block[at : at + CHUNK], after, before


def layers_around(block):
    count = block.shape[1]
    return pltpu.roll(block, count - 1, 1), pltpu.roll(block, 1, 1)


def split3(value):
    top = value.astype(jnp.bfloat16)
    rest = value - top.astype(jnp.float32)
    middle = rest.astype(jnp.bfloat16)
    bottom = (rest - middle.astype(jnp.float32)).astype(jnp.bfloat16)
    return [top, middle, bottom]


def fold_matrix(edge_ref, pole_ref):
    group, tile = lax.axis_index("diamond"), lax.axis_index("tile")
    final = lax.axis_size("tile") - 1
    count = edge_ref.shape[1]
    rows = lax.broadcasted_iota(jnp.int32, (count, count), 0)
    same = lax.broadcasted_iota(jnp.int32, (1, count), 1)
    edge = jnp.where(group == 0, edge_ref[1:2], edge_ref[0:1])
    pole = jnp.where(group == 0, pole_ref[1:2], pole_ref[0:1])
    line = jnp.where(tile == 0, pole, jnp.where(tile == final, edge, same))
    return (rows == line).astype(jnp.bfloat16)


def unfold(matrix_ref, far_ref, out_ref):
    layers = far_ref.shape[2]
    for at in range(far_ref.shape[0]):
        pieces = jnp.concatenate(split3(far_ref[at]), axis=1)
        moved = jnp.dot(matrix_ref[...], pieces, preferred_element_type=jnp.float32)
        out_ref[at] = (
            moved[:, :layers] + moved[:, layers : 2 * layers] + moved[:, 2 * layers :]
        )


def local_kernel(
    temp_hbm, misfit_hbm, visc_hbm, velocity_hbm, forcing_hbm, edge_hbm, pole_hbm,
    half_ref, side_ref, base_ref, right_ref, part_ref, speed_ref, matrix_ref, temp_ref,
    misfit_ref, visc_ref, velocity_ref, edge_ref, pole_ref, sems,
):
    sources = [visc_hbm, temp_hbm, edge_hbm, pole_hbm, velocity_hbm, misfit_hbm, forcing_hbm]
    targets = [visc_ref, temp_ref, edge_ref, pole_ref, velocity_ref, misfit_ref, right_ref]
    copies = [pltpu.make_async_copy(s, t, sems.at[i]) for i, (s, t) in enumerate(zip(sources, targets))]
    for copy in copies:
        copy.start()
    odd = lax.rem(lax.axis_index("tile"), 2)
    half = jnp.where(odd == 0, 0.5, -0.5).astype(jnp.float32)
    total, layers = temp_ref.shape
    for copy in copies:
        copy.wait()
    matrix_ref[...] = fold_matrix(edge_ref, pole_ref)
    for start in range(0, total, CHUNK):
        here = slice(start, start + CHUNK)
        visc, visc_after, visc_before = rows_around(lambda a, b: visc_ref[a:b], start, total)
        temp, temp_after, temp_before = rows_around(lambda a, b: temp_ref[a:b], start, total)
        place = start + lax.broadcasted_iota(jnp.int32, (CHUNK, layers), 0)
        layer = lax.broadcasted_iota(jnp.int32, (CHUNK, layers), 1)
        inside = [place < total - 1, place > 0, layer < layers - 1, layer > 0]
        visc_near = [visc_after, visc_before, *layers_around(visc)]
        temp_near = [temp_after, temp_before, *layers_around(temp)]
        zero = jnp.zeros_like(visc)
        weights = [jnp.where(m, 0.5 * (visc + v), zero) for m, v in zip(inside, visc_near)]
        temps = [jnp.where(m, t, zero) for m, t in zip(inside, temp_near)]
        half_ref[here] = 0.5 * visc
        for k in range(4):
            side_ref[k, here] = weights[k]
        base_ref[here] = MASS_TERM + sum(weights)
        transport = 0.5 * (
            velocity_ref[1, here] * (temps[0] - temps[1]) + velocity_ref[2, here] * (temps[2] - temps[3])
        )
        laplace = sum(temps) - 6.0 * temp
        part_ref[here] = temp + TIME_STEP * (DIFFUSION * laplace + transport) + misfit_ref[here]
        speed_ref[here] = half * velocity_ref[0, here]


def weigh_kernel(
    far_ref, near_ref, half_ref, side_ref, base_ref, right_ref, matrix_ref,
    weights_ref, diagonal_ref, inverse_ref, *refs,
):
    *first_refs, moved_ref = refs
    unfold(matrix_ref, far_ref, moved_ref)
    for start in range(0, half_ref.shape[0], CHUNK):
        here = slice(start, start + CHUNK)
        visc = half_ref[here]
        weights = [visc + 0.5 * near_ref[0, here], visc + 0.5 * moved_ref[0, here]]
        diagonal = base_ref[here] + weights[0] + weights[1]
        diagonal_ref[here] = diagonal
        inverse = 1.0 / diagonal
        inverse_ref[here] = inverse
        for (low, high), first_ref in zip(SPLITS, first_refs):
            for at in range(low, high):
                first_ref[at - low, here] = right_ref[at, here] * inverse
        weights += [side_ref[k, here] for k in range(4)]
        for k in range(6):
            weights_ref[k, here] = weights[k] * inverse


def step_kernel(
    near_ref, far_ref, right_ref, part_ref, speed_ref, inverse_ref, matrix_ref, next_ref, first_ref, moved_ref
):
    unfold(matrix_ref, far_ref, moved_ref)
    for start in range(0, part_ref.shape[0], CHUNK):
        here = slice(start, start + CHUNK)
        near, far = near_ref[0, here], moved_ref[0, here]
        adjoint_next = part_ref[here] + TIME_STEP * (
            DIFFUSION * (near + far) + speed_ref[here] * (near - far)
        )
        next_ref[here] = adjoint_next
        first_ref[0, here] = (right_ref[2, here] + BUOYANCY * adjoint_next) * inverse_ref[here]


def average(start, at, field_ref, near_ref, moved_ref, weights):
    here = slice(start, start + CHUNK)
    mid, after, before = rows_around(lambda a, b: field_ref[at, a:b], start, field_ref.shape[1])
    around = [near_ref[at, here], moved_ref[at, here], after, before, *layers_around(mid)]
    return mid - sum(w * v for w, v in zip(weights, around))


def apply_kernel(far_ref, near_ref, field_ref, weights_ref, matrix_ref, out_ref, moved_ref):
    unfold(matrix_ref, far_ref, moved_ref)
    for start in range(0, field_ref.shape[1], CHUNK):
        here = slice(start, start + CHUNK)
        weights = [weights_ref[k, here] for k in range(6)]
        for at in range(field_ref.shape[0]):
            out_ref[at, here] = average(start, at, field_ref, near_ref, moved_ref, weights)


def fold8(value):
    return jnp.sum(value.reshape(value.shape[0] // 8, 8, value.shape[1]), axis=0)


def moment_lanes(k):
    row = lax.broadcasted_iota(jnp.int32, (8, 128), 0)
    lane = lax.broadcasted_iota(jnp.int32, (8, 128), 1)
    return lane == row + 8 * k


def place_moment(k, sums):
    rows = [jnp.sum(s, axis=0, keepdims=True) for s in sums]
    rows += [rows[0]] * (8 - len(rows))
    column = jnp.sum(jnp.concatenate(rows, axis=0), axis=1, keepdims=True)
    return jnp.where(moment_lanes(k), column, 0.0)


def early_kernel(diagonal_ref, *refs):
    moments_ref, left_ref, shift_ref = refs[-3:]
    total, layers = diagonal_ref.shape
    sums = [[jnp.zeros((8, layers), jnp.float32) for _ in CENTERS] for _ in range(5)]
    for i, (low, high) in enumerate(SPLITS):
        y0_ref, y1_ref, y2_ref = refs[3 * i : 3 * i + 3]
        for start in range(0, total, CHUNK):
            here = slice(start, start + CHUNK)
            diagonal = diagonal_ref[here]
            for at in range(high - low):
                y0, y1, y2 = y0_ref[at, here], y1_ref[at, here], y2_ref[at, here]
                d0 = diagonal * y0
                m0 = fold8(d0 * y0)
                for j, center in enumerate(CENTERS):
                    q1 = y1 - center * y0
                    t2 = y2 - center * y1
                    q2 = t2 - center * q1
                    d1, d2 = diagonal * q1, diagonal * q2
                    left_ref[j, low + at, here] = d2
                    shift_ref[j, low + at, here] = center * (y2 + t2 + q2)
                    sums[0][j] += m0
                    sums[1][j] += fold8(d0 * q1)
                    sums[2][j] += fold8(d1 * q1)
                    sums[3][j] += fold8(d1 * q2)
                    sums[4][j] += fold8(d2 * q2)
    moments_ref[...] = sum(place_moment(k, sums[k]) for k in range(5))


def last_kernel(
    low, far_ref, near_ref, field_ref, weights_ref, matrix_ref, earlier_ref, left_ref, shift_ref,
    out_ref, moments_ref, moved_ref,
):
    unfold(matrix_ref, far_ref, moved_ref)
    total, layers = field_ref.shape[1:]
    sums = [jnp.zeros((8, layers), jnp.float32) for _ in CENTERS]
    for start in range(0, total, CHUNK):
        here = slice(start, start + CHUNK)
        weights = [weights_ref[k, here] for k in range(6)]
        for at in range(field_ref.shape[0]):
            y3 = average(start, at, field_ref, near_ref, moved_ref, weights)
            out_ref[at, here] = y3
            for j in range(len(CENTERS)):
                sums[j] += fold8(left_ref[j, low + at, here] * (y3 - shift_ref[j, low + at, here]))
    message = earlier_ref[...] + place_moment(5, sums)
    if len(moments_ref.shape) == 2:
        moments_ref[...] = message
    else:
        row = jnp.sum(message, axis=0, keepdims=True)
        for device in range(moments_ref.shape[0]):
            moments_ref[device] = row


def inner(left, right, moments, shift=0):
    total = 0.0
    for i, a in enumerate(left):
        for j, b in enumerate(right):
            total = total + (a * b) * moments[i + j + shift]
    return total


def axpy(scale, left, right):
    count = max(len(left), len(right))
    result = []
    for i in range(count):
        if i >= len(left):
            result.append(right[i])
        elif i >= len(right):
            result.append(scale * left[i])
        else:
            result.append(scale * left[i] + right[i])
    return result


def recurrence(moments, centers):
    def operator(poly):
        result = [centers * a for a in poly] + [jnp.zeros_like(centers)]
        for i, a in enumerate(poly):
            result[i + 1] = result[i + 1] + a
        return result

    one = jnp.ones_like(centers)
    residual, direction, answer = [one], [one], []
    product_now = moments[0]
    for step in range(ITERS):
        image = operator(direction)
        step_size = product_now / inner(direction, image, moments)
        answer = axpy(step_size, direction, answer)
        if step + 1 < ITERS:
            residual = axpy(-step_size, image, residual)
            product_next = inner(residual, residual, moments)
            direction = axpy(product_next / product_now, direction, residual)
            product_now = product_next
    return answer


def finish_kernel(moments_ref, diagonal_ref, *refs):
    *refs, solution_hbm, residual_hbm, solution_ref, residual_ref, sems = refs
    streams = [refs[4 * i : 4 * i + 4] for i in range(len(SPLITS))]
    rows = [moments_ref[device] for device in range(moments_ref.shape[0])]
    while len(rows) > 1:
        rows = [a + b for a, b in zip(rows[::2], rows[1::2])]
    row = jnp.broadcast_to(rows[0], (8, 128))
    moments = [jnp.sum(jnp.where(moment_lanes(k), row, 0.0), axis=1, keepdims=True) for k in range(6)]
    place = lax.broadcasted_iota(jnp.int32, (8, 1), 0)
    centers = jnp.zeros((8, 1), jnp.float32)
    for j, center in enumerate(CENTERS):
        centers = jnp.where(place == j, center, centers)
    a0, a1, a2 = recurrence(moments, centers)
    packed = [a0 - centers * (a1 - centers * a2), a1 - (2.0 * centers) * a2, a2]
    mean = centers[0:1] + moments[1][0:1] / moments[0][0:1]
    best = jnp.abs(mean - centers[0:1])
    chosen = [p[0:1] for p in packed]
    for j in range(1, len(CENTERS)):
        away = jnp.abs(mean - centers[j : j + 1])
        better = away < best
        best = jnp.where(better, away, best)
        chosen = [jnp.where(better, p[j : j + 1], c) for p, c in zip(packed, chosen)]
    total, layers = diagonal_ref.shape
    a0, a1, a2 = [jnp.broadcast_to(c, (CHUNK, layers)) for c in chosen]
    copies = []
    for (low, high), stream in zip(SPLITS, streams):
        for at in range(high - low):
            for start in range(0, total, CHUNK):
                here = slice(start, start + CHUNK)
                y0, y1, y2, y3 = [ref[at, here] for ref in stream]
                solution_ref[low + at, here] = a0 * y0 + a1 * y1 + a2 * y2
                residual_ref[low + at, here] = diagonal_ref[here] * (y0 - (a0 * y1 + a1 * y2 + a2 * y3))
            for k, (source, target) in enumerate(((solution_ref, solution_hbm), (residual_ref, residual_hbm))):
                copies.append(pltpu.make_async_copy(source.at[low + at], target.at[low + at], sems.at[k, low + at]))
                copies[-1].start()
    for copy in copies:
        copy.wait()


def call(kernel, out_shapes, *args, scratch=(), place=pltpu.VMEM, out_place=pltpu.VMEM):
    if place is pltpu.HBM:
        args = [pltpu.with_memory_space_constraint(a, place) for a in args]
    outs = [o if isinstance(o, jax.ShapeDtypeStruct) else jax.ShapeDtypeStruct(o, jnp.float32) for o in out_shapes]
    return pl.pallas_call(
        kernel,
        out_shape=outs,
        in_specs=[pl.BlockSpec(memory_space=place)] * len(args),
        out_specs=[pl.BlockSpec(memory_space=out_place)] * len(out_shapes),
        scratch_shapes=[pltpu.VMEM(s, jnp.float32) if isinstance(s, tuple) else s for s in scratch],
        compiler_params=pltpu.CompilerParams(vmem_limit_bytes=24 * 2**20),
    )(*args)


def ring_pairs(groups, tiles):
    beside = [(g * tiles + i, g * tiles + (i ^ 1)) for g in range(groups) for i in range(tiles)]
    across = []
    for g in range(groups):
        for i in range(tiles):
            j = i - 1 if i % 2 == 0 else i + 1
            if j < 0 or j >= tiles:
                across.append((g * tiles + i, (1 - g) * tiles + i))
            else:
                across.append((g * tiles + i, g * tiles + j))
    return beside, across


NAMES = ("diamond", "tile")


def exchange(value):
    beside, across = ring_pairs(lax.axis_size("diamond"), lax.axis_size("tile"))
    far = lax.ppermute(value, NAMES, across)
    near = lax.ppermute(value, NAMES, beside)
    return near, far


def body(adjoint_temp, misfit, viscosity, velocity, forcing, edge_table, pole_table):
    rows, layers = adjoint_temp.shape[2:]
    devices = lax.axis_size("diamond") * lax.axis_size("tile")
    flat, triple = (rows, layers), (3, rows, layers)
    temp, source, visc = (v.reshape(flat) for v in (adjoint_temp, misfit, viscosity))
    visc_near, visc_far = exchange(visc[None])
    table = pltpu.VMEM(edge_table.shape, edge_table.dtype)
    half, side, base, right, part, speed, matrix, sent = call(
        local_kernel,
        [flat, (4, *flat), flat, triple, flat, flat, jax.ShapeDtypeStruct((rows, rows), jnp.bfloat16), flat],
        temp, source, visc, velocity.reshape(triple), forcing.reshape(triple), edge_table, pole_table,
        scratch=[flat, flat, triple, table, table, pltpu.SemaphoreType.DMA((7,))],
        place=pltpu.HBM,
    )
    temp_near, temp_far = exchange(sent[None])
    shapes = [(high - low, rows, layers) for low, high in SPLITS]
    weights, diagonal, inverse, *first = call(
        weigh_kernel, [(6, *flat), flat, flat, *shapes[:-1]],
        visc_far, visc_near, half, side, base, right, matrix, scratch=[(1, *flat)],
    )
    adjoint_next, *rest = call(
        step_kernel, [flat, shapes[-1]],
        temp_near, temp_far, right, part, speed, inverse, matrix, scratch=[(1, *flat)],
    )
    first += rest
    streams = [[field] for field in first]
    swapped = [exchange(field) for field in first]
    for step in range(ITERS - 1):
        for i, shape in enumerate(shapes):
            near, far = swapped[i]
            (field,) = call(apply_kernel, [shape], far, near, streams[i][-1], weights, matrix, scratch=[shape])
            swapped[i] = exchange(field)
            streams[i].append(field)
    many = (len(CENTERS), *triple)
    moments, left, shift = call(
        early_kernel, [(8, 128), many, many], diagonal, *[field for stream in streams for field in stream]
    )
    for i, shape in enumerate(shapes):
        near, far = swapped[i]
        sums = (8, 128) if i + 1 < len(shapes) else (devices, 1, 128)
        field, moments = call(
            functools.partial(last_kernel, SPLITS[i][0]), [shape, sums],
            far, near, streams[i][-1], weights, matrix, moments, left, shift, scratch=[shape],
        )
        streams[i].append(field)
    moments = lax.all_to_all(moments, NAMES, 0, 0)
    fields = [field for stream in streams for field in stream]
    answer, residual = call(
        finish_kernel, [triple, triple], moments, diagonal, *fields,
        scratch=[triple, triple, pltpu.SemaphoreType.DMA((2, 3))], out_place=pltpu.HBM,
    )
    whole = (3, 1, 1, rows, layers)
    return answer.reshape(whole), residual.reshape(whole), adjoint_next.reshape(adjoint_temp.shape)


def solution(mesh):
    flat = P("diamond", "tile", None, None)
    triple = P(None, "diamond", "tile", None, None)
    return jax.shard_map(
        body,
        mesh=mesh,
        in_specs=(flat, flat, flat, triple, triple, P(), P()),
        out_specs=(triple, triple, flat),
        check_vma=False,
    )
```

```python
import functools

import jax
import jax.numpy as jnp
from jax import lax
from jax.experimental import pallas as pl
from jax.experimental.pallas import tpu as pltpu
from jax.sharding import PartitionSpec as P

ITERS = 3
TIME_STEP = 0.1
DIFFUSION = 1.0
MASS_TERM = 0.5
BUOYANCY = 1.0
CENTERS = (0.8, 0.4, 1.3, 0.05, 1.8)
CHUNK = 32
SPLITS = ((0, 1), (1, 2), (2, 3))


def rows_around(load, start, total):
    low, high = max(start - 8, 0), min(start + CHUNK + 8, total)
    block = load(low, high)
    at = start - low
    after = pltpu.roll(block, high - low - 1, 0)[at : at + CHUNK]
    before = pltpu.roll(block, 1, 0)[at : at + CHUNK]
    return block[at : at + CHUNK], after, before


def layers_around(block):
    count = block.shape[1]
    return pltpu.roll(block, count - 1, 1), pltpu.roll(block, 1, 1)


def split3(value):
    top = value.astype(jnp.bfloat16)
    rest = value - top.astype(jnp.float32)
    middle = rest.astype(jnp.bfloat16)
    bottom = (rest - middle.astype(jnp.float32)).astype(jnp.bfloat16)
    return [top, middle, bottom]


def fold_matrix(edge_ref, pole_ref):
    group, tile = lax.axis_index("diamond"), lax.axis_index("tile")
    final = lax.axis_size("tile") - 1
    count = edge_ref.shape[1]
    rows = lax.broadcasted_iota(jnp.int32, (count, count), 0)
    same = lax.broadcasted_iota(jnp.int32, (1, count), 1)
    edge = jnp.where(group == 0, edge_ref[1:2], edge_ref[0:1])
    pole = jnp.where(group == 0, pole_ref[1:2], pole_ref[0:1])
    line = jnp.where(tile == 0, pole, jnp.where(tile == final, edge, same))
    return (rows == line).astype(jnp.bfloat16)


def unfold(matrix_ref, far_ref, out_ref):
    layers = far_ref.shape[2]
    for at in range(far_ref.shape[0]):
        pieces = jnp.concatenate(split3(far_ref[at]), axis=1)
        moved = jnp.dot(matrix_ref[...], pieces, preferred_element_type=jnp.float32)
        out_ref[at] = (
            moved[:, :layers] + moved[:, layers : 2 * layers] + moved[:, 2 * layers :]
        )


def local_kernel(
    temp_hbm, misfit_hbm, visc_hbm, velocity_hbm, forcing_hbm, edge_hbm, pole_hbm,
    half_ref, side_ref, base_ref, right_ref, part_ref, speed_ref, matrix_ref, temp_ref,
    misfit_ref, visc_ref, velocity_ref, edge_ref, pole_ref, sems,
):
    sources = [visc_hbm, temp_hbm, edge_hbm, pole_hbm, velocity_hbm, misfit_hbm, forcing_hbm]
    targets = [visc_ref, temp_ref, edge_ref, pole_ref, velocity_ref, misfit_ref, right_ref]
    copies = [pltpu.make_async_copy(s, t, sems.at[i]) for i, (s, t) in enumerate(zip(sources, targets))]
    for copy in copies:
        copy.start()
    odd = lax.rem(lax.axis_index("tile"), 2)
    half = jnp.where(odd == 0, 0.5, -0.5).astype(jnp.float32)
    total, layers = temp_ref.shape
    for copy in copies:
        copy.wait()
    matrix_ref[...] = fold_matrix(edge_ref, pole_ref)
    for start in range(0, total, CHUNK):
        here = slice(start, start + CHUNK)
        visc, visc_after, visc_before = rows_around(lambda a, b: visc_ref[a:b], start, total)
        temp, temp_after, temp_before = rows_around(lambda a, b: temp_ref[a:b], start, total)
        place = start + lax.broadcasted_iota(jnp.int32, (CHUNK, layers), 0)
        layer = lax.broadcasted_iota(jnp.int32, (CHUNK, layers), 1)
        inside = [place < total - 1, place > 0, layer < layers - 1, layer > 0]
        visc_near = [visc_after, visc_before, *layers_around(visc)]
        temp_near = [temp_after, temp_before, *layers_around(temp)]
        zero = jnp.zeros_like(visc)
        weights = [jnp.where(m, 0.5 * (visc + v), zero) for m, v in zip(inside, visc_near)]
        temps = [jnp.where(m, t, zero) for m, t in zip(inside, temp_near)]
        half_ref[here] = 0.5 * visc
        for k in range(4):
            side_ref[k, here] = weights[k]
        base_ref[here] = MASS_TERM + sum(weights)
        transport = 0.5 * (
            velocity_ref[1, here] * (temps[0] - temps[1]) + velocity_ref[2, here] * (temps[2] - temps[3])
        )
        laplace = sum(temps) - 6.0 * temp
        part_ref[here] = temp + TIME_STEP * (DIFFUSION * laplace + transport) + misfit_ref[here]
        speed_ref[here] = half * velocity_ref[0, here]


def weigh_kernel(
    far_ref, near_ref, half_ref, side_ref, base_ref, right_ref, matrix_ref,
    weights_ref, diagonal_ref, inverse_ref, *refs,
):
    *first_refs, moved_ref = refs
    unfold(matrix_ref, far_ref, moved_ref)
    for start in range(0, half_ref.shape[0], CHUNK):
        here = slice(start, start + CHUNK)
        visc = half_ref[here]
        weights = [visc + 0.5 * near_ref[0, here], visc + 0.5 * moved_ref[0, here]]
        diagonal = base_ref[here] + weights[0] + weights[1]
        diagonal_ref[here] = diagonal
        inverse = 1.0 / diagonal
        inverse_ref[here] = inverse
        for (low, high), first_ref in zip(SPLITS, first_refs):
            for at in range(low, high):
                first_ref[at - low, here] = right_ref[at, here] * inverse
        weights += [side_ref[k, here] for k in range(4)]
        for k in range(6):
            weights_ref[k, here] = weights[k] * inverse


def step_kernel(
    near_ref, far_ref, right_ref, part_ref, speed_ref, inverse_ref, matrix_ref, next_ref, first_ref, moved_ref
):
    unfold(matrix_ref, far_ref, moved_ref)
    for start in range(0, part_ref.shape[0], CHUNK):
        here = slice(start, start + CHUNK)
        near, far = near_ref[0, here], moved_ref[0, here]
        adjoint_next = part_ref[here] + TIME_STEP * (
            DIFFUSION * (near + far) + speed_ref[here] * (near - far)
        )
        next_ref[here] = adjoint_next
        first_ref[0, here] = (right_ref[2, here] + BUOYANCY * adjoint_next) * inverse_ref[here]


def average(start, at, field_ref, near_ref, moved_ref, weights):
    here = slice(start, start + CHUNK)
    mid, after, before = rows_around(lambda a, b: field_ref[at, a:b], start, field_ref.shape[1])
    around = [near_ref[at, here], moved_ref[at, here], after, before, *layers_around(mid)]
    return mid - sum(w * v for w, v in zip(weights, around))


def apply_kernel(near_ref, far_ref, field_ref, weights_ref, matrix_ref, out_ref, moved_ref):
    unfold(matrix_ref, far_ref, moved_ref)
    for start in range(0, field_ref.shape[1], CHUNK):
        here = slice(start, start + CHUNK)
        weights = [weights_ref[k, here] for k in range(6)]
        for at in range(field_ref.shape[0]):
            out_ref[at, here] = average(start, at, field_ref, near_ref, moved_ref, weights)


def fold8(value):
    return jnp.sum(value.reshape(value.shape[0] // 8, 8, value.shape[1]), axis=0)


def moment_lanes(k):
    row = lax.broadcasted_iota(jnp.int32, (8, 128), 0)
    lane = lax.broadcasted_iota(jnp.int32, (8, 128), 1)
    return lane == row + 8 * k


def place_moment(k, sums):
    rows = [jnp.sum(s, axis=0, keepdims=True) for s in sums]
    rows += [rows[0]] * (8 - len(rows))
    column = jnp.sum(jnp.concatenate(rows, axis=0), axis=1, keepdims=True)
    return jnp.where(moment_lanes(k), column, 0.0)


def early_kernel(diagonal_ref, *refs):
    moments_ref, left_ref, shift_ref = refs[-3:]
    total, layers = diagonal_ref.shape
    sums = [[jnp.zeros((8, layers), jnp.float32) for _ in CENTERS] for _ in range(5)]
    for i, (low, high) in enumerate(SPLITS):
        y0_ref, y1_ref, y2_ref = refs[3 * i : 3 * i + 3]
        for start in range(0, total, CHUNK):
            here = slice(start, start + CHUNK)
            diagonal = diagonal_ref[here]
            for at in range(high - low):
                y0, y1, y2 = y0_ref[at, here], y1_ref[at, here], y2_ref[at, here]
                d0 = diagonal * y0
                m0 = fold8(d0 * y0)
                for j, center in enumerate(CENTERS):
                    q1 = y1 - center * y0
                    t2 = y2 - center * y1
                    q2 = t2 - center * q1
                    d1, d2 = diagonal * q1, diagonal * q2
                    left_ref[j, low + at, here] = d2
                    shift_ref[j, low + at, here] = center * (y2 + t2 + q2)
                    sums[0][j] += m0
                    sums[1][j] += fold8(d0 * q1)
                    sums[2][j] += fold8(d1 * q1)
                    sums[3][j] += fold8(d1 * q2)
                    sums[4][j] += fold8(d2 * q2)
    moments_ref[...] = sum(place_moment(k, sums[k]) for k in range(5))


def last_kernel(
    low, far_ref, near_ref, field_ref, weights_ref, matrix_ref, earlier_ref, left_ref, shift_ref,
    out_ref, moments_ref, moved_ref,
):
    unfold(matrix_ref, far_ref, moved_ref)
    total, layers = field_ref.shape[1:]
    sums = [jnp.zeros((8, layers), jnp.float32) for _ in CENTERS]
    for start in range(0, total, CHUNK):
        here = slice(start, start + CHUNK)
        weights = [weights_ref[k, here] for k in range(6)]
        for at in range(field_ref.shape[0]):
            y3 = average(start, at, field_ref, near_ref, moved_ref, weights)
            out_ref[at, here] = y3
            for j in range(len(CENTERS)):
                sums[j] += fold8(left_ref[j, low + at, here] * (y3 - shift_ref[j, low + at, here]))
    message = earlier_ref[...] + place_moment(5, sums)
    if len(moments_ref.shape) == 2:
        moments_ref[...] = message
    else:
        row = jnp.sum(message, axis=0, keepdims=True)
        for device in range(moments_ref.shape[0]):
            moments_ref[device] = row


def last_near_kernel(low, near_ref, far_ref, *refs):
    last_kernel(low, far_ref, near_ref, *refs)


def inner(left, right, moments, shift=0):
    total = 0.0
    for i, a in enumerate(left):
        for j, b in enumerate(right):
            total = total + (a * b) * moments[i + j + shift]
    return total


def axpy(scale, left, right):
    count = max(len(left), len(right))
    result = []
    for i in range(count):
        if i >= len(left):
            result.append(right[i])
        elif i >= len(right):
            result.append(scale * left[i])
        else:
            result.append(scale * left[i] + right[i])
    return result


def recurrence(moments, centers):
    def operator(poly):
        result = [centers * a for a in poly] + [jnp.zeros_like(centers)]
        for i, a in enumerate(poly):
            result[i + 1] = result[i + 1] + a
        return result

    one = jnp.ones_like(centers)
    residual, direction, answer = [one], [one], []
    product_now = moments[0]
    for step in range(ITERS):
        image = operator(direction)
        step_size = product_now / inner(direction, image, moments)
        answer = axpy(step_size, direction, answer)
        if step + 1 < ITERS:
            residual = axpy(-step_size, image, residual)
            product_next = inner(residual, residual, moments)
            direction = axpy(product_next / product_now, direction, residual)
            product_now = product_next
    return answer


def finish_kernel(moments_ref, diagonal_ref, *refs):
    *refs, solution_hbm, residual_hbm, solution_ref, residual_ref, sems = refs
    streams = [refs[4 * i : 4 * i + 4] for i in range(len(SPLITS))]
    rows = [moments_ref[device] for device in range(moments_ref.shape[0])]
    while len(rows) > 1:
        rows = [a + b for a, b in zip(rows[::2], rows[1::2])]
    row = jnp.broadcast_to(rows[0], (8, 128))
    moments = [jnp.sum(jnp.where(moment_lanes(k), row, 0.0), axis=1, keepdims=True) for k in range(6)]
    place = lax.broadcasted_iota(jnp.int32, (8, 1), 0)
    centers = jnp.zeros((8, 1), jnp.float32)
    for j, center in enumerate(CENTERS):
        centers = jnp.where(place == j, center, centers)
    a0, a1, a2 = recurrence(moments, centers)
    packed = [a0 - centers * (a1 - centers * a2), a1 - (2.0 * centers) * a2, a2]
    mean = centers[0:1] + moments[1][0:1] / moments[0][0:1]
    best = jnp.abs(mean - centers[0:1])
    chosen = [p[0:1] for p in packed]
    for j in range(1, len(CENTERS)):
        away = jnp.abs(mean - centers[j : j + 1])
        better = away < best
        best = jnp.where(better, away, best)
        chosen = [jnp.where(better, p[j : j + 1], c) for p, c in zip(packed, chosen)]
    total, layers = diagonal_ref.shape
    a0, a1, a2 = [jnp.broadcast_to(c, (CHUNK, layers)) for c in chosen]
    copies = []
    for (low, high), stream in zip(SPLITS, streams):
        for at in range(high - low):
            for start in range(0, total, CHUNK):
                here = slice(start, start + CHUNK)
                y0, y1, y2, y3 = [ref[at, here] for ref in stream]
                solution_ref[low + at, here] = a0 * y0 + a1 * y1 + a2 * y2
                residual_ref[low + at, here] = diagonal_ref[here] * (y0 - (a0 * y1 + a1 * y2 + a2 * y3))
            for k, (source, target) in enumerate(((solution_ref, solution_hbm), (residual_ref, residual_hbm))):
                copies.append(pltpu.make_async_copy(source.at[low + at], target.at[low + at], sems.at[k, low + at]))
                copies[-1].start()
    for copy in copies:
        copy.wait()


def call(kernel, out_shapes, *args, scratch=(), place=pltpu.VMEM, out_place=pltpu.VMEM):
    if place is pltpu.HBM:
        args = [pltpu.with_memory_space_constraint(a, place) for a in args]
    outs = [o if isinstance(o, jax.ShapeDtypeStruct) else jax.ShapeDtypeStruct(o, jnp.float32) for o in out_shapes]
    return pl.pallas_call(
        kernel,
        out_shape=outs,
        in_specs=[pl.BlockSpec(memory_space=place)] * len(args),
        out_specs=[pl.BlockSpec(memory_space=out_place)] * len(out_shapes),
        scratch_shapes=[pltpu.VMEM(s, jnp.float32) if isinstance(s, tuple) else s for s in scratch],
        compiler_params=pltpu.CompilerParams(vmem_limit_bytes=24 * 2**20),
    )(*args)


def ring_pairs(groups, tiles):
    beside = [(g * tiles + i, g * tiles + (i ^ 1)) for g in range(groups) for i in range(tiles)]
    across = []
    for g in range(groups):
        for i in range(tiles):
            j = i - 1 if i % 2 == 0 else i + 1
            if j < 0 or j >= tiles:
                across.append((g * tiles + i, (1 - g) * tiles + i))
            else:
                across.append((g * tiles + i, g * tiles + j))
    return beside, across


NAMES = ("diamond", "tile")


def exchange(value):
    beside, across = ring_pairs(lax.axis_size("diamond"), lax.axis_size("tile"))
    far = lax.ppermute(value, NAMES, across)
    near = lax.ppermute(value, NAMES, beside)
    return near, far


def body(adjoint_temp, misfit, viscosity, velocity, forcing, edge_table, pole_table):
    rows, layers = adjoint_temp.shape[2:]
    devices = lax.axis_size("diamond") * lax.axis_size("tile")
    flat, triple = (rows, layers), (3, rows, layers)
    temp, source, visc = (v.reshape(flat) for v in (adjoint_temp, misfit, viscosity))
    visc_near, visc_far = exchange(visc[None])
    table = pltpu.VMEM(edge_table.shape, edge_table.dtype)
    half, side, base, right, part, speed, matrix, sent = call(
        local_kernel,
        [flat, (4, *flat), flat, triple, flat, flat, jax.ShapeDtypeStruct((rows, rows), jnp.bfloat16), flat],
        temp, source, visc, velocity.reshape(triple), forcing.reshape(triple), edge_table, pole_table,
        scratch=[flat, flat, triple, table, table, pltpu.SemaphoreType.DMA((7,))],
        place=pltpu.HBM,
    )
    temp_near, temp_far = exchange(sent[None])
    shapes = [(high - low, rows, layers) for low, high in SPLITS]
    weights, diagonal, inverse, *first = call(
        weigh_kernel, [(6, *flat), flat, flat, *shapes[:-1]],
        visc_far, visc_near, half, side, base, right, matrix, scratch=[(1, *flat)],
    )
    adjoint_next, *rest = call(
        step_kernel, [flat, shapes[-1]],
        temp_near, temp_far, right, part, speed, inverse, matrix, scratch=[(1, *flat)],
    )
    first += rest
    streams = [[field] for field in first]
    swapped = [exchange(field) for field in first]
    for step in range(ITERS - 1):
        for i, shape in enumerate(shapes):
            near, far = swapped[i]
            (field,) = call(apply_kernel, [shape], near, far, streams[i][-1], weights, matrix, scratch=[shape])
            swapped[i] = exchange(field)
            streams[i].append(field)
    many = (len(CENTERS), *triple)
    moments, left, shift = call(
        early_kernel, [(8, 128), many, many], diagonal, *[field for stream in streams for field in stream]
    )
    for i, shape in enumerate(shapes):
        near, far = swapped[i]
        sums = (8, 128) if i + 1 < len(shapes) else (devices, 1, 128)
        kernel, halo = (last_near_kernel, [near, far]) if i == 0 else (last_kernel, [far, near])
        field, moments = call(
            functools.partial(kernel, SPLITS[i][0]), [shape, sums],
            *halo, streams[i][-1], weights, matrix, moments, left, shift, scratch=[shape],
        )
        streams[i].append(field)
    moments = lax.all_to_all(moments, NAMES, 0, 0)
    fields = [field for stream in streams for field in stream]
    answer, residual = call(
        finish_kernel, [triple, triple], moments, diagonal, *fields,
        scratch=[triple, triple, pltpu.SemaphoreType.DMA((2, 3))], out_place=pltpu.HBM,
    )
    whole = (3, 1, 1, rows, layers)
    return answer.reshape(whole), residual.reshape(whole), adjoint_next.reshape(adjoint_temp.shape)


def solution(mesh):
    flat = P("diamond", "tile", None, None)
    triple = P(None, "diamond", "tile", None, None)
    return jax.shard_map(
        body,
        mesh=mesh,
        in_specs=(flat, flat, flat, triple, triple, P(), P()),
        out_specs=(triple, triple, flat),
        check_vma=False,
    )
```

```python
import functools

import jax
import jax.numpy as jnp
from jax import lax
from jax.experimental import pallas as pl
from jax.experimental.pallas import tpu as pltpu
from jax.sharding import PartitionSpec as P

ITERS = 3
TIME_STEP = 0.1
DIFFUSION = 1.0
MASS_TERM = 0.5
BUOYANCY = 1.0
CENTERS = (0.8, 0.4, 1.3, 0.05, 1.8)
CHUNK = 32
SPLITS = ((0, 1), (1, 2), (2, 3))


def rows_around(load, start, total):
    low, high = max(start - 8, 0), min(start + CHUNK + 8, total)
    block = load(low, high)
    at = start - low
    after = pltpu.roll(block, high - low - 1, 0)[at : at + CHUNK]
    before = pltpu.roll(block, 1, 0)[at : at + CHUNK]
    return block[at : at + CHUNK], after, before


def layers_around(block):
    count = block.shape[1]
    return pltpu.roll(block, count - 1, 1), pltpu.roll(block, 1, 1)


def split3(value):
    top = value.astype(jnp.bfloat16)
    rest = value - top.astype(jnp.float32)
    middle = rest.astype(jnp.bfloat16)
    bottom = (rest - middle.astype(jnp.float32)).astype(jnp.bfloat16)
    return [top, middle, bottom]


def fold_matrix(edge_ref, pole_ref):
    group, tile = lax.axis_index("diamond"), lax.axis_index("tile")
    final = lax.axis_size("tile") - 1
    count = edge_ref.shape[1]
    rows = lax.broadcasted_iota(jnp.int32, (count, count), 0)
    same = lax.broadcasted_iota(jnp.int32, (1, count), 1)
    edge = jnp.where(group == 0, edge_ref[1:2], edge_ref[0:1])
    pole = jnp.where(group == 0, pole_ref[1:2], pole_ref[0:1])
    line = jnp.where(tile == 0, pole, jnp.where(tile == final, edge, same))
    return (rows == line).astype(jnp.bfloat16)


def unfold(matrix_ref, far_ref, out_ref):
    layers = far_ref.shape[2]
    for at in range(far_ref.shape[0]):
        pieces = jnp.concatenate(split3(far_ref[at]), axis=1)
        moved = jnp.dot(matrix_ref[...], pieces, preferred_element_type=jnp.float32)
        out_ref[at] = (
            moved[:, :layers] + moved[:, layers : 2 * layers] + moved[:, 2 * layers :]
        )


def local_kernel(
    temp_hbm, misfit_hbm, visc_hbm, velocity_hbm, forcing_hbm, edge_hbm, pole_hbm,
    half_ref, side_ref, base_ref, right_ref, part_ref, speed_ref, matrix_ref, temp_ref,
    misfit_ref, visc_ref, velocity_ref, edge_ref, pole_ref, sems,
):
    sources = [visc_hbm, temp_hbm, edge_hbm, pole_hbm, velocity_hbm, misfit_hbm, forcing_hbm]
    targets = [visc_ref, temp_ref, edge_ref, pole_ref, velocity_ref, misfit_ref, right_ref]
    copies = [pltpu.make_async_copy(s, t, sems.at[i]) for i, (s, t) in enumerate(zip(sources, targets))]
    for copy in copies:
        copy.start()
    odd = lax.rem(lax.axis_index("tile"), 2)
    half = jnp.where(odd == 0, 0.5, -0.5).astype(jnp.float32)
    total, layers = temp_ref.shape
    for copy in copies:
        copy.wait()
    matrix_ref[...] = fold_matrix(edge_ref, pole_ref)
    for start in range(0, total, CHUNK):
        here = slice(start, start + CHUNK)
        visc, visc_after, visc_before = rows_around(lambda a, b: visc_ref[a:b], start, total)
        temp, temp_after, temp_before = rows_around(lambda a, b: temp_ref[a:b], start, total)
        place = start + lax.broadcasted_iota(jnp.int32, (CHUNK, layers), 0)
        layer = lax.broadcasted_iota(jnp.int32, (CHUNK, layers), 1)
        inside = [place < total - 1, place > 0, layer < layers - 1, layer > 0]
        visc_near = [visc_after, visc_before, *layers_around(visc)]
        temp_near = [temp_after, temp_before, *layers_around(temp)]
        zero = jnp.zeros_like(visc)
        weights = [jnp.where(m, 0.5 * (visc + v), zero) for m, v in zip(inside, visc_near)]
        temps = [jnp.where(m, t, zero) for m, t in zip(inside, temp_near)]
        half_ref[here] = 0.5 * visc
        for k in range(4):
            side_ref[k, here] = weights[k]
        base_ref[here] = MASS_TERM + sum(weights)
        transport = 0.5 * (
            velocity_ref[1, here] * (temps[0] - temps[1]) + velocity_ref[2, here] * (temps[2] - temps[3])
        )
        laplace = sum(temps) - 6.0 * temp
        part_ref[here] = temp + TIME_STEP * (DIFFUSION * laplace + transport) + misfit_ref[here]
        speed_ref[here] = half * velocity_ref[0, here]


def weigh_kernel(
    far_ref, near_ref, half_ref, side_ref, base_ref, right_ref, matrix_ref,
    weights_ref, diagonal_ref, inverse_ref, *refs,
):
    *first_refs, moved_ref = refs
    unfold(matrix_ref, far_ref, moved_ref)
    for start in range(0, half_ref.shape[0], CHUNK):
        here = slice(start, start + CHUNK)
        visc = half_ref[here]
        weights = [visc + 0.5 * near_ref[0, here], visc + 0.5 * moved_ref[0, here]]
        diagonal = base_ref[here] + weights[0] + weights[1]
        diagonal_ref[here] = diagonal
        inverse = 1.0 / diagonal
        inverse_ref[here] = inverse
        for (low, high), first_ref in zip(SPLITS, first_refs):
            for at in range(low, high):
                first_ref[at - low, here] = right_ref[at, here] * inverse
        weights += [side_ref[k, here] for k in range(4)]
        for k in range(6):
            weights_ref[k, here] = weights[k] * inverse


def step_kernel(
    near_ref, far_ref, right_ref, part_ref, speed_ref, inverse_ref, matrix_ref, next_ref, first_ref, moved_ref
):
    unfold(matrix_ref, far_ref, moved_ref)
    for start in range(0, part_ref.shape[0], CHUNK):
        here = slice(start, start + CHUNK)
        near, far = near_ref[0, here], moved_ref[0, here]
        adjoint_next = part_ref[here] + TIME_STEP * (
            DIFFUSION * (near + far) + speed_ref[here] * (near - far)
        )
        next_ref[here] = adjoint_next
        first_ref[0, here] = (right_ref[2, here] + BUOYANCY * adjoint_next) * inverse_ref[here]


def average(start, at, field_ref, near_ref, moved_ref, weights):
    here = slice(start, start + CHUNK)
    mid, after, before = rows_around(lambda a, b: field_ref[at, a:b], start, field_ref.shape[1])
    around = [near_ref[at, here], moved_ref[at, here], after, before, *layers_around(mid)]
    return mid - sum(w * v for w, v in zip(weights, around))


def apply_kernel(near_ref, far_ref, field_ref, weights_ref, matrix_ref, out_ref, moved_ref):
    unfold(matrix_ref, far_ref, moved_ref)
    for start in range(0, field_ref.shape[1], CHUNK):
        here = slice(start, start + CHUNK)
        weights = [weights_ref[k, here] for k in range(6)]
        for at in range(field_ref.shape[0]):
            out_ref[at, here] = average(start, at, field_ref, near_ref, moved_ref, weights)


def fold8(value):
    return jnp.sum(value.reshape(value.shape[0] // 8, 8, value.shape[1]), axis=0)


def moment_lanes(k):
    row = lax.broadcasted_iota(jnp.int32, (8, 128), 0)
    lane = lax.broadcasted_iota(jnp.int32, (8, 128), 1)
    return lane == row + 8 * k


def place_moment(k, sums):
    rows = [jnp.sum(s, axis=0, keepdims=True) for s in sums]
    rows += [rows[0]] * (8 - len(rows))
    column = jnp.sum(jnp.concatenate(rows, axis=0), axis=1, keepdims=True)
    return jnp.where(moment_lanes(k), column, 0.0)


def early_kernel(diagonal_ref, *refs):
    moments_ref, left_ref, shift_ref = refs[-3:]
    total, layers = diagonal_ref.shape
    sums = [[jnp.zeros((8, layers), jnp.float32) for _ in CENTERS] for _ in range(5)]
    for i, (low, high) in enumerate(SPLITS):
        y0_ref, y1_ref, y2_ref = refs[3 * i : 3 * i + 3]
        for start in range(0, total, CHUNK):
            here = slice(start, start + CHUNK)
            diagonal = diagonal_ref[here]
            for at in range(high - low):
                y0, y1, y2 = y0_ref[at, here], y1_ref[at, here], y2_ref[at, here]
                d0 = diagonal * y0
                m0 = fold8(d0 * y0)
                for j, center in enumerate(CENTERS):
                    q1 = y1 - center * y0
                    t2 = y2 - center * y1
                    q2 = t2 - center * q1
                    d1, d2 = diagonal * q1, diagonal * q2
                    left_ref[j, low + at, here] = d2
                    shift_ref[j, low + at, here] = center * (y2 + t2 + q2)
                    sums[0][j] += m0
                    sums[1][j] += fold8(d0 * q1)
                    sums[2][j] += fold8(d1 * q1)
                    sums[3][j] += fold8(d1 * q2)
                    sums[4][j] += fold8(d2 * q2)
    moments_ref[...] = sum(place_moment(k, sums[k]) for k in range(5))


def last_kernel(
    low, far_ref, near_ref, field_ref, weights_ref, matrix_ref, earlier_ref, left_ref, shift_ref,
    out_ref, moments_ref, moved_ref,
):
    unfold(matrix_ref, far_ref, moved_ref)
    total, layers = field_ref.shape[1:]
    sums = [jnp.zeros((8, layers), jnp.float32) for _ in CENTERS]
    for start in range(0, total, CHUNK):
        here = slice(start, start + CHUNK)
        weights = [weights_ref[k, here] for k in range(6)]
        for at in range(field_ref.shape[0]):
            y3 = average(start, at, field_ref, near_ref, moved_ref, weights)
            out_ref[at, here] = y3
            for j in range(len(CENTERS)):
                sums[j] += fold8(left_ref[j, low + at, here] * (y3 - shift_ref[j, low + at, here]))
    message = earlier_ref[...] + place_moment(5, sums)
    if len(moments_ref.shape) == 2:
        moments_ref[...] = message
    else:
        row = jnp.sum(message, axis=0, keepdims=True)
        for device in range(moments_ref.shape[0]):
            moments_ref[device] = row


def last_near_kernel(low, near_ref, far_ref, *refs):
    last_kernel(low, far_ref, near_ref, *refs)


def inner(left, right, moments, shift=0):
    total = 0.0
    for i, a in enumerate(left):
        for j, b in enumerate(right):
            total = total + (a * b) * moments[i + j + shift]
    return total


def axpy(scale, left, right):
    count = max(len(left), len(right))
    result = []
    for i in range(count):
        if i >= len(left):
            result.append(right[i])
        elif i >= len(right):
            result.append(scale * left[i])
        else:
            result.append(scale * left[i] + right[i])
    return result


def recurrence(moments, centers):
    def operator(poly):
        result = [centers * a for a in poly] + [jnp.zeros_like(centers)]
        for i, a in enumerate(poly):
            result[i + 1] = result[i + 1] + a
        return result

    one = jnp.ones_like(centers)
    residual, direction, answer = [one], [one], []
    product_now = moments[0]
    for step in range(ITERS):
        image = operator(direction)
        step_size = product_now / inner(direction, image, moments)
        answer = axpy(step_size, direction, answer)
        if step + 1 < ITERS:
            residual = axpy(-step_size, image, residual)
            product_next = inner(residual, residual, moments)
            direction = axpy(product_next / product_now, direction, residual)
            product_now = product_next
    return answer


def finish_kernel(moments_ref, diagonal_ref, next_ref, *refs):
    *refs, solution_hbm, residual_hbm, next_hbm, solution_ref, residual_ref, sems, next_sem = refs
    copies = [pltpu.make_async_copy(next_ref, next_hbm, next_sem)]
    copies[0].start()
    streams = [refs[4 * i : 4 * i + 4] for i in range(len(SPLITS))]
    rows = [moments_ref[device] for device in range(moments_ref.shape[0])]
    while len(rows) > 1:
        rows = [a + b for a, b in zip(rows[::2], rows[1::2])]
    row = jnp.broadcast_to(rows[0], (8, 128))
    moments = [jnp.sum(jnp.where(moment_lanes(k), row, 0.0), axis=1, keepdims=True) for k in range(6)]
    place = lax.broadcasted_iota(jnp.int32, (8, 1), 0)
    centers = jnp.zeros((8, 1), jnp.float32)
    for j, center in enumerate(CENTERS):
        centers = jnp.where(place == j, center, centers)
    a0, a1, a2 = recurrence(moments, centers)
    packed = [a0 - centers * (a1 - centers * a2), a1 - (2.0 * centers) * a2, a2]
    mean = centers[0:1] + moments[1][0:1] / moments[0][0:1]
    best = jnp.abs(mean - centers[0:1])
    chosen = [p[0:1] for p in packed]
    for j in range(1, len(CENTERS)):
        away = jnp.abs(mean - centers[j : j + 1])
        better = away < best
        best = jnp.where(better, away, best)
        chosen = [jnp.where(better, p[j : j + 1], c) for p, c in zip(packed, chosen)]
    total, layers = diagonal_ref.shape
    a0, a1, a2 = [jnp.broadcast_to(c, (CHUNK, layers)) for c in chosen]
    for (low, high), stream in zip(SPLITS, streams):
        for at in range(high - low):
            for start in range(0, total, CHUNK):
                here = slice(start, start + CHUNK)
                y0, y1, y2, y3 = [ref[at, here] for ref in stream]
                solution_ref[low + at, here] = a0 * y0 + a1 * y1 + a2 * y2
                residual_ref[low + at, here] = diagonal_ref[here] * (y0 - (a0 * y1 + a1 * y2 + a2 * y3))
            for k, (source, target) in enumerate(((solution_ref, solution_hbm), (residual_ref, residual_hbm))):
                copies.append(pltpu.make_async_copy(source.at[low + at], target.at[low + at], sems.at[k, low + at]))
                copies[-1].start()
    for copy in copies:
        copy.wait()


def call(kernel, out_shapes, *args, scratch=(), place=pltpu.VMEM, out_place=pltpu.VMEM):
    if place is pltpu.HBM:
        args = [pltpu.with_memory_space_constraint(a, place) for a in args]
    outs = [o if isinstance(o, jax.ShapeDtypeStruct) else jax.ShapeDtypeStruct(o, jnp.float32) for o in out_shapes]
    return pl.pallas_call(
        kernel,
        out_shape=outs,
        in_specs=[pl.BlockSpec(memory_space=place)] * len(args),
        out_specs=[pl.BlockSpec(memory_space=out_place)] * len(out_shapes),
        scratch_shapes=[pltpu.VMEM(s, jnp.float32) if isinstance(s, tuple) else s for s in scratch],
        compiler_params=pltpu.CompilerParams(vmem_limit_bytes=24 * 2**20),
    )(*args)


def ring_pairs(groups, tiles):
    beside = [(g * tiles + i, g * tiles + (i ^ 1)) for g in range(groups) for i in range(tiles)]
    across = []
    for g in range(groups):
        for i in range(tiles):
            j = i - 1 if i % 2 == 0 else i + 1
            if j < 0 or j >= tiles:
                across.append((g * tiles + i, (1 - g) * tiles + i))
            else:
                across.append((g * tiles + i, g * tiles + j))
    return beside, across


NAMES = ("diamond", "tile")


def exchange(value):
    beside, across = ring_pairs(lax.axis_size("diamond"), lax.axis_size("tile"))
    far = lax.ppermute(value, NAMES, across)
    near = lax.ppermute(value, NAMES, beside)
    return near, far


def body(adjoint_temp, misfit, viscosity, velocity, forcing, edge_table, pole_table):
    rows, layers = adjoint_temp.shape[2:]
    devices = lax.axis_size("diamond") * lax.axis_size("tile")
    flat, triple = (rows, layers), (3, rows, layers)
    temp, source, visc = (v.reshape(flat) for v in (adjoint_temp, misfit, viscosity))
    visc_near, visc_far = exchange(visc[None])
    table = pltpu.VMEM(edge_table.shape, edge_table.dtype)
    half, side, base, right, part, speed, matrix, sent = call(
        local_kernel,
        [flat, (4, *flat), flat, triple, flat, flat, jax.ShapeDtypeStruct((rows, rows), jnp.bfloat16), flat],
        temp, source, visc, velocity.reshape(triple), forcing.reshape(triple), edge_table, pole_table,
        scratch=[flat, flat, triple, table, table, pltpu.SemaphoreType.DMA((7,))],
        place=pltpu.HBM,
    )
    temp_near, temp_far = exchange(sent[None])
    shapes = [(high - low, rows, layers) for low, high in SPLITS]
    weights, diagonal, inverse, *first = call(
        weigh_kernel, [(6, *flat), flat, flat, *shapes[:-1]],
        visc_far, visc_near, half, side, base, right, matrix, scratch=[(1, *flat)],
    )
    adjoint_next, *rest = call(
        step_kernel, [flat, shapes[-1]],
        temp_near, temp_far, right, part, speed, inverse, matrix, scratch=[(1, *flat)],
    )
    first += rest
    streams = [[field] for field in first]
    swapped = [exchange(field) for field in first]
    for step in range(ITERS - 1):
        for i, shape in enumerate(shapes):
            near, far = swapped[i]
            (field,) = call(apply_kernel, [shape], near, far, streams[i][-1], weights, matrix, scratch=[shape])
            swapped[i] = exchange(field)
            streams[i].append(field)
    many = (len(CENTERS), *triple)
    moments, left, shift = call(
        early_kernel, [(8, 128), many, many], diagonal, *[field for stream in streams for field in stream]
    )
    for i, shape in enumerate(shapes):
        near, far = swapped[i]
        sums = (8, 128) if i + 1 < len(shapes) else (devices, 1, 128)
        kernel, halo = (last_near_kernel, [near, far]) if i == 0 else (last_kernel, [far, near])
        field, moments = call(
            functools.partial(kernel, SPLITS[i][0]), [shape, sums],
            *halo, streams[i][-1], weights, matrix, moments, left, shift, scratch=[shape],
        )
        streams[i].append(field)
    moments = lax.all_to_all(moments, NAMES, 0, 0)
    fields = [field for stream in streams for field in stream]
    answer, residual, adjoint_next = call(
        finish_kernel, [triple, triple, flat], moments, diagonal, adjoint_next, *fields,
        scratch=[triple, triple, pltpu.SemaphoreType.DMA((2, 3)), pltpu.SemaphoreType.DMA], out_place=pltpu.HBM,
    )
    whole = (3, 1, 1, rows, layers)
    return answer.reshape(whole), residual.reshape(whole), adjoint_next.reshape(adjoint_temp.shape)


def solution(mesh):
    flat = P("diamond", "tile", None, None)
    triple = P(None, "diamond", "tile", None, None)
    return jax.shard_map(
        body,
        mesh=mesh,
        in_specs=(flat, flat, flat, triple, triple, P(), P()),
        out_specs=(triple, triple, flat),
        check_vma=False,
    )
```

```python
import functools

import jax
import jax.numpy as jnp
from jax import lax
from jax.experimental import pallas as pl
from jax.experimental.pallas import tpu as pltpu
from jax.sharding import PartitionSpec as P

ITERS = 3
TIME_STEP = 0.1
DIFFUSION = 1.0
MASS_TERM = 0.5
BUOYANCY = 1.0
CENTERS = (0.8, 0.4, 1.3, 0.05, 1.8)
CHUNK = 32
SPLITS = ((0, 1), (1, 2), (2, 3))


def rows_around(load, start, total):
    low, high = max(start - 8, 0), min(start + CHUNK + 8, total)
    block = load(low, high)
    at = start - low
    after = pltpu.roll(block, high - low - 1, 0)[at : at + CHUNK]
    before = pltpu.roll(block, 1, 0)[at : at + CHUNK]
    return block[at : at + CHUNK], after, before


def layers_around(block):
    count = block.shape[1]
    return pltpu.roll(block, count - 1, 1), pltpu.roll(block, 1, 1)


def split3(value):
    top = value.astype(jnp.bfloat16)
    rest = value - top.astype(jnp.float32)
    middle = rest.astype(jnp.bfloat16)
    bottom = (rest - middle.astype(jnp.float32)).astype(jnp.bfloat16)
    return [top, middle, bottom]


def fold_matrix(edge_ref, pole_ref):
    group, tile = lax.axis_index("diamond"), lax.axis_index("tile")
    final = lax.axis_size("tile") - 1
    count = edge_ref.shape[1]
    rows = lax.broadcasted_iota(jnp.int32, (count, count), 0)
    same = lax.broadcasted_iota(jnp.int32, (1, count), 1)
    edge = jnp.where(group == 0, edge_ref[1:2], edge_ref[0:1])
    pole = jnp.where(group == 0, pole_ref[1:2], pole_ref[0:1])
    line = jnp.where(tile == 0, pole, jnp.where(tile == final, edge, same))
    return (rows == line).astype(jnp.bfloat16)


def unfold(matrix_ref, far_ref, out_ref):
    layers = far_ref.shape[2]
    tile = lax.axis_index("tile")
    folded = jnp.logical_or(tile == 0, tile == lax.axis_size("tile") - 1)

    @pl.when(folded)
    def _():
        for at in range(far_ref.shape[0]):
            pieces = jnp.concatenate(split3(far_ref[at]), axis=1)
            moved = jnp.dot(matrix_ref[...], pieces, preferred_element_type=jnp.float32)
            out_ref[at] = (
                moved[:, :layers] + moved[:, layers : 2 * layers] + moved[:, 2 * layers :]
            )

    @pl.when(jnp.logical_not(folded))
    def _():
        out_ref[...] = far_ref[...]


def local_kernel(
    temp_hbm, misfit_hbm, visc_hbm, velocity_hbm, forcing_hbm, edge_hbm, pole_hbm,
    half_ref, side_ref, base_ref, right_ref, part_ref, speed_ref, matrix_ref, temp_ref,
    misfit_ref, visc_ref, velocity_ref, edge_ref, pole_ref, sems,
):
    sources = [visc_hbm, temp_hbm, edge_hbm, pole_hbm, velocity_hbm, misfit_hbm, forcing_hbm]
    targets = [visc_ref, temp_ref, edge_ref, pole_ref, velocity_ref, misfit_ref, right_ref]
    copies = [pltpu.make_async_copy(s, t, sems.at[i]) for i, (s, t) in enumerate(zip(sources, targets))]
    for copy in copies:
        copy.start()
    odd = lax.rem(lax.axis_index("tile"), 2)
    half = jnp.where(odd == 0, 0.5, -0.5).astype(jnp.float32)
    total, layers = temp_ref.shape
    for copy in copies:
        copy.wait()
    matrix_ref[...] = fold_matrix(edge_ref, pole_ref)
    for start in range(0, total, CHUNK):
        here = slice(start, start + CHUNK)
        visc, visc_after, visc_before = rows_around(lambda a, b: visc_ref[a:b], start, total)
        temp, temp_after, temp_before = rows_around(lambda a, b: temp_ref[a:b], start, total)
        place = start + lax.broadcasted_iota(jnp.int32, (CHUNK, layers), 0)
        layer = lax.broadcasted_iota(jnp.int32, (CHUNK, layers), 1)
        inside = [place < total - 1, place > 0, layer < layers - 1, layer > 0]
        visc_near = [visc_after, visc_before, *layers_around(visc)]
        temp_near = [temp_after, temp_before, *layers_around(temp)]
        zero = jnp.zeros_like(visc)
        weights = [jnp.where(m, 0.5 * (visc + v), zero) for m, v in zip(inside, visc_near)]
        temps = [jnp.where(m, t, zero) for m, t in zip(inside, temp_near)]
        half_ref[here] = 0.5 * visc
        for k in range(4):
            side_ref[k, here] = weights[k]
        base_ref[here] = MASS_TERM + sum(weights)
        transport = 0.5 * (
            velocity_ref[1, here] * (temps[0] - temps[1]) + velocity_ref[2, here] * (temps[2] - temps[3])
        )
        laplace = sum(temps) - 6.0 * temp
        part_ref[here] = temp + TIME_STEP * (DIFFUSION * laplace + transport) + misfit_ref[here]
        speed_ref[here] = half * velocity_ref[0, here]


def weigh_kernel(
    far_ref, near_ref, half_ref, side_ref, base_ref, right_ref, matrix_ref,
    weights_ref, diagonal_ref, inverse_ref, *refs,
):
    *first_refs, moved_ref = refs
    unfold(matrix_ref, far_ref, moved_ref)
    for start in range(0, half_ref.shape[0], CHUNK):
        here = slice(start, start + CHUNK)
        visc = half_ref[here]
        weights = [visc + 0.5 * near_ref[0, here], visc + 0.5 * moved_ref[0, here]]
        diagonal = base_ref[here] + weights[0] + weights[1]
        diagonal_ref[here] = diagonal
        inverse = 1.0 / diagonal
        inverse_ref[here] = inverse
        for (low, high), first_ref in zip(SPLITS, first_refs):
            for at in range(low, high):
                first_ref[at - low, here] = right_ref[at, here] * inverse
        weights += [side_ref[k, here] for k in range(4)]
        for k in range(6):
            weights_ref[k, here] = weights[k] * inverse


def step_kernel(
    near_ref, far_ref, right_ref, part_ref, speed_ref, inverse_ref, matrix_ref, next_ref, first_ref, moved_ref
):
    unfold(matrix_ref, far_ref, moved_ref)
    for start in range(0, part_ref.shape[0], CHUNK):
        here = slice(start, start + CHUNK)
        near, far = near_ref[0, here], moved_ref[0, here]
        adjoint_next = part_ref[here] + TIME_STEP * (
            DIFFUSION * (near + far) + speed_ref[here] * (near - far)
        )
        next_ref[here] = adjoint_next
        first_ref[0, here] = (right_ref[2, here] + BUOYANCY * adjoint_next) * inverse_ref[here]


def average(start, at, field_ref, near_ref, moved_ref, weights):
    here = slice(start, start + CHUNK)
    mid, after, before = rows_around(lambda a, b: field_ref[at, a:b], start, field_ref.shape[1])
    around = [near_ref[at, here], moved_ref[at, here], after, before, *layers_around(mid)]
    return mid - sum(w * v for w, v in zip(weights, around))


def apply_kernel(near_ref, far_ref, field_ref, weights_ref, matrix_ref, out_ref, moved_ref):
    unfold(matrix_ref, far_ref, moved_ref)
    for start in range(0, field_ref.shape[1], CHUNK):
        here = slice(start, start + CHUNK)
        weights = [weights_ref[k, here] for k in range(6)]
        for at in range(field_ref.shape[0]):
            out_ref[at, here] = average(start, at, field_ref, near_ref, moved_ref, weights)


def fold8(value):
    return jnp.sum(value.reshape(value.shape[0] // 8, 8, value.shape[1]), axis=0)


def moment_lanes(k):
    row = lax.broadcasted_iota(jnp.int32, (8, 128), 0)
    lane = lax.broadcasted_iota(jnp.int32, (8, 128), 1)
    return lane == row + 8 * k


def place_moment(k, sums):
    rows = [jnp.sum(s, axis=0, keepdims=True) for s in sums]
    rows += [rows[0]] * (8 - len(rows))
    column = jnp.sum(jnp.concatenate(rows, axis=0), axis=1, keepdims=True)
    return jnp.where(moment_lanes(k), column, 0.0)


def early_kernel(diagonal_ref, *refs):
    moments_ref, left_ref, shift_ref = refs[-3:]
    total, layers = diagonal_ref.shape
    sums = [[jnp.zeros((8, layers), jnp.float32) for _ in CENTERS] for _ in range(5)]
    for i, (low, high) in enumerate(SPLITS):
        y0_ref, y1_ref, y2_ref = refs[3 * i : 3 * i + 3]
        for start in range(0, total, CHUNK):
            here = slice(start, start + CHUNK)
            diagonal = diagonal_ref[here]
            for at in range(high - low):
                y0, y1, y2 = y0_ref[at, here], y1_ref[at, here], y2_ref[at, here]
                d0 = diagonal * y0
                m0 = fold8(d0 * y0)
                for j, center in enumerate(CENTERS):
                    q1 = y1 - center * y0
                    t2 = y2 - center * y1
                    q2 = t2 - center * q1
                    d1, d2 = diagonal * q1, diagonal * q2
                    left_ref[j, low + at, here] = d2
                    shift_ref[j, low + at, here] = center * (y2 + t2 + q2)
                    sums[0][j] += m0
                    sums[1][j] += fold8(d0 * q1)
                    sums[2][j] += fold8(d1 * q1)
                    sums[3][j] += fold8(d1 * q2)
                    sums[4][j] += fold8(d2 * q2)
    moments_ref[...] = sum(place_moment(k, sums[k]) for k in range(5))


def last_kernel(
    low, far_ref, near_ref, field_ref, weights_ref, matrix_ref, earlier_ref, left_ref, shift_ref,
    out_ref, moments_ref, moved_ref,
):
    unfold(matrix_ref, far_ref, moved_ref)
    total, layers = field_ref.shape[1:]
    sums = [jnp.zeros((8, layers), jnp.float32) for _ in CENTERS]
    for start in range(0, total, CHUNK):
        here = slice(start, start + CHUNK)
        weights = [weights_ref[k, here] for k in range(6)]
        for at in range(field_ref.shape[0]):
            y3 = average(start, at, field_ref, near_ref, moved_ref, weights)
            out_ref[at, here] = y3
            for j in range(len(CENTERS)):
                sums[j] += fold8(left_ref[j, low + at, here] * (y3 - shift_ref[j, low + at, here]))
    message = earlier_ref[...] + place_moment(5, sums)
    if len(moments_ref.shape) == 2:
        moments_ref[...] = message
    else:
        row = jnp.sum(message, axis=0, keepdims=True)
        for device in range(moments_ref.shape[0]):
            moments_ref[device] = row


def last_near_kernel(low, near_ref, far_ref, *refs):
    last_kernel(low, far_ref, near_ref, *refs)


def inner(left, right, moments, shift=0):
    total = 0.0
    for i, a in enumerate(left):
        for j, b in enumerate(right):
            total = total + (a * b) * moments[i + j + shift]
    return total


def axpy(scale, left, right):
    count = max(len(left), len(right))
    result = []
    for i in range(count):
        if i >= len(left):
            result.append(right[i])
        elif i >= len(right):
            result.append(scale * left[i])
        else:
            result.append(scale * left[i] + right[i])
    return result


def recurrence(moments, centers):
    def operator(poly):
        result = [centers * a for a in poly] + [jnp.zeros_like(centers)]
        for i, a in enumerate(poly):
            result[i + 1] = result[i + 1] + a
        return result

    one = jnp.ones_like(centers)
    residual, direction, answer = [one], [one], []
    product_now = moments[0]
    for step in range(ITERS):
        image = operator(direction)
        step_size = product_now / inner(direction, image, moments)
        answer = axpy(step_size, direction, answer)
        if step + 1 < ITERS:
            residual = axpy(-step_size, image, residual)
            product_next = inner(residual, residual, moments)
            direction = axpy(product_next / product_now, direction, residual)
            product_now = product_next
    return answer


def finish_kernel(moments_ref, diagonal_ref, *refs):
    *refs, solution_hbm, residual_hbm, solution_ref, residual_ref, sems = refs
    streams = [refs[4 * i : 4 * i + 4] for i in range(len(SPLITS))]
    rows = [moments_ref[device] for device in range(moments_ref.shape[0])]
    while len(rows) > 1:
        rows = [a + b for a, b in zip(rows[::2], rows[1::2])]
    row = jnp.broadcast_to(rows[0], (8, 128))
    moments = [jnp.sum(jnp.where(moment_lanes(k), row, 0.0), axis=1, keepdims=True) for k in range(6)]
    place = lax.broadcasted_iota(jnp.int32, (8, 1), 0)
    centers = jnp.zeros((8, 1), jnp.float32)
    for j, center in enumerate(CENTERS):
        centers = jnp.where(place == j, center, centers)
    a0, a1, a2 = recurrence(moments, centers)
    packed = [a0 - centers * (a1 - centers * a2), a1 - (2.0 * centers) * a2, a2]
    mean = centers[0:1] + moments[1][0:1] / moments[0][0:1]
    best = jnp.abs(mean - centers[0:1])
    chosen = [p[0:1] for p in packed]
    for j in range(1, len(CENTERS)):
        away = jnp.abs(mean - centers[j : j + 1])
        better = away < best
        best = jnp.where(better, away, best)
        chosen = [jnp.where(better, p[j : j + 1], c) for p, c in zip(packed, chosen)]
    total, layers = diagonal_ref.shape
    a0, a1, a2 = [jnp.broadcast_to(c, (CHUNK, layers)) for c in chosen]
    copies = []
    for (low, high), stream in zip(SPLITS, streams):
        for at in range(high - low):
            for start in range(0, total, CHUNK):
                here = slice(start, start + CHUNK)
                y0, y1, y2, y3 = [ref[at, here] for ref in stream]
                solution_ref[low + at, here] = a0 * y0 + a1 * y1 + a2 * y2
                residual_ref[low + at, here] = diagonal_ref[here] * (y0 - (a0 * y1 + a1 * y2 + a2 * y3))
            for k, (source, target) in enumerate(((solution_ref, solution_hbm), (residual_ref, residual_hbm))):
                copies.append(pltpu.make_async_copy(source.at[low + at], target.at[low + at], sems.at[k, low + at]))
                copies[-1].start()
    for copy in copies:
        copy.wait()


def call(kernel, out_shapes, *args, scratch=(), place=pltpu.VMEM, out_place=pltpu.VMEM):
    if place is pltpu.HBM:
        args = [pltpu.with_memory_space_constraint(a, place) for a in args]
    outs = [o if isinstance(o, jax.ShapeDtypeStruct) else jax.ShapeDtypeStruct(o, jnp.float32) for o in out_shapes]
    return pl.pallas_call(
        kernel,
        out_shape=outs,
        in_specs=[pl.BlockSpec(memory_space=place)] * len(args),
        out_specs=[pl.BlockSpec(memory_space=out_place)] * len(out_shapes),
        scratch_shapes=[pltpu.VMEM(s, jnp.float32) if isinstance(s, tuple) else s for s in scratch],
        compiler_params=pltpu.CompilerParams(vmem_limit_bytes=24 * 2**20),
    )(*args)


def ring_pairs(groups, tiles):
    beside = [(g * tiles + i, g * tiles + (i ^ 1)) for g in range(groups) for i in range(tiles)]
    across = []
    for g in range(groups):
        for i in range(tiles):
            j = i - 1 if i % 2 == 0 else i + 1
            if j < 0 or j >= tiles:
                across.append((g * tiles + i, (1 - g) * tiles + i))
            else:
                across.append((g * tiles + i, g * tiles + j))
    return beside, across


NAMES = ("diamond", "tile")


def exchange(value):
    beside, across = ring_pairs(lax.axis_size("diamond"), lax.axis_size("tile"))
    far = lax.ppermute(value, NAMES, across)
    near = lax.ppermute(value, NAMES, beside)
    return near, far


def body(adjoint_temp, misfit, viscosity, velocity, forcing, edge_table, pole_table):
    rows, layers = adjoint_temp.shape[2:]
    devices = lax.axis_size("diamond") * lax.axis_size("tile")
    flat, triple = (rows, layers), (3, rows, layers)
    temp, source, visc = (v.reshape(flat) for v in (adjoint_temp, misfit, viscosity))
    visc_near, visc_far = exchange(visc[None])
    table = pltpu.VMEM(edge_table.shape, edge_table.dtype)
    half, side, base, right, part, speed, matrix, sent = call(
        local_kernel,
        [flat, (4, *flat), flat, triple, flat, flat, jax.ShapeDtypeStruct((rows, rows), jnp.bfloat16), flat],
        temp, source, visc, velocity.reshape(triple), forcing.reshape(triple), edge_table, pole_table,
        scratch=[flat, flat, triple, table, table, pltpu.SemaphoreType.DMA((7,))],
        place=pltpu.HBM,
    )
    temp_near, temp_far = exchange(sent[None])
    shapes = [(high - low, rows, layers) for low, high in SPLITS]
    weights, diagonal, inverse, *first = call(
        weigh_kernel, [(6, *flat), flat, flat, *shapes[:-1]],
        visc_far, visc_near, half, side, base, right, matrix, scratch=[(1, *flat)],
    )
    adjoint_next, *rest = call(
        step_kernel, [flat, shapes[-1]],
        temp_near, temp_far, right, part, speed, inverse, matrix, scratch=[(1, *flat)],
    )
    first += rest
    streams = [[field] for field in first]
    swapped = [exchange(field) for field in first]
    for step in range(ITERS - 1):
        for i, shape in enumerate(shapes):
            near, far = swapped[i]
            (field,) = call(apply_kernel, [shape], near, far, streams[i][-1], weights, matrix, scratch=[shape])
            swapped[i] = exchange(field)
            streams[i].append(field)
    many = (len(CENTERS), *triple)
    moments, left, shift = call(
        early_kernel, [(8, 128), many, many], diagonal, *[field for stream in streams for field in stream]
    )
    for i, shape in enumerate(shapes):
        near, far = swapped[i]
        sums = (8, 128) if i + 1 < len(shapes) else (devices, 1, 128)
        kernel, halo = (last_near_kernel, [near, far]) if i == 0 else (last_kernel, [far, near])
        field, moments = call(
            functools.partial(kernel, SPLITS[i][0]), [shape, sums],
            *halo, streams[i][-1], weights, matrix, moments, left, shift, scratch=[shape],
        )
        streams[i].append(field)
    moments = lax.all_to_all(moments, NAMES, 0, 0)
    fields = [field for stream in streams for field in stream]
    answer, residual = call(
        finish_kernel, [triple, triple], moments, diagonal, *fields,
        scratch=[triple, triple, pltpu.SemaphoreType.DMA((2, 3))], out_place=pltpu.HBM,
    )
    whole = (3, 1, 1, rows, layers)
    return answer.reshape(whole), residual.reshape(whole), adjoint_next.reshape(adjoint_temp.shape)


def solution(mesh):
    flat = P("diamond", "tile", None, None)
    triple = P(None, "diamond", "tile", None, None)
    return jax.shard_map(
        body,
        mesh=mesh,
        in_specs=(flat, flat, flat, triple, triple, P(), P()),
        out_specs=(triple, triple, flat),
        check_vma=False,
    )
```
